32 devices in a mesh: batch: 4 (over y, x), expert: 8 (over z, core).
Axes of the slice: x: 2, y: 2, z: 4, core: 2. Of those that a mesh axis runs over, the one named last changes fastest.
Arguments:
- tokens: bfloat16 [32768, 768], P(('batch', 'expert')), may hold values from -6 to 6
- cotangent: bfloat16 [32768, 768], P(('batch', 'expert')), may hold values from -6 to 6
- segment_ids: int32 [32, 1024], P(('batch', 'expert')), may hold values from 0 to 5, never falling along the last dimension, each value on 1 to 384 neighbouring positions
- routes: int32 [32768, 1], P(('batch', 'expert')), may hold values from 0 to 31, as said below
- capacity: int32 [32], replicated, may hold values from 32 to 64, as said below
- ln1_gain: bfloat16 [768], P(('batch', 'expert')), may hold values from 0.5 to 1.5
- ln1_bias: bfloat16 [768], P(('batch', 'expert')), may hold values from -1.25 to 1.25
- w_query: bfloat16 [768, 768], P(('batch', 'expert')), may hold values from -0.21875 to 0.21875
- b_query: bfloat16 [768], P(('batch', 'expert')), may hold values from -1.25 to 1.25
- w_key: bfloat16 [768, 768], P(('batch', 'expert')), may hold values from -0.21875 to 0.21875
- w_value: bfloat16 [768, 768], P(('batch', 'expert')), may hold values from -0.21875 to 0.21875
- b_value: bfloat16 [768], P(('batch', 'expert')), may hold values from -1.25 to 1.25
- w_output: bfloat16 [768, 768], P(('batch', 'expert')), may hold values from -1.25 to 1.25
- b_output: bfloat16 [768], P(('batch', 'expert')), may hold values from -1.25 to 1.25
- ln2_gain: bfloat16 [768], P(('batch', 'expert')), may hold values from 0.5 to 1.5
- ln2_bias: bfloat16 [768], P(('batch', 'expert')), may hold values from -1.25 to 1.25
- w_router: bfloat16 [768, 32], P(('batch', 'expert')), may hold values from -0.15625 to 0.15625
- w_in: bfloat16 [32, 768, 3072], P('expert', None, 'batch'), may hold values from -0.21875 to 0.21875
- b_in: bfloat16 [32, 3072], P('expert', 'batch'), may hold values from -0.625 to 0.625
- w_out: bfloat16 [32, 3072, 768], P('expert', 'batch'), may hold values from -3.5 to 3.5
- b_out: bfloat16 [32, 768], P(None, ('batch', 'expert')), may hold values from -12 to 12
Outputs:
- block_out: bfloat16 [32768, 768], P(('batch', 'expert'))
- balance_loss: float32 [], replicated
- expert_shares: float32 [2, 32], replicated
- input_grad: float32 [32768, 768], P(('batch', 'expert'))
- grad_ln1_gain: float32 [768], P(('batch', 'expert'))
- grad_ln1_bias: float32 [768], P(('batch', 'expert'))
- grad_w_query: float32 [768, 768], P(('batch', 'expert'))
- grad_b_query: float32 [768], P(('batch', 'expert'))
- grad_w_key: float32 [768, 768], P(('batch', 'expert'))
- grad_w_value: float32 [768, 768], P(('batch', 'expert'))
- grad_b_value: float32 [768], P(('batch', 'expert'))
- grad_w_output: float32 [768, 768], P(('batch', 'expert'))
- grad_b_output: float32 [768], P(('batch', 'expert'))
- grad_ln2_gain: float32 [768], P(('batch', 'expert'))
- grad_ln2_bias: float32 [768], P(('batch', 'expert'))
- grad_w_router: float32 [768, 32], P(('batch', 'expert'))
- grad_w_in: float32 [32, 768, 3072], P('expert', None, 'batch')
- grad_b_in: float32 [32, 3072], P('expert', 'batch')
- grad_w_out: float32 [32, 3072, 768], P('expert', 'batch')
- grad_b_out: float32 [32, 768], P(None, ('batch', 'expert'))
The draws below stay inside these ranges and needn't reach their ends.
Inputs may be any that keep to these rules, and one draw needn't show every extreme that they name: `routes`: the rows of one device name each expert at most 64 times, and on every device some expert exactly 64 times; every expert is named by the rows of some device. Some expert has capacity 64. `segment_ids`: segment ids never fall along a packed row.
All inputs are finite; a program needn't handle non-finite values.
Results may differ from the reference program's by a relative error of at most 0.014.
Values may be sent and summed in bfloat16 or wider, within the bound.
No kernel may reach another device: no remote copies, remote signals or barrier semaphores. Data moves between devices by JAX's collectives and lax.ppermute only.
A program may use at most 384 MiB of HBM per device.

```python
import math
import jax
import jax.numpy as jnp
import numpy as np
from jax import lax

D = 768
HEADS = 12
HEAD = 64
EXPERTS = 32
LEN = 1024
SPLIT = 1
GROUPS = 32
FF_GROUP = 3072
TOK_DEV = 1024
CAP = 64
SEQS = 32
TOKENS = 32768
DEVICES = 32


def draw_capacity(key, part):
    draw_key, pick_key = jax.random.split(jax.random.fold_in(key, 17))
    levels = jax.random.randint(draw_key, (EXPERTS,), CAP // 2, CAP + 1)
    picked = jax.random.randint(pick_key, (), 0, EXPERTS)
    return levels.at[picked].set(CAP).astype(jnp.int32)


def draw_routes(key, part):
    device_count = TOKENS // TOK_DEV
    jitter_key, order_key = jax.random.split(jax.random.fold_in(key, 29))
    device = jnp.arange(device_count, dtype=jnp.int32)[:, None]
    expert = jnp.arange(EXPERTS, dtype=jnp.int32)[None, :]
    home = device * EXPERTS // device_count
    distance = jnp.minimum((expert - home) % EXPERTS, (home - expert) % EXPERTS)
    jitter = jax.random.randint(jitter_key, (device_count, EXPERTS), 0, 6)
    score = (4 * distance + jitter) * EXPERTS + expert
    ranked = jnp.argsort(score, axis=1).astype(jnp.int32)
    position = jnp.arange(TOK_DEV, dtype=jnp.int32)
    quarter = EXPERTS // 4
    half_cap = CAP // 2
    rank_of = jnp.where(position < quarter * CAP, position // CAP, quarter + (position - quarter * CAP) // half_cap)
    chosen = ranked[:, rank_of]
    shuffle_keys = jax.random.split(order_key, device_count)
    shuffled = jax.vmap(lambda one_key, row: jax.random.permutation(one_key, row))(shuffle_keys, chosen)
    return shuffled.reshape(TOKENS, 1).astype(jnp.int32)


def level_of(key, shape, cuts, least, top_value):
    gain, own = 1.0, jax.random.fold_in(key, 6)
    for dim, shards_of in cuts:
        draws = jnp.exp(jax.random.uniform(jax.random.fold_in(own, dim), (shards_of,), jnp.float32, least / len(cuts), top_value / len(cuts)))
        gain = gain * jnp.repeat(draws, shape[dim] // shards_of).reshape([-1 if axis == dim else 1 for axis in range(len(shape))])
    return gain


def split_up(number_of, total, limit, lean):
    portions = [(1 << 20) // math.isqrt(grade ** lean) + 1 for grade in range(2, number_of + 1)]
    spare, holding = total - limit - (number_of - 1), [1] * (number_of - 1)
    while spare > 0:
        candidates = [i for i in range(number_of - 1) if holding[i] < limit]
        pool, budget = sum([portions[i] for i in candidates]), spare
        for i in candidates:
            extra = min(limit - holding[i], max(1, budget * portions[i] // pool), spare)
            holding[i] = holding[i] + extra
            spare = spare - extra
    return np.array([limit] + holding)


def uneven(own_key, count, total, bound, slope):
    if count == 2:
        one = jax.random.randint(own_key, (), max(1, total - bound), min(bound, total - 1) + 1)
        return jnp.stack([one, total - one])
    tallies = jnp.asarray(split_up(count, total, bound, slope), jnp.int32)
    twos = (count - 1) // 2
    source_of, sink = tallies[1:1 + 2 * twos:2], tallies[2:2 + 2 * twos:2]
    slack = jnp.minimum(source_of - 1, bound - sink)
    shifted = jax.random.randint(jax.random.fold_in(own_key, 1), (twos,), 0, 1 << 20) % (slack + 1)
    tallies = tallies.at[1:1 + 2 * twos:2].set(source_of - shifted).at[2:2 + 2 * twos:2].set(sink + shifted)
    return tallies[jax.random.permutation(jax.random.fold_in(own_key, 2), count)]


def gaussian(own_key, extent, deviation, reach, shards=(), held_as=jnp.bfloat16):
    loudness = level_of(own_key, extent, shards, -0.22, 0.18) if shards else 1.0
    values = jax.random.normal(own_key, extent, jnp.float32) * deviation * loudness
    return jnp.minimum(jnp.maximum(values, -reach), reach).astype(held_as)


def setup_inputs(seed: int = 0) -> dict:
    arg_keys = jax.random.split(jax.random.key(seed), 22)
    return {
        "tokens": gaussian(arg_keys[0], (TOKENS, D), 1.0, 6.0, ((0, 32),)),
        "cotangent": gaussian(arg_keys[1], (TOKENS, D), 1.0, 6.0, ((0, 32),)),
        "segment_ids": jax.vmap(lambda own: jnp.searchsorted(jnp.cumsum(uneven(own, 6, LEN, LEN * 3 // 8, 2)), jnp.arange(LEN), side="right"))(jax.random.split(arg_keys[2], SEQS)).reshape((SEQS, LEN)).astype(jnp.int32),
        "routes": draw_routes(jax.random.fold_in(arg_keys[21], 71), 0),
        "capacity": draw_capacity(jax.random.fold_in(arg_keys[21], 71), 0),
        "ln1_gain": jnp.clip(1.0 + 0.1 * jax.random.normal(arg_keys[5], (D,), jnp.float32), 0.5, 1.5).astype(jnp.bfloat16),
        "ln1_bias": gaussian(arg_keys[6], (D,), 0.2, 1.25, ((0, 32),)),
        "w_query": gaussian(arg_keys[7], (D, D), D ** -0.5, 0.21875, ((0, 32),)),
        "b_query": gaussian(arg_keys[8], (D,), 0.2, 1.25, ((0, 32),)),
        "w_key": gaussian(arg_keys[9], (D, D), D ** -0.5, 0.21875, ((0, 32),)),
        "w_value": gaussian(arg_keys[10], (D, D), D ** -0.5, 0.21875, ((0, 32),)),
        "b_value": gaussian(arg_keys[11], (D,), 0.2, 1.25, ((0, 32),)),
        "w_output": gaussian(arg_keys[12], (D, D), (D // 32) ** -0.5, 1.25, ((0, 32),)),
        "b_output": gaussian(arg_keys[13], (D,), 0.2, 1.25, ((0, 32),)),
        "ln2_gain": jnp.clip(1.0 + 0.1 * jax.random.normal(arg_keys[14], (D,), jnp.float32), 0.5, 1.5).astype(jnp.bfloat16),
        "ln2_bias": gaussian(arg_keys[15], (D,), 0.2, 1.25, ((0, 32),)),
        "w_router": gaussian(arg_keys[16], (D, EXPERTS), 0.025, 0.15625, ((0, 32),)),
        "w_in": gaussian(arg_keys[17], (GROUPS, D, FF_GROUP), D ** -0.5, 0.21875, ((0, 8), (2, 4))),
        "b_in": gaussian(arg_keys[18], (GROUPS, FF_GROUP), 0.1, 0.625, ((0, 8), (1, 4))),
        "w_out": gaussian(arg_keys[19], (GROUPS, FF_GROUP, D), (0.018 * EXPERTS), 3.5, ((0, 8), (1, 4))),
        "b_out": gaussian(arg_keys[20], (EXPERTS, D), (0.06 * EXPERTS), 12.0, ((1, 32),)),
    }


epsilon = 1e-05
balance_weight = 0.01
highest = lax.Precision.HIGHEST

@jax.custom_vjp
def low(v):
    return lax.optimization_barrier(v.astype(jnp.bfloat16)).astype(jnp.float32)

@jax.custom_vjp
def low_back(v):
    return v

def low_keep(v):
    return (low(v), None)

def low_pass(kept, grad):
    return (grad,)

def back_keep(v):
    return (v, None)

def back_low(kept, grad):
    return (low(grad),)
low.defvjp(low_keep, low_pass)
low_back.defvjp(back_keep, back_low)

def round_both(values):
    return low_back(low(values))

def layer_norm(inputs, gain_vec, shift_vec):
    average = lax.optimization_barrier(jnp.mean(inputs, axis=-1, keepdims=True))
    centred = inputs - average
    variance = lax.optimization_barrier(jnp.mean(centred * centred, axis=-1, keepdims=True))
    return centred * lax.rsqrt(variance + epsilon) * gain_vec + shift_vec

def attend(items):
    queries, key_rows, values, segments = items
    scores = jnp.einsum('qhd,khd->hqk', queries, key_rows, precision=highest) * HEAD ** (-0.5)
    scores = low_back(scores)
    position = jnp.arange(segments.shape[0])
    visible = (position[None, :] <= position[:, None]) & (segments[None, :] == segments[:, None])
    scores = jnp.where(visible[None], scores, -jnp.inf)
    attn_probs = low(jax.nn.softmax(scores, axis=-1))
    return jnp.einsum('hqk,khd->qhd', attn_probs, values, precision=highest)

def expert_apply(items):
    slot_rows, weight_in, bias_in, weight_out = items
    flat_rows = slot_rows.reshape(DEVICES * CAP, D)
    preact = low_back(jnp.dot(flat_rows, weight_in, precision=highest) + bias_in)
    hidden = low(jax.nn.gelu(preact, approximate=False))
    result = round_both(jnp.dot(hidden, weight_out, precision=highest))
    return result.reshape(DEVICES, CAP, D)

def forward(tokens, ln1_gain, ln1_bias, w_query, b_query, w_key, w_value, b_value, w_output, b_output, ln2_gain, ln2_bias, w_router, w_in, b_in, w_out, b_out, segment_ids, routes, capacity):
    h_one = low(layer_norm(tokens, ln1_gain, ln1_bias))
    queries = round_both(jnp.dot(h_one, w_query, precision=highest) + b_query)
    key_rows = round_both(jnp.dot(h_one, w_key, precision=highest))
    values = round_both(jnp.dot(h_one, w_value, precision=highest) + b_value)
    head_shape = (SEQS, LEN, HEADS, HEAD)
    attended = lax.map(jax.checkpoint(attend), (queries.reshape(head_shape), key_rows.reshape(head_shape), values.reshape(head_shape), segment_ids))
    attended = round_both(attended.reshape(TOKENS, D))
    resid = tokens + low_back(jnp.dot(attended, w_output, precision=highest) + b_output)
    h_two = low(layer_norm(resid, ln2_gain, ln2_bias))
    logits = low_back(jnp.dot(h_two, w_router, precision=highest))
    router_probs = jax.nn.softmax(logits, axis=-1)
    chosen = routes[:, 0].astype(jnp.int32)
    picked = chosen[:, None] == jnp.arange(EXPERTS).astype(jnp.int32)[None, :]
    picked_float = picked.astype(jnp.float32)
    picked_int = picked.astype(jnp.int32)
    counts = lax.optimization_barrier(jnp.sum(picked_float, axis=0))
    mean_probs = lax.optimization_barrier(jnp.mean(router_probs, axis=0))
    balance_loss = EXPERTS * jnp.sum(counts / TOKENS * mean_probs)
    expert_shares = jnp.stack([EXPERTS * counts / TOKENS, EXPERTS * mean_probs])
    gate_prob = lax.optimization_barrier(jnp.sum(router_probs * picked_float, axis=1))
    blocked = picked_int.reshape(DEVICES, TOK_DEV, EXPERTS)
    rank = (jnp.cumsum(blocked, axis=1) - blocked).reshape(TOKENS, EXPERTS)
    slot_index = lax.optimization_barrier(jnp.sum(rank * picked_int, axis=1)).astype(jnp.int32)
    kept_mask = slot_index < capacity[chosen]
    device_index = (jnp.arange(TOKENS) // TOK_DEV).astype(jnp.int32)
    target = jnp.where(kept_mask, slot_index, CAP).astype(jnp.int32)
    lookup = jnp.minimum(slot_index, CAP - 1).astype(jnp.int32)
    buffer = jnp.zeros((GROUPS, DEVICES, CAP, D), jnp.float32)
    for part_index in range(SPLIT):
        group_index = (chosen * SPLIT + part_index).astype(jnp.int32)
        buffer = buffer.at[group_index, device_index, target].add(low_back(h_two), mode='drop')
    expert_rows = lax.map(jax.checkpoint(expert_apply), (buffer, w_in, b_in, w_out))
    fetched = jnp.zeros((TOKENS, D), jnp.float32)
    for part_index in range(SPLIT):
        group_index = (chosen * SPLIT + part_index).astype(jnp.int32)
        fetched = fetched + expert_rows[group_index, device_index, lookup]
    expert_out = fetched + b_out[chosen]
    block_out = resid + (kept_mask.astype(jnp.float32) * gate_prob)[:, None] * expert_out
    return ((block_out, balance_loss), expert_shares)

def reference(tokens, cotangent, segment_ids, routes, capacity, ln1_gain, ln1_bias, w_query, b_query, w_key, w_value, b_value, w_output, b_output, ln2_gain, ln2_bias, w_router, w_in, b_in, w_out, b_out):
    floats = [arg.astype(jnp.float32) for arg in (tokens, ln1_gain, ln1_bias, w_query, b_query, w_key, w_value, b_value, w_output, b_output, ln2_gain, ln2_bias, w_router, w_in, b_in, w_out, b_out)]

    def apply_block(*params):
        return forward(*params, segment_ids, routes, capacity)
    (block_out, balance_loss), pull, expert_shares = jax.vjp(apply_block, *floats, has_aux=True)
    grads = pull((cotangent.astype(jnp.float32), jnp.ones_like(balance_loss) * balance_weight))
    return (block_out.astype(jnp.bfloat16), balance_loss, expert_shares, grads[0], grads[1], grads[2], grads[3], grads[4], grads[5], grads[6], grads[7], grads[8], grads[9], grads[10], grads[11], grads[12], grads[13], grads[14], grads[15], grads[16])
```

```python
import functools

import jax
import jax.numpy as jnp
from jax import lax
from jax.experimental import pallas as pl
from jax.experimental.pallas import tpu as pltpu
from jax.sharding import PartitionSpec as P

HEAD = 64
LANES = 128
REACH = 384
QROWS = 256
EPSILON = 1e-05
BALANCE = 0.01
ALL = ("batch", "expert")
VMEM = 60 * 1024 * 1024
F32 = jnp.float32
BF16 = jnp.bfloat16


def dot(a, b):
    return jnp.dot(a, b, preferred_element_type=F32)


def dot_nt(a, b):
    return lax.dot_general(a, b, (((1,), (1,)), ((), ())), preferred_element_type=F32)


def dot_tn(a, b):
    return lax.dot_general(a, b, (((0,), (0,)), ((), ())), preferred_element_type=F32)


def swap(x, axis, mask):
    return lax.ppermute(x, axis, [(i, i ^ mask) for i in range(lax.axis_size(axis))])


def shift(x, step):
    size = lax.axis_size("expert")
    return lax.ppermute(x, "expert", [(i, (i + step) % size) for i in range(size)])


def staged():
    return lax.axis_size("batch") == 4 and lax.axis_size("expert") == 8


def gather_rows(x):
    if not staged():
        return lax.all_gather(x, ALL, axis=0, tiled=True)
    mb, me = lax.axis_index("batch"), lax.axis_index("expert")
    mz, mc = me // 2, me % 2
    ring = [shift(x, 2 * k) for k in (3, 2, 1)] + [x]
    ring = jnp.stack(ring + ring[:3])
    zs = lax.dynamic_slice_in_dim(ring, 3 - mz, 4, 0)
    b = [zs] + [swap(zs, "batch", k) for k in (1, 2, 3)]
    odd, high = (mb & 1) == 1, (mb & 2) == 2
    u = [jnp.where(odd, b[i ^ 1], b[i]) for i in range(4)]
    rows = jnp.stack([jnp.where(high, u[i ^ 2], u[i]) for i in range(4)])
    other = swap(rows, "expert", 1)
    both = jnp.stack(
        [jnp.where(mc == 0, rows, other), jnp.where(mc == 0, other, rows)], axis=2
    )
    return both.reshape(32 * x.shape[0], x.shape[1])


def scatter_rows(g):
    if not staged():
        return lax.psum_scatter(g, ALL, scatter_dimension=0, tiled=True).astype(F32)
    mb, me = lax.axis_index("batch"), lax.axis_index("expert")
    mz, mc = me // 2, me % 2
    r, c = g.shape[0] // 32, g.shape[1]
    g = g.reshape(4, 4, 2, r, c)
    mine = jnp.where(mc == 0, g[:, :, 0], g[:, :, 1])
    other = swap(jnp.where(mc == 0, g[:, :, 1], g[:, :, 0]), "expert", 1)
    s = (mine.astype(F32) + other.astype(F32)).astype(BF16)
    pick = lambda t, i: lax.dynamic_index_in_dim(t, i, 0, keepdims=False)
    parts = [swap(pick(s, mb ^ k), "batch", k) for k in (1, 2, 3)]
    t = sum((p.astype(F32) for p in parts), pick(s, mb).astype(F32)).astype(BF16)
    parts = [shift(pick(t, (mz + k) % 4), 2 * k) for k in (1, 2, 3)]
    return sum((p.astype(F32) for p in parts), pick(t, mz).astype(F32))


def total(x):
    if not staged():
        return lax.psum(x, ALL)
    for axis, mask in (("expert", 1), ("batch", 1), ("batch", 2), ("expert", 2), ("expert", 4)):
        x = x + swap(x, axis, mask)
    return x


def to_owners(x):
    return lax.all_to_all(x, "expert", split_axis=1, concat_axis=1, tiled=True)


def windows(length):
    for start in range(0, length, QROWS):
        yield start, max(0, start - REACH), start + QROWS


def half_masks():
    lane = lax.broadcasted_iota(jnp.int32, (1, LANES), 1)
    first = (lane < HEAD).astype(F32)
    return first, (first.astype(BF16), (1.0 - first).astype(BF16))


def attend_kernel(q_ref, k_ref, v_ref, row_ref, col_ref, out_ref, log_ref, mask_ref):
    length = q_ref.shape[0]

    @pl.when(pl.program_id(0) == 0)
    def _():
        for n, (start, low, stop) in enumerate(windows(length)):
            shape = (QROWS, stop - low)
            i = lax.broadcasted_iota(jnp.int32, shape, 0) + start
            j = lax.broadcasted_iota(jnp.int32, shape, 1) + low
            same = col_ref[start:stop, :] == row_ref[:, low:stop]
            mask_ref[n, :, : stop - low] = jnp.where((j <= i) & same, 0.0, -1e30)

    first, halves = half_masks()
    for n, (start, low, stop) in enumerate(windows(length)):
        q = q_ref[start:stop, :] * jnp.asarray(HEAD**-0.5, BF16)
        k, v = k_ref[low:stop, :], v_ref[low:stop, :]
        outs, logs = [], []
        for half in halves:
            s = dot_nt(q * half, k) + mask_ref[n, :, : stop - low]
            top = jnp.max(s, axis=1, keepdims=True)
            e = jnp.exp(s - top)
            sums = jnp.sum(e, axis=1, keepdims=True)
            outs.append(dot(e.astype(BF16), v) / sums)
            logs.append(top + jnp.log(sums))
        out_ref[start:stop, :] = (outs[0] * first + outs[1] * (1.0 - first)).astype(BF16)
        log_ref[start:stop, :] = logs[0] * first + logs[1] * (1.0 - first)


def attend(qkv, seg_row, seg_col, width):
    length = qkv.shape[0]
    pairs = width // LANES
    spec = lambda offset: pl.BlockSpec((length, LANES), lambda p, o=offset: (0, o + p))
    whole = lambda shape: pl.BlockSpec(shape, lambda p: (0,) * len(shape))
    return pl.pallas_call(
        attend_kernel,
        grid=(pairs,),
        in_specs=[spec(0), spec(pairs), spec(2 * pairs), whole((1, length)), whole((length, 1))],
        out_specs=[spec(0), spec(0)],
        out_shape=[
            jax.ShapeDtypeStruct((length, width), BF16),
            jax.ShapeDtypeStruct((length, width), F32),
        ],
        scratch_shapes=[pltpu.VMEM((length // QROWS, QROWS, QROWS + REACH), F32)],
        compiler_params=pltpu.CompilerParams(vmem_limit_bytes=VMEM),
        cost_estimate=pl.CostEstimate(
            flops=4 * length * 512 * width, bytes_accessed=12 * length * width, transcendentals=12 * length * 512
        ),
        name="attend",
    )(qkv, qkv, qkv, seg_row, seg_col)


def attend_back_kernel(
    q_ref, k_ref, v_ref, g_ref, log_ref, row_ref, col_ref, out_ref, mask_ref, dk_ref, dv_ref
):
    length = q_ref.shape[0]

    @pl.when(pl.program_id(0) == 0)
    def _():
        for n, (start, low, stop) in enumerate(windows(length)):
            shape = (stop - low, QROWS)
            j = lax.broadcasted_iota(jnp.int32, shape, 0) + low
            i = lax.broadcasted_iota(jnp.int32, shape, 1) + start
            same = col_ref[low:stop, :] == row_ref[:, start:stop]
            mask_ref[n, : stop - low, :] = jnp.where((j <= i) & same, 0.0, -1e30)

    dk_ref[...] = jnp.zeros_like(dk_ref)
    dv_ref[...] = jnp.zeros_like(dv_ref)
    _, halves = half_masks()
    scale = HEAD**-0.5
    for n, (start, low, stop) in enumerate(windows(length)):
        q = q_ref[start:stop, :] * jnp.asarray(scale, BF16)
        g = g_ref[start:stop, :]
        k, v = k_ref[low:stop, :], v_ref[low:stop, :]
        logs = log_ref[start:stop, :].T
        dq = jnp.zeros((QROWS, LANES), F32)
        for at, half in zip((0, HEAD), halves):
            qh, gh = q * half, g * half
            s = dot_nt(k, qh) + mask_ref[n, : stop - low, :]
            p = jnp.exp(s - logs[at : at + 1, :])
            dp = dot_nt(v, gh)
            centre = jnp.sum(dp * p, axis=0, keepdims=True)
            ds = (p * (dp - centre)).astype(BF16)
            dv_ref[low:stop, :] += dot(p.astype(BF16), gh)
            dk_ref[low:stop, :] += dot(ds, qh)
            dq += dot_tn(ds, k * half)
        out_ref[0, start:stop, :] = (dq * scale).astype(BF16)
    out_ref[1] = dk_ref[...].astype(BF16)
    out_ref[2] = dv_ref[...].astype(BF16)


def attend_back(qkv, grad, logs, seg_row, seg_col, width):
    length = qkv.shape[0]
    pairs = width // LANES
    spec = lambda offset: pl.BlockSpec((length, LANES), lambda p, o=offset: (0, o + p))
    whole = lambda shape: pl.BlockSpec(shape, lambda p: (0,) * len(shape))
    return pl.pallas_call(
        attend_back_kernel,
        grid=(pairs,),
        in_specs=[spec(0), spec(pairs), spec(2 * pairs), spec(0), spec(0), whole((1, length)), whole((length, 1))],
        out_specs=pl.BlockSpec((3, length, LANES), lambda p: (0, 0, p)),
        out_shape=jax.ShapeDtypeStruct((3, length, width), BF16),
        scratch_shapes=[
            pltpu.VMEM((length // QROWS, QROWS + REACH, QROWS), F32),
            pltpu.VMEM((length, LANES), F32),
            pltpu.VMEM((length, LANES), F32),
        ],
        compiler_params=pltpu.CompilerParams(vmem_limit_bytes=VMEM),
        cost_estimate=pl.CostEstimate(
            flops=10 * length * 512 * width, bytes_accessed=18 * length * width, transcendentals=12 * length * 512
        ),
        name="attend_back",
    )(qkv, qkv, qkv, grad, logs, seg_row, seg_col)


def slot_ids(shape, axis, base, groups, owners, split, slots):
    at = lax.broadcasted_iota(jnp.int32, shape, axis) + base
    row, slot = at // slots, at % slots
    return ((row % owners) * groups + row // owners) // split * slots + slot


def dispatch_kernel(groups, owners, split, slots, id_ref, x_ref, out_ref):
    rows, tokens = out_ref.shape[0], x_ref.shape[0]
    ids = slot_ids((rows, 1), 0, pl.program_id(0) * rows, groups, owners, split, slots)
    chosen = (ids == id_ref[...]).astype(F32).astype(BF16)
    out_ref[...] = dot(chosen, x_ref[...]).astype(BF16)


def dispatch(ids, x, groups, owners, split, slots):
    tokens, width = x.shape
    count, block = groups * owners * slots, 256
    return pl.pallas_call(
        functools.partial(dispatch_kernel, groups, owners, split, slots),
        grid=(count // block,),
        in_specs=[
            pl.BlockSpec((1, tokens), lambda i: (0, 0)),
            pl.BlockSpec((tokens, width), lambda i: (0, 0)),
        ],
        out_specs=pl.BlockSpec((block, width), lambda i: (i, 0)),
        out_shape=jax.ShapeDtypeStruct((count, width), BF16),
        compiler_params=pltpu.CompilerParams(vmem_limit_bytes=VMEM),
        cost_estimate=pl.CostEstimate(
            flops=2 * count * tokens * width, bytes_accessed=4 * count * width, transcendentals=0
        ),
        name="dispatch",
    )(ids, x)


def combine_kernel(groups, owners, split, slots, id_ref, x_ref, out_ref):
    rows, count = out_ref.shape[0], x_ref.shape[0]
    out_ref[...] = jnp.zeros_like(out_ref)
    step = 512
    for base in range(0, count, step):
        ids = slot_ids((1, step), 1, base, groups, owners, split, slots)
        chosen = (id_ref[...] == ids).astype(F32).astype(BF16)
        out_ref[...] += dot(chosen, x_ref[base : base + step, :])


def combine(ids, x, groups, owners, split, slots):
    tokens, (count, width), block = ids.shape[0], x.shape, 256
    return pl.pallas_call(
        functools.partial(combine_kernel, groups, owners, split, slots),
        grid=(tokens // block,),
        in_specs=[
            pl.BlockSpec((block, 1), lambda i: (i, 0)),
            pl.BlockSpec((count, width), lambda i: (0, 0)),
        ],
        out_specs=pl.BlockSpec((block, width), lambda i: (i, 0)),
        out_shape=jax.ShapeDtypeStruct((tokens, width), F32),
        compiler_params=pltpu.CompilerParams(vmem_limit_bytes=VMEM),
        cost_estimate=pl.CostEstimate(
            flops=2 * count * tokens * width, bytes_accessed=2 * count * width + 4 * tokens * width, transcendentals=0
        ),
        name="combine",
    )(ids, x)


def gelu_parts(x):
    size = jnp.abs(x)
    t = 1.0 / (1.0 + (0.3275911 * 0.5**0.5) * size)
    bell = jnp.exp(-0.5 * x * x)
    poly = t * (
        0.5 * 0.254829592
        + t * (0.5 * -0.284496736 + t * (0.5 * 1.421413741 + t * (0.5 * -1.453152027 + t * (0.5 * 1.061405429))))
    )
    tail = poly * bell
    return jnp.where(x < 0, tail, 1.0 - tail), bell * 0.3989422804014327


def expert_kernel(
    steps, experts,
    id_ref, h0, h1, z0, z1, win_a, wout_a, win_b, wout_b, wr_ref,
    p0, p1, d0, d1, gwin_a, gwout_a, gwin_b, gwout_b, groute,
    hid_a, hid_b, dpre_a, dpre_b, dexp_s, acc_win, acc_wout,
):
    i = pl.program_id(0)
    width = wr_ref.shape[0]
    rows = h0.shape[1]
    sub = min(rows, 256)

    @pl.when(i == 0)
    def _():
        gwin_a[...] = jnp.zeros_like(gwin_a)
        gwout_a[...] = jnp.zeros_like(gwout_a)
        acc_win[...] = jnp.zeros_like(acc_win)
        acc_wout[...] = jnp.zeros_like(acc_wout)
        groute[...] = jnp.zeros_like(groute)

    def work(h_ref, z_ref, p_ref, d_ref):
        lane = lax.broadcasted_iota(jnp.int32, (1, LANES), 1)
        own = (lane == id_ref[0]).astype(F32)

        def block(n, _):
            at = pl.ds(pl.multiple_of(n * sub, sub), sub)
            h = h_ref[0, at, :]
            logits = jnp.where(lane < experts, dot(h, wr_ref[...]), -1e30)
            e = jnp.exp(logits - jnp.max(logits, axis=1, keepdims=True))
            probs = e / jnp.sum(e, axis=1, keepdims=True)
            gate = jnp.sum(probs * own, axis=1, keepdims=True)
            dz = z_ref[0, at, :].astype(F32)
            dexp = (gate * dz).astype(BF16)
            dexp_s[at, :] = dexp
            piece = back = None
            for win, wout, hid_s, dpre_s in ((win_a, wout_a, hid_a, dpre_a), (win_b, wout_b, hid_b, dpre_b)):
                pre = dot(h, win[:width, :]) + win[width : width + 1, :].astype(F32)
                phi, bell = gelu_parts(pre)
                hid = (pre * phi).astype(BF16)
                hid_s[at, :] = hid
                out = dot(hid, wout[...])
                piece = out if piece is None else piece + out
                dpre = (dot_nt(dexp, wout[...]) * (phi + pre * bell)).astype(BF16)
                dpre_s[at, :] = dpre
                out = dot_nt(dpre, win[:width, :])
                back = out if back is None else back + out
            p_ref[at, :] = piece.astype(BF16)
            dgate = jnp.sum(dz * piece, axis=1, keepdims=True)
            dlog = (dgate * probs * (own - gate)).astype(BF16)
            d_ref[at, :] = (back + dot_nt(dlog, wr_ref[...])).astype(BF16)
            groute[...] += dot_tn(h, dlog)
            return 0

        lax.fori_loop(0, rows // sub, block, 0)
        for dpre_s, hid_s, to_win, to_wout in (
            (dpre_a, hid_a, gwin_a, gwout_a),
            (dpre_b, hid_b, acc_win, acc_wout),
        ):
            dpre = dpre_s[...]
            to_win[:width, :] += dot_tn(h_ref[0], dpre)
            to_win[width : width + 8, :] += jnp.broadcast_to(
                jnp.sum(dpre.astype(F32), axis=0, keepdims=True), (8, dpre.shape[1])
            )
            to_wout[...] += dot_tn(hid_s[...], dexp_s[...])

    @pl.when(i < steps)
    def _():
        work(h0, z0, p0, d0)

    @pl.when(i >= steps)
    def _():
        work(h1, z1, p1, d1)

    @pl.when(i == 2 * steps - 1)
    def _():
        gwin_b[...] = acc_win[...].astype(BF16)
        gwout_b[...] = acc_wout[...].astype(BF16)


def expert(expert_id, own_h, other_h, own_z, other_z, at, weights, w_route, experts):
    win_a, wout_a, win_b, wout_b = weights
    rows, width = own_h.shape[1:]
    hidden = wout_a.shape[0]
    block = min(rows, 512)
    steps = rows // block
    early = lambda i: jnp.minimum(i, steps - 1)
    late = lambda i: jnp.maximum(i - steps, 0)
    once = lambda a: pl.BlockSpec(a.shape, lambda i: (0,) * a.ndim)
    first = pl.BlockSpec((1, block, width), lambda i: (at, early(i), 0))
    second = pl.BlockSpec((1, block, width), lambda i: (0, late(i), 0))
    out_first = pl.BlockSpec((block, width), lambda i: (early(i), 0))
    out_second = pl.BlockSpec((block, width), lambda i: (late(i), 0))
    shape = jax.ShapeDtypeStruct
    outs = [shape((rows, width), BF16)] * 4 + [
        shape((width + 16, hidden), F32),
        shape((hidden, width), F32),
        shape((width + 16, hidden), BF16),
        shape((hidden, width), BF16),
        shape((width, LANES), F32),
    ]
    return pl.pallas_call(
        functools.partial(expert_kernel, steps, experts),
        grid=(2 * steps,),
        in_specs=[pl.BlockSpec(memory_space=pltpu.SMEM), first, second, first, second]
        + [once(w) for w in (win_a, wout_a, win_b, wout_b, w_route)],
        out_specs=[out_first, out_second, out_first, out_second] + [once(o) for o in outs[4:]],
        out_shape=outs,
        scratch_shapes=[
            *[pltpu.VMEM((block, hidden), BF16)] * 4,
            pltpu.VMEM((block, width), BF16),
            pltpu.VMEM((width + 16, hidden), F32),
            pltpu.VMEM((hidden, width), F32),
        ],
        compiler_params=pltpu.CompilerParams(vmem_limit_bytes=VMEM),
        cost_estimate=pl.CostEstimate(
            flops=48 * rows * hidden * width, bytes_accessed=28 * width * hidden, transcendentals=4 * rows * hidden
        ),
        name="expert",
    )(expert_id, own_h, other_h, own_z, other_z, win_a, wout_a, win_b, wout_b, w_route)


def normed(x):
    centred = x - jnp.mean(x, axis=-1, keepdims=True)
    rstd = lax.rsqrt(jnp.mean(centred * centred, axis=-1, keepdims=True) + EPSILON)
    return centred * rstd, rstd


def norm_back(grad, gain, unit, rstd):
    g = grad * gain
    mean = lambda t: jnp.mean(t, axis=-1, keepdims=True)
    return rstd * (g - mean(g) - unit * mean(g * unit))


def pad_columns(x, count):
    return jnp.pad(x, ((0, 0), (0, count - x.shape[1])))


def up(count):
    return -(-count // LANES) * LANES


def local(
    tokens, cotangent, segment_ids, routes, capacity, ln1_gain, ln1_bias, w_query, b_query, w_key, w_value,
    b_value, w_output, b_output, ln2_gain, ln2_bias, w_router, w_in, b_in, w_out, b_out,
):
    row_count, width = tokens.shape
    experts = capacity.shape[0]
    slots = 2 * row_count // experts
    groups = w_in.shape[0]
    owners = lax.axis_size("expert")
    split = groups * owners // experts
    share = w_query.shape[0]
    devices = lax.axis_size("batch") * owners
    me = lax.axis_index("expert")
    layout = (groups, owners, split, slots)

    chosen = routes[:, 0]
    picked = chosen[:, None] == jnp.arange(experts, dtype=jnp.int32)[None, :]
    picked_float = picked.astype(F32)
    position = jnp.arange(row_count, dtype=jnp.int32)
    earlier = (position[None, :] < position[:, None]).astype(BF16)
    rank = dot(earlier, picked.astype(BF16))
    slot = jnp.sum(rank * picked_float, axis=1)
    limit = jnp.sum(capacity.astype(F32)[None, :] * picked_float, axis=1)
    kept = slot < limit
    kept_float = kept.astype(F32)
    ids = jnp.where(kept, chosen * slots + slot.astype(jnp.int32), -1)
    id_row, id_col = ids[None, :], ids[:, None]
    counts = jnp.sum(picked_float, axis=0)

    spread = -(-experts // share)
    small = jnp.stack([ln1_gain, ln1_bias, b_query, b_value, b_output, ln2_gain, ln2_bias], axis=1)
    tally = jnp.pad(counts, (0, spread * share - experts)).reshape(spread, share).T.astype(BF16)
    extra = pad_columns(jnp.concatenate([small, tally], axis=1), up(7 + spread))
    wide = gather_rows(jnp.concatenate([w_query, w_key, w_value, extra], axis=1))
    rest = gather_rows(jnp.concatenate([w_output, pad_columns(jnp.concatenate([w_router, b_out.T], axis=1), up(2 * experts))], axis=1))
    vectors = wide[:, 3 * width : 3 * width + 7].astype(F32).T
    gain_one, shift_one, bias_query, bias_value, bias_output, gain_two, shift_two = vectors
    tallies = wide[:, 3 * width + 7 : 3 * width + 7 + spread].astype(F32).reshape(devices, share, spread)
    all_counts = jnp.sum(tallies, axis=0).T.reshape(-1)[:experts]
    full_output = rest[:, :width]
    full_router = pad_columns(rest[:, width : width + experts], LANES)
    bias_expert = rest[:, width + experts : width + 2 * experts].T

    token_total = float(row_count * devices)
    fraction = all_counts / token_total

    weights = []
    for l in range(groups):
        mask = 1 if l % 2 == 0 else 2
        win = jnp.concatenate([w_in[l], jnp.broadcast_to(b_in[l][None, :], (16, b_in.shape[1]))], axis=0)
        weights.append((win, w_out[l], swap(win, "batch", mask), swap(w_out[l], "batch", mask)))

    chunk = min(2, groups)
    flat = (chunk, owners * slots, width)

    def send(x):
        rows = dispatch(id_row, x, *layout).reshape(groups, owners, slots, width)
        got = []
        for c in range(0, groups, chunk):
            mine = to_owners(rows[c : c + chunk]).reshape(flat)
            for l in range(chunk):
                theirs = swap(mine[l : l + 1], "batch", 2 if (c + l) % 2 == 0 else 1)
                got.append((mine, theirs, l))
        return got

    def bring(pieces):
        back = []
        for c in range(0, groups, chunk):
            rows = []
            for l in range(c, c + chunk):
                own, sent = pieces[l]
                rows.append((own.astype(F32) + swap(sent, "batch", 2 if l % 2 == 0 else 1).astype(F32)).astype(BF16))
            rows = jnp.stack(rows).reshape(chunk, owners, slots, width)
            back.append(to_owners(rows).reshape(chunk * owners * slots, width))
        return jnp.concatenate(back) if len(back) > 1 else back[0]

    grad_rows = send(cotangent)

    inputs = tokens.astype(F32)
    unit_one, rstd_one = normed(inputs)
    h_one = (unit_one * gain_one + shift_one).astype(BF16)
    nothing = jnp.zeros((width,), F32)
    bias = jnp.concatenate([bias_query, nothing, bias_value, jnp.zeros((wide.shape[1] - 3 * width,), F32)])
    qkv = (dot(h_one, wide) + bias).astype(BF16)
    seg_row = segment_ids.reshape(1, row_count)
    seg_col = segment_ids.reshape(row_count, 1)
    attended, logs = attend(qkv, seg_row, seg_col, width)
    resid = inputs + dot(attended, full_output) + bias_output
    unit_two, rstd_two = normed(resid)
    h_two = (unit_two * gain_two + shift_two).astype(BF16)

    token_rows = send(h_two)
    made = []
    for l in range(groups):
        mine_h, theirs_h, at = token_rows[l]
        mine_z, theirs_z, _ = grad_rows[l]
        number = ((me * groups + l) // split).astype(jnp.int32).reshape(1)
        made.append(expert(number, mine_h, theirs_h, mine_z, theirs_z, at, weights[l], full_router, experts))

    router_probs = jax.nn.softmax(dot(h_two, full_router)[:, :experts], axis=-1)
    mixing = kept_float * jnp.sum(router_probs * picked_float, axis=1)
    grad_out = cotangent.astype(F32)
    expert_bias = dot(picked.astype(BF16), bias_expert)
    gate_bias = kept_float * jnp.sum(grad_out * expert_bias, axis=1)
    grad_probs = picked_float * gate_bias[:, None] + BALANCE * experts * fraction[None, :] / token_total
    grad_logits = router_probs * (grad_probs - jnp.sum(grad_probs * router_probs, axis=1, keepdims=True))
    grad_logits = grad_logits.astype(BF16)
    mixed = picked_float * mixing[:, None]
    mixed_high = mixed.astype(BF16)
    mixed_low = (mixed - mixed_high.astype(F32)).astype(BF16)
    grad_bias_expert = dot_tn(cotangent, mixed_high) + dot_tn(cotangent, mixed_low)
    grad_router = dot_tn(h_two, grad_logits) + sum(m[8] for m in made)[:, :experts]
    prob_sums = total(jnp.sum(router_probs, axis=0))
    mean_probs = prob_sums / token_total
    balance_loss = experts * jnp.sum(fraction * mean_probs)
    expert_shares = jnp.stack([experts * fraction, experts * mean_probs])

    returned = bring([(m[2], m[3]) for m in made])
    grad_h_two = dot_nt(grad_logits, full_router[:, :experts]) + combine(id_col, returned, *layout)

    grad_resid = grad_out + norm_back(grad_h_two, gain_two, unit_two, rstd_two)
    grad_branch = grad_resid.astype(BF16)
    grad_att = dot_nt(grad_branch, full_output).astype(BF16)
    dqkv = attend_back(qkv, grad_att, logs, seg_row, seg_col, width)

    columns = lambda *rows: jnp.stack(rows, axis=1)
    grads_two = columns(
        jnp.sum(grad_h_two * unit_two, axis=0), jnp.sum(grad_h_two, axis=0), jnp.sum(grad_branch.astype(F32), axis=0)
    )
    packed = jnp.concatenate([grad_router, grad_bias_expert, grads_two], axis=1)
    packed = jnp.concatenate([dot_tn(attended, grad_branch), pad_columns(packed, up(packed.shape[1]))], axis=1)
    rest_sum = scatter_rows(packed.astype(BF16))

    grad_in, grad_in_bias, grad_w_out = [], [], []
    for l in range(groups):
        mask = 1 if l % 2 == 0 else 2
        got_in, got_out = swap(made[l][6], "batch", mask), swap(made[l][7], "batch", mask)
        grad_in.append(made[l][4][:width] + got_in[:width].astype(F32))
        grad_in_bias.append(made[l][4][width] + got_in[width].astype(F32))
        grad_w_out.append(made[l][5] + got_out.astype(F32))

    fetched = combine(id_col, bring([(m[0], m[1]) for m in made]), *layout)
    block_out = (resid + mixing[:, None] * (fetched + expert_bias)).astype(BF16)

    grads_w = jnp.concatenate([dot_tn(h_one, dqkv[s]) for s in range(3)], axis=1)
    grad_h_one = sum(dot_nt(dqkv[s], wide[:, s * width : (s + 1) * width]) for s in range(3))
    input_grad = grad_resid + norm_back(grad_h_one, gain_one, unit_one, rstd_one)
    grads_one = columns(
        jnp.sum(grad_h_one * unit_one, axis=0),
        jnp.sum(grad_h_one, axis=0),
        jnp.sum(dqkv[0].astype(F32), axis=0),
        jnp.sum(dqkv[2].astype(F32), axis=0),
    )
    wide_sum = scatter_rows(jnp.concatenate([grads_w, pad_columns(grads_one, LANES)], axis=1).astype(BF16))

    tail = 3 * width
    side = width + 2 * experts
    return (
        block_out,
        balance_loss,
        expert_shares,
        input_grad,
        wide_sum[:, tail],
        wide_sum[:, tail + 1],
        wide_sum[:, :width],
        wide_sum[:, tail + 2],
        wide_sum[:, width : 2 * width],
        wide_sum[:, 2 * width : 3 * width],
        wide_sum[:, tail + 3],
        rest_sum[:, :width],
        rest_sum[:, side + 2],
        rest_sum[:, side],
        rest_sum[:, side + 1],
        rest_sum[:, width : width + experts],
        jnp.stack(grad_in),
        jnp.stack(grad_in_bias),
        jnp.stack(grad_w_out),
        rest_sum[:, width + experts : side].T,
    )


def solution(mesh):
    rows, split = P(ALL, None), P(ALL)
    experts = (P("expert", None, "batch"), P("expert", "batch"), P("expert", "batch", None), P(None, ALL))
    return jax.shard_map(
        local,
        mesh=mesh,
        in_specs=(
            rows, rows, rows, rows, P(), split, split, rows, split, rows, rows, split, rows, split, split, split,
            rows, *experts,
        ),
        out_specs=(
            rows, P(), P(), rows, split, split, rows, split, rows, rows, split, rows, split, split, split, rows,
            *experts,
        ),
        check_vma=False,
    )
```

```python
import functools

import jax
import jax.numpy as jnp
from jax import lax
from jax.experimental import pallas as pl
from jax.experimental.pallas import tpu as pltpu
from jax.sharding import PartitionSpec as P

HEAD = 64
LANES = 128
REACH = 384
QROWS = 256
EPSILON = 1e-05
BALANCE = 0.01
ALL = ("batch", "expert")
VMEM = 60 * 1024 * 1024
COST = pl.CostEstimate(flops=1, bytes_accessed=1, transcendentals=0)
F32 = jnp.float32
BF16 = jnp.bfloat16


def dot(a, b):
    return jnp.dot(a, b, preferred_element_type=F32)


def dot_nt(a, b):
    return lax.dot_general(a, b, (((1,), (1,)), ((), ())), preferred_element_type=F32)


def dot_tn(a, b):
    return lax.dot_general(a, b, (((0,), (0,)), ((), ())), preferred_element_type=F32)


def swap(x, axis, mask):
    return lax.ppermute(x, axis, [(i, i ^ mask) for i in range(lax.axis_size(axis))])


def shift(x, step):
    size = lax.axis_size("expert")
    return lax.ppermute(x, "expert", [(i, (i + step) % size) for i in range(size)])


def staged():
    return lax.axis_size("batch") == 4 and lax.axis_size("expert") == 8


def gather_first(x):
    mz = lax.axis_index("expert") // 2
    ring = [shift(x, 2 * k) for k in (3, 2, 1)] + [x]
    ring = jnp.stack(ring + ring[:3])
    return lax.dynamic_slice_in_dim(ring, 3 - mz, 4, 0)


def gather_second(zs, beside):
    mb = lax.axis_index("batch")
    b = after([zs] + [swap(zs, "batch", k) for k in (1, 2, 3)], beside)
    odd, high = (mb & 1) == 1, (mb & 2) == 2
    u = [jnp.where(odd, b[i ^ 1], b[i]) for i in range(4)]
    return jnp.stack([jnp.where(high, u[i ^ 2], u[i]) for i in range(4)])


def gather_third(rows, beside=()):
    mc = lax.axis_index("expert") % 2
    other = after(swap(rows, "expert", 1), beside)
    both = jnp.stack(
        [jnp.where(mc == 0, rows, other), jnp.where(mc == 0, other, rows)], axis=2
    )
    return both.reshape(-1, rows.shape[-1])


def scatter_rows(g, before, beside):
    if not staged():
        return lax.psum_scatter(g, ALL, scatter_dimension=0, tiled=True).astype(F32), beside(before)
    mb, me = lax.axis_index("batch"), lax.axis_index("expert")
    mz, mc = me // 2, me % 2
    r, c = g.shape[0] // 32, g.shape[1]
    g = g.reshape(4, 4, 2, r, c)
    mine = jnp.where(mc == 0, g[:, :, 0], g[:, :, 1])
    other = swap(jnp.where(mc == 0, g[:, :, 1], g[:, :, 0]), "expert", 1)
    s = (mine.astype(F32) + other.astype(F32)).astype(BF16)
    s, before = after((s, before), before)
    made = beside(after(before, s))
    pick = lambda t, i: lax.dynamic_index_in_dim(t, i, 0, keepdims=False)
    parts = after([swap(pick(s, mb ^ k), "batch", k) for k in (1, 2, 3)], made)
    t = sum((p.astype(F32) for p in parts), pick(s, mb).astype(F32)).astype(BF16)
    parts = [shift(pick(t, (mz + k) % 4), 2 * k) for k in (1, 2, 3)]
    return sum((p.astype(F32) for p in parts), pick(t, mz).astype(F32)), made


def to_owners(x):
    return lax.all_to_all(x, "expert", split_axis=0, concat_axis=0, tiled=True)


def after(x, *others):
    return lax.optimization_barrier((x, others))[0]


def windows(length):
    for start in range(0, length, QROWS):
        yield start, max(0, start - REACH), start + QROWS


def half_masks():
    lane = lax.broadcasted_iota(jnp.int32, (1, LANES), 1)
    first = (lane < HEAD).astype(F32)
    return first, (first.astype(BF16), (1.0 - first).astype(BF16))


def attend_kernel(q_ref, k_ref, v_ref, row_ref, col_ref, out_ref, log_ref, mask_ref):
    length = q_ref.shape[0]

    @pl.when(pl.program_id(0) == 0)
    def _():
        for n, (start, low, stop) in enumerate(windows(length)):
            shape = (QROWS, stop - low)
            i = lax.broadcasted_iota(jnp.int32, shape, 0) + start
            j = lax.broadcasted_iota(jnp.int32, shape, 1) + low
            same = col_ref[start:stop, :] == row_ref[:, low:stop]
            mask_ref[n, :, : stop - low] = jnp.where((j <= i) & same, 0.0, -1e30)

    first, halves = half_masks()
    for n, (start, low, stop) in enumerate(windows(length)):
        q = q_ref[start:stop, :] * jnp.asarray(HEAD**-0.5, BF16)
        k, v = k_ref[low:stop, :], v_ref[low:stop, :]
        outs, logs = [], []
        for half in halves:
            s = dot_nt(q * half, k) + mask_ref[n, :, : stop - low]
            top = jnp.max(s, axis=1, keepdims=True)
            e = jnp.exp(s - top)
            sums = jnp.sum(e, axis=1, keepdims=True)
            outs.append(dot(e.astype(BF16), v) / sums)
            logs.append(top + jnp.log(sums))
        out_ref[start:stop, :] = (outs[0] * first + outs[1] * (1.0 - first)).astype(BF16)
        log_ref[start:stop, :] = logs[0] * first + logs[1] * (1.0 - first)


def attend(qkv, seg_row, seg_col, width):
    length = qkv.shape[0]
    pairs = width // LANES
    spec = lambda offset: pl.BlockSpec((length, LANES), lambda p, o=offset: (0, o + p))
    whole = lambda shape: pl.BlockSpec(shape, lambda p: (0,) * len(shape))
    return pl.pallas_call(
        attend_kernel,
        grid=(pairs,),
        in_specs=[spec(0), spec(pairs), spec(2 * pairs), whole((1, length)), whole((length, 1))],
        out_specs=[spec(0), spec(0)],
        out_shape=[
            jax.ShapeDtypeStruct((length, width), BF16),
            jax.ShapeDtypeStruct((length, width), F32),
        ],
        scratch_shapes=[pltpu.VMEM((length // QROWS, QROWS, QROWS + REACH), F32)],
        compiler_params=pltpu.CompilerParams(vmem_limit_bytes=VMEM),
        cost_estimate=pl.CostEstimate(
            flops=4 * length * 512 * width, bytes_accessed=12 * length * width, transcendentals=12 * length * 512
        ),
        name="attend",
    )(qkv, qkv, qkv, seg_row, seg_col)


def attend_back_kernel(
    q_ref, k_ref, v_ref, g_ref, log_ref, row_ref, col_ref, out_ref, mask_ref, dk_ref, dv_ref
):
    length = q_ref.shape[0]

    @pl.when(pl.program_id(0) == 0)
    def _():
        for n, (start, low, stop) in enumerate(windows(length)):
            shape = (stop - low, QROWS)
            j = lax.broadcasted_iota(jnp.int32, shape, 0) + low
            i = lax.broadcasted_iota(jnp.int32, shape, 1) + start
            same = col_ref[low:stop, :] == row_ref[:, start:stop]
            mask_ref[n, : stop - low, :] = jnp.where((j <= i) & same, 0.0, -1e30)

    dk_ref[...] = jnp.zeros_like(dk_ref)
    dv_ref[...] = jnp.zeros_like(dv_ref)
    _, halves = half_masks()
    scale = HEAD**-0.5
    for n, (start, low, stop) in enumerate(windows(length)):
        q = q_ref[start:stop, :] * jnp.asarray(scale, BF16)
        g = g_ref[start:stop, :]
        k, v = k_ref[low:stop, :], v_ref[low:stop, :]
        logs = log_ref[start:stop, :].T
        dq = jnp.zeros((QROWS, LANES), F32)
        for at, half in zip((0, HEAD), halves):
            qh, gh = q * half, g * half
            s = dot_nt(k, qh) + mask_ref[n, : stop - low, :]
            p = jnp.exp(s - logs[at : at + 1, :])
            dp = dot_nt(v, gh)
            centre = jnp.sum(dp * p, axis=0, keepdims=True)
            ds = (p * (dp - centre)).astype(BF16)
            dv_ref[low:stop, :] += dot(p.astype(BF16), gh)
            dk_ref[low:stop, :] += dot(ds, qh)
            dq += dot_tn(ds, k * half)
        out_ref[0, start:stop, :] = (dq * scale).astype(BF16)
    out_ref[1] = dk_ref[...].astype(BF16)
    out_ref[2] = dv_ref[...].astype(BF16)


def attend_back(qkv, grad, logs, seg_row, seg_col, width):
    length = qkv.shape[0]
    pairs = width // LANES
    spec = lambda offset: pl.BlockSpec((length, LANES), lambda p, o=offset: (0, o + p))
    whole = lambda shape: pl.BlockSpec(shape, lambda p: (0,) * len(shape))
    return pl.pallas_call(
        attend_back_kernel,
        grid=(pairs,),
        in_specs=[spec(0), spec(pairs), spec(2 * pairs), spec(0), spec(0), whole((1, length)), whole((length, 1))],
        out_specs=pl.BlockSpec((3, length, LANES), lambda p: (0, 0, p)),
        out_shape=jax.ShapeDtypeStruct((3, length, width), BF16),
        scratch_shapes=[
            pltpu.VMEM((length // QROWS, QROWS + REACH, QROWS), F32),
            pltpu.VMEM((length, LANES), F32),
            pltpu.VMEM((length, LANES), F32),
        ],
        compiler_params=pltpu.CompilerParams(vmem_limit_bytes=VMEM),
        cost_estimate=COST,
        name="attend_back",
    )(qkv, qkv, qkv, grad, logs, seg_row, seg_col)


def slot_ids(shape, axis, base, layout, first):
    groups, chunk, split, slots = layout
    at = lax.broadcasted_iota(jnp.int32, shape, axis) + base
    row, slot = at // slots, at % slots
    return (row // chunk * groups + first + row % chunk) // split * slots + slot


def dispatch_kernel(layout, first, id_ref, x_ref, out_ref):
    rows, tokens = out_ref.shape[0], x_ref.shape[0]
    ids = slot_ids((rows, 1), 0, pl.program_id(0) * rows, layout, first)
    chosen = jnp.where(ids == id_ref[...], 1.0, 0.0).astype(BF16)
    out_ref[...] = dot(chosen, x_ref[...]).astype(BF16)


def dispatch(ids, x, count, layout, first):
    tokens, width = x.shape
    block = min(count, 512)
    return pl.pallas_call(
        functools.partial(dispatch_kernel, layout, first),
        grid=(count // block,),
        in_specs=[
            pl.BlockSpec((1, tokens), lambda i: (0, 0)),
            pl.BlockSpec((tokens, width), lambda i: (0, 0)),
        ],
        out_specs=pl.BlockSpec((block, width), lambda i: (i, 0)),
        out_shape=jax.ShapeDtypeStruct((count, width), BF16),
        compiler_params=pltpu.CompilerParams(vmem_limit_bytes=VMEM),
        cost_estimate=pl.CostEstimate(
            flops=2 * count * tokens * width, bytes_accessed=4 * count * width, transcendentals=0
        ),
        name="dispatch",
    )(ids, x)


def combine_kernel(layout, firsts, id_ref, *refs):
    *x_refs, out_ref = refs
    out_ref[...] = jnp.zeros_like(out_ref)
    for first, x_ref in zip(firsts, x_refs):
        step = min(x_ref.shape[0], 512)
        for base in range(0, x_ref.shape[0], step):
            ids = slot_ids((1, step), 1, base, layout, first)
            chosen = jnp.where(id_ref[...] == ids, 1.0, 0.0).astype(BF16)
            out_ref[...] += dot(chosen, x_ref[base : base + step, :])


def combine(ids, xs, layout, firsts):
    tokens, (count, width), block = ids.shape[0], xs[0].shape, 256
    return pl.pallas_call(
        functools.partial(combine_kernel, layout, firsts),
        grid=(tokens // block,),
        in_specs=[pl.BlockSpec((block, 1), lambda i: (i, 0))]
        + [pl.BlockSpec((count, width), lambda i: (0, 0)) for _ in xs],
        out_specs=pl.BlockSpec((block, width), lambda i: (i, 0)),
        out_shape=jax.ShapeDtypeStruct((tokens, width), F32),
        compiler_params=pltpu.CompilerParams(vmem_limit_bytes=VMEM),
        cost_estimate=pl.CostEstimate(
            flops=2 * count * len(xs) * tokens * width,
            bytes_accessed=2 * count * len(xs) * width + 4 * tokens * width,
            transcendentals=0,
        ),
        name="combine",
    )(ids, *xs)


def merge_kernel(*refs):
    *parts, out_ref = refs
    owners, chunk, slots, width = out_ref.shape
    for l in range(chunk):
        both = parts[2 * l][...].astype(F32) + parts[2 * l + 1][...].astype(F32)
        out_ref[:, l] = both.astype(BF16).reshape(owners, slots, width)


def merge(pairs, owners, slots):
    rows, width = pairs[0][0].shape
    block = min(owners, 4)
    flat = [part for pair in pairs for part in pair]
    return pl.pallas_call(
        merge_kernel,
        grid=(owners // block,),
        in_specs=[pl.BlockSpec((block * slots, width), lambda i: (i, 0)) for _ in flat],
        out_specs=pl.BlockSpec((block, len(pairs), slots, width), lambda i: (i, 0, 0, 0)),
        out_shape=jax.ShapeDtypeStruct((owners, len(pairs), slots, width), BF16),
        compiler_params=pltpu.CompilerParams(vmem_limit_bytes=VMEM),
        cost_estimate=pl.CostEstimate(
            flops=len(flat) * rows * width, bytes_accessed=3 * len(flat) * rows * width, transcendentals=0
        ),
        name="merge",
    )(*flat)


def gelu_parts(x):
    size = jnp.abs(x)
    t = 1.0 / (1.0 + (0.3275911 * 0.5**0.5) * size)
    bell = jnp.exp(-0.5 * x * x)
    poly = t * (
        0.5 * 0.254829592
        + t * (0.5 * -0.284496736 + t * (0.5 * 1.421413741 + t * (0.5 * -1.453152027 + t * (0.5 * 1.061405429))))
    )
    tail = poly * bell
    return jnp.where(x < 0, tail, 1.0 - tail), bell * 0.3989422804014327


def expert_kernel(steps, experts, n, *refs):
    id_ref, h0, h1, z0, z1 = refs[:5]
    weights = refs[5:8], refs[8:11]
    wr_ref, p0, p1, d0, d1 = refs[11:16]
    own_g, got_g = refs[16 : 16 + n], refs[16 + n : 16 + 2 * n]
    refs = refs[16 + 2 * n :]
    groute, hid_a, hid_b, dpre_a, dpre_b, dexp_s, *sums = refs
    i = pl.program_id(0)
    width = wr_ref.shape[0]
    slots = h0.shape[2]
    rows = h0.shape[0] * slots
    sub = min(h0.shape[0], 4)
    hidden = hid_a.shape[1]

    def parts(w):
        if n == 1:
            return w[0].at[0, :width], w[0].at[0, width : 2 * width], w[0].at[0, 2 * width :]
        return w[0].at[0, :width], w[1].at[0], w[0].at[0, width:]

    @pl.when(i == 0)
    def _():
        groute[...] = jnp.zeros_like(groute)
        for total_ref in sums:
            total_ref[...] = jnp.zeros_like(total_ref)

    def work(h_ref, z_ref, p_ref, d_ref):
        lane = lax.broadcasted_iota(jnp.int32, (1, LANES), 1)
        own = (lane == id_ref[0]).astype(F32)

        def block(m, _):
            part = pl.ds(m * sub, sub)
            at = pl.ds(pl.multiple_of(m * sub * slots, sub * slots), sub * slots)
            h = h_ref[part, 0].reshape(sub * slots, width)
            logits = jnp.where(lane < experts, dot(h, wr_ref[...]), -1e30)
            e = jnp.exp(logits - jnp.max(logits, axis=1, keepdims=True))
            probs = e / jnp.sum(e, axis=1, keepdims=True)
            gate = jnp.sum(probs * own, axis=1, keepdims=True)
            dz = z_ref[part, 0].reshape(sub * slots, width).astype(F32)
            dexp = (gate * dz).astype(BF16)
            dexp_s[at, :] = dexp
            piece = back = None
            for (win, wout, bias), hid_s, dpre_s in zip(weights, (hid_a, hid_b), (dpre_a, dpre_b)):
                pre = dot(h, win[...]) + bias[...].astype(F32)
                phi, bell = gelu_parts(pre)
                hid = (pre * phi).astype(BF16)
                hid_s[at, :] = hid
                out = dot(hid, wout[...])
                piece = out if piece is None else piece + out
                dpre = (dot_nt(dexp, wout[...]) * (phi + pre * bell)).astype(BF16)
                dpre_s[at, :] = dpre
                out = dot_nt(dpre, win[...])
                back = out if back is None else back + out
            p_ref[at, :] = piece.astype(BF16)
            dgate = jnp.sum(dz * piece, axis=1, keepdims=True)
            dlog = (dgate * probs * (own - gate)).astype(BF16)
            d_ref[at, :] = (back + dot_nt(dlog, wr_ref[...])).astype(BF16)
            groute[...] += dot_tn(h, dlog)
            return 0

        lax.fori_loop(0, h_ref.shape[0] // sub, block, 0)
        for k, (dpre_s, hid_s) in enumerate(((dpre_a, hid_a), (dpre_b, hid_b))):
            to_win, to_bias, to_wout = sums[3 * k : 3 * k + 3]
            dpre = dpre_s[...]
            to_win[...] += dot_tn(h_ref[...].reshape(rows, width), dpre)
            to_bias[...] += jnp.broadcast_to(jnp.sum(dpre.astype(F32), axis=0, keepdims=True), to_bias.shape)
            to_wout[...] += dot_tn(hid_s[...], dexp_s[...])

    @pl.when(i < steps)
    def _():
        work(h0, z0, p0, d0)

    @pl.when(i >= steps)
    def _():
        work(h1, z1, p1, d1)

    @pl.when(i == 2 * steps - 1)
    def _():
        for k, g in enumerate((own_g, got_g)):
            win, wout, bias = parts(g)
            win[...] = sums[3 * k][...].astype(BF16)
            bias[...] = sums[3 * k + 1][...].astype(BF16)
            wout[...] = sums[3 * k + 2][...].astype(BF16)


def expert(expert_id, own_h, other_h, own_z, other_z, places, own_w, got_w, at, w_route, experts):
    sources, _, slots, width = own_h.shape
    rows = sources * slots
    hidden = own_w[0].shape[2]
    group = min(sources, 8)
    block, steps = group * slots, sources // group
    early = lambda i: jnp.minimum(i, steps - 1)
    late = lambda i: jnp.maximum(i - steps, 0)
    once = lambda shape: pl.BlockSpec(shape, lambda i: (0,) * len(shape))
    rows_spec = lambda place, when: pl.BlockSpec((group, 1, slots, width), lambda i: (when(i), place, 0, 0))
    weight = lambda w, k: pl.BlockSpec((None, *w.shape[1:]), lambda i: (k, 0, 0))
    out_first = pl.BlockSpec((block, width), lambda i: (early(i), 0))
    out_second = pl.BlockSpec((block, width), lambda i: (late(i), 0))
    shape = jax.ShapeDtypeStruct
    if hidden == width:
        grads = [shape((1, 2 * width + 16, hidden), BF16)]
    else:
        grads = [shape((1, width + 16, hidden), BF16), shape((1, hidden, width), BF16)]
    outs = [shape((rows, width), BF16)] * 4 + grads * 2 + [shape((width, LANES), F32)]
    spots = (own_h, other_h, own_z, other_z)
    return pl.pallas_call(
        functools.partial(expert_kernel, steps, experts, len(grads)),
        grid=(2 * steps,),
        in_specs=[pl.BlockSpec(memory_space=pltpu.SMEM)]
        + [rows_spec(p, w) for p, w in zip(places, (early, late, early, late))]
        + [weight(w, k) for w, k in zip((*own_w, *got_w), at)]
        + [once(w_route.shape)],
        out_specs=[out_first, out_second, out_first, out_second] + [once(o.shape) for o in outs[4:]],
        out_shape=outs,
        scratch_shapes=[
            *[pltpu.VMEM((block, hidden), BF16)] * 4,
            pltpu.VMEM((block, width), BF16),
            *[pltpu.VMEM(s, F32) for s in ((width, hidden), (16, hidden), (hidden, width))] * 2,
        ],
        compiler_params=pltpu.CompilerParams(vmem_limit_bytes=VMEM),
        cost_estimate=pl.CostEstimate(
            flops=48 * rows * hidden * width, bytes_accessed=20 * width * hidden, transcendentals=4 * rows * hidden
        ),
        name="expert",
    )(expert_id, *spots, *own_w, *got_w, w_route)


def finish_kernel(n, *refs):
    parts, (win, wout, bias) = refs[: 6 * n], refs[-3:]
    for l in range(n):
        for k, out in enumerate((win, wout, bias)):
            out[l] = parts[6 * l + k][...].astype(F32) + parts[6 * l + 3 + k][...].astype(F32)


def finish(own, got):
    n, (_, height, hidden) = len(own), own[0].shape
    width = (height - 16) // 2
    tile = 128
    steps = width // tile
    spec = lambda r, k: pl.BlockSpec((None, r, hidden), lambda i: (0, k(i), 0))
    three = [spec(tile, lambda i: i), spec(tile, lambda i: steps + i), spec(16, lambda i: 2 * width // 16)]
    flat = [x for pair in zip(own, got) for a in pair for x in (a, a, a)]
    big = pl.BlockSpec((n, tile, hidden), lambda i: (0, i, 0))
    shape = jax.ShapeDtypeStruct
    return pl.pallas_call(
        functools.partial(finish_kernel, n),
        grid=(steps,),
        in_specs=three * (2 * n),
        out_specs=[big, big, pl.BlockSpec((n, 16, hidden), lambda i: (0, 0, 0))],
        out_shape=[shape((n, width, hidden), F32), shape((n, width, hidden), F32), shape((n, 16, hidden), F32)],
        compiler_params=pltpu.CompilerParams(vmem_limit_bytes=VMEM),
        cost_estimate=pl.CostEstimate(
            flops=2 * n * height * hidden, bytes_accessed=8 * n * height * hidden, transcendentals=0
        ),
        name="finish",
    )(*flat)


def to_send_kernel(in_ref, out_ref, *refs):
    for l in range(in_ref.shape[0]):
        refs[2 * l][0] = in_ref[l]
        refs[2 * l + 1][0] = out_ref[l]


def to_send(w_in, w_out):
    groups = w_in.shape[0]
    steps = w_in.shape[1] // 128
    spec = lambda a, k: pl.BlockSpec((k, a.shape[1] // steps, a.shape[2]), lambda i: (0, i, 0))
    flat = pl.pallas_call(
        to_send_kernel,
        grid=(steps,),
        in_specs=[spec(w_in, groups), spec(w_out, groups)],
        out_specs=[spec(w_in, 1), spec(w_out, 1)] * groups,
        out_shape=[jax.ShapeDtypeStruct((1, *a.shape[1:]), BF16) for a in (w_in, w_out)] * groups,
        compiler_params=pltpu.CompilerParams(vmem_limit_bytes=VMEM),
        name="to_send",
    )(w_in, w_out)
    return [flat[2 * l : 2 * l + 2] for l in range(groups)]


def turn_kernel(x_ref, y_ref, x_out, y_out):
    x_out[...] = x_ref[...].T
    y_out[...] = y_ref[...].T


def turn(x, y):
    whole = lambda a, b: pl.BlockSpec((a, b), lambda i: (0, 0))
    tokens, width = x.shape
    return pl.pallas_call(
        turn_kernel,
        grid=(1,),
        in_specs=[whole(tokens, width)] * 2,
        out_specs=[whole(width, tokens)] * 2,
        out_shape=[jax.ShapeDtypeStruct((width, tokens), x.dtype)] * 2,
        compiler_params=pltpu.CompilerParams(vmem_limit_bytes=VMEM),
        name="turn",
    )(x, y)


def outer_kernel(h_ref, a_ref, g_ref, b_ref, rest_ref, sums_ref, out_ref):
    width = b_ref.shape[1]
    for k in range(3):
        out_ref[:, k * width : (k + 1) * width] = dot(h_ref[...], g_ref[k]).astype(BF16)
    out_ref[:, 3 * width : 4 * width] = dot(a_ref[...], b_ref[...]).astype(BF16)
    out_ref[:, 4 * width : 4 * width + LANES] = rest_ref[...]
    out_ref[:, 4 * width + LANES :] = sums_ref[...].T.astype(BF16)


def outer(h, a, g, b, rest, sums):
    width, tokens = h.shape
    tile = 256
    whole = lambda *shape: pl.BlockSpec(shape, lambda i: (0,) * len(shape))
    rows = lambda n: pl.BlockSpec((tile, n), lambda i: (i, 0))
    columns = 4 * width + 2 * LANES
    return pl.pallas_call(
        outer_kernel,
        grid=(width // tile,),
        in_specs=[
            rows(tokens), rows(tokens), whole(3, tokens, width), whole(tokens, width), rows(LANES),
            pl.BlockSpec((LANES, tile), lambda i: (0, i)),
        ],
        out_specs=rows(columns),
        out_shape=jax.ShapeDtypeStruct((width, columns), BF16),
        compiler_params=pltpu.CompilerParams(vmem_limit_bytes=VMEM),
        cost_estimate=COST,
        name="outer",
    )(h, a, g, b, rest, sums)


def input_kernel(g_ref, w_ref, x_ref, dy_ref, gain_ref, out_ref, sums_ref):
    width = x_ref.shape[1]

    @pl.when(pl.program_id(0) == 0)
    def _():
        sums_ref[...] = jnp.zeros_like(sums_ref)

    grad = dot_nt(g_ref[0], w_ref[:, :width])
    for k in (1, 2):
        grad += dot_nt(g_ref[k], w_ref[:, k * width : (k + 1) * width])
    unit, rstd = normed(x_ref[...].astype(F32))
    out_ref[...] = dy_ref[...] + norm_back(grad, gain_ref[...], unit, rstd)
    add = lambda t: jnp.sum(t, axis=0, keepdims=True)
    sums_ref[0:1, :] += add(grad * unit)
    sums_ref[1:2, :] += add(grad)
    sums_ref[2:3, :] += add(g_ref[0].astype(F32))
    sums_ref[3:4, :] += add(g_ref[2].astype(F32))


def input_back(g, wide, tokens, dy, gain):
    count, width = tokens.shape
    tile = 256
    rows = pl.BlockSpec((tile, width), lambda i: (i, 0))
    whole = lambda *shape: pl.BlockSpec(shape, lambda i: (0,) * len(shape))
    return pl.pallas_call(
        input_kernel,
        grid=(count // tile,),
        in_specs=[
            pl.BlockSpec((3, tile, width), lambda i: (0, i, 0)), whole(*wide.shape), rows, rows, whole(1, width),
        ],
        out_specs=[rows, whole(LANES, width)],
        out_shape=[jax.ShapeDtypeStruct((count, width), F32), jax.ShapeDtypeStruct((LANES, width), F32)],
        compiler_params=pltpu.CompilerParams(vmem_limit_bytes=VMEM),
        cost_estimate=COST,
        name="input_back",
    )(g, wide, tokens, dy, gain)


def normed(x):
    centred = x - jnp.mean(x, axis=-1, keepdims=True)
    rstd = lax.rsqrt(jnp.mean(centred * centred, axis=-1, keepdims=True) + EPSILON)
    return centred * rstd, rstd


def norm_back(grad, gain, unit, rstd):
    g = grad * gain
    mean = lambda t: jnp.mean(t, axis=-1, keepdims=True)
    return rstd * (g - mean(g) - unit * mean(g * unit))


def pad_columns(x, count):
    return jnp.pad(x, ((0, 0), (0, count - x.shape[1])))


def up(count):
    return -(-count // LANES) * LANES


def local(
    tokens, cotangent, segment_ids, routes, capacity, ln1_gain, ln1_bias, w_query, b_query, w_key, w_value,
    b_value, w_output, b_output, ln2_gain, ln2_bias, w_router, w_in, b_in, w_out, b_out,
):
    row_count, width = tokens.shape
    experts = capacity.shape[0]
    slots = 2 * row_count // experts
    groups = w_in.shape[0]
    owners = lax.axis_size("expert")
    split = groups * owners // experts
    share = w_query.shape[0]
    devices = lax.axis_size("batch") * owners
    me = lax.axis_index("expert")
    chunk = min(2, groups)
    layout = (groups, chunk, split, slots)
    firsts = tuple(range(0, groups, chunk))
    pair = lambda first: range(first, first + chunk)
    heavy = lambda l: 1 if l % 2 == 0 else 2
    light = lambda l: 3 - heavy(l)

    spread = -(-experts // share)
    fold = lambda x: jnp.pad(x, (0, spread * share - experts)).reshape(spread, share).T
    unfold = lambda x: x.T.reshape(-1)[:experts]

    chosen = routes[:, 0]
    picked = chosen[:, None] == jnp.arange(experts, dtype=jnp.int32)[None, :]
    picked_float = picked.astype(F32)
    position = jnp.arange(row_count, dtype=jnp.int32)
    earlier = (position[None, :] < position[:, None]).astype(BF16)
    rank = dot(earlier, picked.astype(BF16))
    slot = jnp.sum(rank * picked_float, axis=1)
    limit = jnp.sum(capacity.astype(F32)[None, :] * picked_float, axis=1)
    kept = slot < limit
    kept_float = kept.astype(F32)
    ids = jnp.where(kept, chosen * slots + slot.astype(jnp.int32), -1)
    id_row, id_col = ids[None, :], ids[:, None]
    counts = jnp.sum(picked_float, axis=0)

    def send(x, first, count):
        rows = dispatch(id_row, x, count * owners * slots, (groups, count, split, slots), first)
        return rows.reshape(owners, count, slots, width)

    grad_send = send(cotangent, 0, groups)

    small = jnp.stack([ln1_gain, ln1_bias, b_query, b_value, b_output, ln2_gain, ln2_bias], axis=1)
    tally = fold(counts).astype(BF16)
    extra = pad_columns(jnp.concatenate([small, tally], axis=1), up(7 + spread))
    wide = jnp.concatenate([w_query, w_key, w_value, extra], axis=1)
    rest = jnp.concatenate([w_router, b_out.T], axis=1)
    rest = jnp.concatenate([w_output, pad_columns(rest, up(2 * experts))], axis=1)
    if staged():
        wide, rest = gather_first(wide), gather_first(rest)
        rest_first = rest
        sent_w = to_send(*after((w_in, w_out), grad_send))
        free = gather_second(wide, (grad_send, sent_w))
        wide = gather_third(free)
        rest = after(rest, free)
    else:
        wide = lax.all_gather(wide, ALL, axis=0, tiled=True)
        rest = lax.all_gather(rest, ALL, axis=0, tiled=True)
        free = rest_first = ()
        sent_w = to_send(w_in, w_out)

    bias_rows = b_in[:, None, :]
    got_bias = [swap(after(bias_rows, free), "batch", mask) for mask in (1, 2)]
    got_w, last = [], free
    for l in range(groups):
        if l % chunk == 0:
            last = got_w[-chunk:] or free
        got_w.append([swap(w, "batch", heavy(l)) for w in after(sent_w[l], last)])

    own_z = to_owners(after(grad_send, rest_first))
    theirs = lambda rows, l, at: swap(rows[:, at : at + 1], "batch", light(l))
    other_z = [theirs(own_z, l, l) for l in range(groups)]

    vectors = wide[:, 3 * width : 3 * width + 7].astype(F32).T
    gain_one, shift_one, bias_query, bias_value, bias_output, gain_two, shift_two = vectors
    tallies = wide[:, 3 * width + 7 : 3 * width + 7 + spread].astype(F32).reshape(devices, share, spread)
    all_counts = unfold(jnp.sum(tallies, axis=0))
    token_total = float(row_count * devices)
    fraction = all_counts / token_total

    inputs = tokens.astype(F32)
    unit_one, rstd_one = normed(inputs)
    h_one = (unit_one * gain_one + shift_one).astype(BF16)
    nothing = jnp.zeros((width,), F32)
    bias = jnp.concatenate([bias_query, nothing, bias_value, jnp.zeros((wide.shape[1] - 3 * width,), F32)])
    qkv = (dot(h_one, wide) + bias).astype(BF16)
    if staged():
        rest = gather_second(rest, qkv)
    seg_row = segment_ids.reshape(1, row_count)
    seg_col = segment_ids.reshape(row_count, 1)
    attended, logs = attend(qkv, seg_row, seg_col, width)
    attended = after(attended, [w[0] for w in got_w[:chunk]])
    if staged():
        rest = gather_third(rest, attended)
    full_output = rest[:, :width]
    full_router = pad_columns(rest[:, width : width + experts], LANES)
    bias_expert = rest[:, width + experts : width + 2 * experts].T
    resid = inputs + dot(attended, full_output) + bias_output
    unit_two, rstd_two = normed(resid)
    h_two = (unit_two * gain_two + shift_two).astype(BF16)
    h_two = after(h_two, own_z, [w[1] for w in got_w[:chunk]])

    rows = [send(h_two, first, chunk) for first in firsts]
    token_rows = []
    for at in range(len(firsts)):
        if at:
            rows[at] = after(rows[at], token_rows[-1], [w[0] for w in got_w[chunk:]])
        token_rows.append(to_owners(rows[at]))
    token_rows = [after(t, rows) for t in token_rows]
    their_h = [token_rows[l // chunk][:, l % chunk : l % chunk + 1] for l in range(groups)]
    their_h = [lax.optimization_barrier(their_h[first : first + chunk]) for first in firsts]
    other_h = [swap(their_h[l // chunk][l % chunk], "batch", light(l)) for l in range(groups)]
    h_turned, att_turned = turn(h_one, attended)

    router_probs = jax.nn.softmax(dot(h_two, full_router)[:, :experts], axis=-1)
    mixing = kept_float * jnp.sum(router_probs * picked_float, axis=1)
    grad_out = cotangent.astype(F32)
    expert_bias = dot(picked.astype(BF16), bias_expert)
    gate_bias = kept_float * jnp.sum(grad_out * expert_bias, axis=1)
    grad_probs = picked_float * gate_bias[:, None] + BALANCE * experts * fraction[None, :] / token_total
    grad_logits = router_probs * (grad_probs - jnp.sum(grad_probs * router_probs, axis=1, keepdims=True))
    grad_logits = grad_logits.astype(BF16)
    mixed = picked_float * mixing[:, None]
    mixed_high = mixed.astype(BF16)
    mixed_low = (mixed - mixed_high.astype(F32)).astype(BF16)
    grad_bias_expert = dot_tn(cotangent, mixed_high) + dot_tn(cotangent, mixed_low)
    home_router = dot_tn(h_two, grad_logits)
    home_h_two = dot_nt(grad_logits, full_router[:, :experts])
    home_h_two, home_router, grad_bias_expert, probs_sum = lax.optimization_barrier(
        (home_h_two, home_router, grad_bias_expert, jnp.sum(router_probs, axis=0))
    )
    made, returned, piece_sums, got_g = [], [], [], []
    for at, first in enumerate(firsts):
        for l in pair(first):
            number = ((me * groups + l) // split).astype(jnp.int32).reshape(1)
            if l == 0:
                number = after(number, h_turned, home_h_two)
            if l == 1:
                number = after(number, made[-1], got_w[-chunk:], their_h)
            made.append(
                expert(
                    number, token_rows[at], other_h[l], own_z, other_z[l], (l - first, 0, l, 0),
                    (w_in, w_out, bias_rows), (*got_w[l], got_bias[heavy(l) - 1]), (l, l, l, 0, 0, l),
                    full_router, experts,
                )
            )
        sums = [(made[l][2], swap(after(made[l][3], other_h), "batch", light(l))) for l in pair(first)]
        rows = merge(sums, owners, slots)
        if returned:
            rows = after(rows, returned[-1], got_g)
        returned.append(to_owners(rows).reshape(-1, width))
        n = (len(made[0]) - 5) // 2
        if first + chunk == groups:
            piece_sums = [(m[0], swap(after(m[1], sums), "batch", light(l))) for l, m in enumerate(made)]
        for l in pair(first):
            grads = after(made[l][4 + n : 4 + 2 * n], sums, other_h, piece_sums)
            got_g.append([swap(g, "batch", heavy(l)) for g in grads])
    own_g = [m[4 : 4 + n] for m in made]

    grad_router = home_router + sum(m[-1] for m in made)[:, :experts]

    grad_h_two = home_h_two + combine(after(id_col, piece_sums), returned, layout, firsts)
    grad_resid = grad_out + norm_back(grad_h_two, gain_two, unit_two, rstd_two)
    grad_branch = grad_resid.astype(BF16)
    grad_att = dot_nt(grad_branch, full_output).astype(BF16)
    columns = lambda *rows: jnp.stack(rows, axis=1)
    prob_sums = jnp.tile(fold(probs_sum), (devices, 1))
    sums = columns(
        jnp.sum(grad_h_two * unit_two, axis=0), jnp.sum(grad_h_two, axis=0), jnp.sum(grad_branch.astype(F32), axis=0)
    )
    packed = jnp.concatenate([grad_router, grad_bias_expert, sums, prob_sums], axis=1)
    packed = pad_columns(packed, LANES).astype(BF16)
    merged = merge(after(piece_sums, grad_att, packed), owners, slots)
    pieces = to_owners(merged).reshape(-1, width)
    grad_att = after(grad_att, merged, packed)
    dqkv = attend_back(qkv, grad_att, logs, seg_row, seg_col, width)

    dqkv, got_g = after((dqkv, got_g), got_g)
    input_grad, sums = input_back(dqkv, wide, tokens, grad_resid, gain_one[None])
    def close(waiting):
        own, got, _ = waiting
        if n == 1:
            win, wout, bias = finish([g[0] for g in own], [g[0] for g in got])
            return win, bias[:, 0], wout
        both = [[a[0].astype(F32) + b[0].astype(F32) for a, b in zip(*pair_g)] for pair_g in zip(own, got)]
        return (
            jnp.stack([g[0][:width] for g in both]),
            jnp.stack([g[0][width] for g in both]),
            jnp.stack([g[1] for g in both]),
        )

    wide_sum, (grad_w_in, grad_b_in, grad_w_out) = scatter_rows(
        outer(h_turned, att_turned, dqkv, grad_branch, packed, sums), (own_g, got_g, pieces), close
    )
    pieces = after(pieces, grad_b_in)
    fetched = combine(id_col, [pieces], (groups, groups, split, slots), (0,))
    block_out = (resid + mixing[:, None] * (fetched + expert_bias)).astype(BF16)
    router_sum = wide_sum[:, 4 * width : 4 * width + 2 * experts]
    side = wide_sum[:, 4 * width + 2 * experts :]
    late_side = wide_sum[:, 4 * width + LANES :]
    mean_probs = unfold(side[:, 3 : 3 + spread]) / token_total
    balance_loss = experts * jnp.sum(fraction * mean_probs)
    expert_shares = jnp.stack([experts * fraction, experts * mean_probs])

    return (
        block_out,
        balance_loss,
        expert_shares,
        input_grad,
        late_side[:, 0],
        late_side[:, 1],
        wide_sum[:, :width],
        late_side[:, 2],
        wide_sum[:, width : 2 * width],
        wide_sum[:, 2 * width : 3 * width],
        late_side[:, 3],
        wide_sum[:, 3 * width : 4 * width],
        side[:, 2],
        side[:, 0],
        side[:, 1],
        router_sum[:, :experts],
        grad_w_in,
        grad_b_in,
        grad_w_out,
        router_sum[:, experts:].T,
    )


def solution(mesh):
    rows, split = P(ALL, None), P(ALL)
    experts = (P("expert", None, "batch"), P("expert", "batch"), P("expert", "batch", None), P(None, ALL))
    return jax.shard_map(
        local,
        mesh=mesh,
        in_specs=(
            rows, rows, rows, rows, P(), split, split, rows, split, rows, rows, split, rows, split, split, split,
            rows, *experts,
        ),
        out_specs=(
            rows, P(), P(), rows, split, split, rows, split, rows, rows, split, rows, split, split, split, rows,
            *experts,
        ),
        check_vma=False,
    )
```

```python
import functools

import jax
import jax.numpy as jnp
from jax import lax
from jax.experimental import pallas as pl
from jax.experimental.pallas import tpu as pltpu
from jax.sharding import PartitionSpec as P

HEAD = 64
LANES = 128
REACH = 384
QROWS = 256
EPSILON = 1e-05
BALANCE = 0.01
ALL = ("batch", "expert")
VMEM = 60 * 1024 * 1024
COST = pl.CostEstimate(flops=1, bytes_accessed=1, transcendentals=0)
F32 = jnp.float32
BF16 = jnp.bfloat16


def dot(a, b):
    return jnp.dot(a, b, preferred_element_type=F32)


def dot_nt(a, b):
    return lax.dot_general(a, b, (((1,), (1,)), ((), ())), preferred_element_type=F32)


def dot_tn(a, b):
    return lax.dot_general(a, b, (((0,), (0,)), ((), ())), preferred_element_type=F32)


def swap(x, axis, mask):
    return lax.ppermute(x, axis, [(i, i ^ mask) for i in range(lax.axis_size(axis))])


def shift(x, step):
    size = lax.axis_size("expert")
    return lax.ppermute(x, "expert", [(i, (i + step) % size) for i in range(size)])


def staged():
    return lax.axis_size("batch") == 4 and lax.axis_size("expert") == 8


def gather_first(x):
    mz = lax.axis_index("expert") // 2
    ring = [shift(x, 2 * k) for k in (3, 2, 1)] + [x]
    ring = jnp.stack(ring + ring[:3])
    return lax.dynamic_slice_in_dim(ring, 3 - mz, 4, 0)


def gather_second(zs, beside):
    mb = lax.axis_index("batch")
    b = after([zs] + [swap(zs, "batch", k) for k in (1, 2, 3)], beside)
    odd, high = (mb & 1) == 1, (mb & 2) == 2
    u = [jnp.where(odd, b[i ^ 1], b[i]) for i in range(4)]
    return jnp.stack([jnp.where(high, u[i ^ 2], u[i]) for i in range(4)])


def gather_third(rows, beside=()):
    mc = lax.axis_index("expert") % 2
    other = after(swap(rows, "expert", 1), beside)
    both = jnp.stack(
        [jnp.where(mc == 0, rows, other), jnp.where(mc == 0, other, rows)], axis=2
    )
    return both.reshape(-1, rows.shape[-1])


def scatter_rows(g, before, beside):
    if not staged():
        return lax.psum_scatter(g, ALL, scatter_dimension=0, tiled=True).astype(F32), beside(before)
    mb, me = lax.axis_index("batch"), lax.axis_index("expert")
    mz, mc = me // 2, me % 2
    r, c = g.shape[0] // 32, g.shape[1]
    g = g.reshape(4, 4, 2, r, c)
    mine = jnp.where(mc == 0, g[:, :, 0], g[:, :, 1])
    other = swap(jnp.where(mc == 0, g[:, :, 1], g[:, :, 0]), "expert", 1)
    s = (mine.astype(F32) + other.astype(F32)).astype(BF16)
    s, before = after((s, before), before)
    made = beside(after(before, s))
    pick = lambda t, i: lax.dynamic_index_in_dim(t, i, 0, keepdims=False)
    parts = after([swap(pick(s, mb ^ k), "batch", k) for k in (1, 2, 3)], made)
    t = sum((p.astype(F32) for p in parts), pick(s, mb).astype(F32)).astype(BF16)
    parts = [shift(pick(t, (mz + k) % 4), 2 * k) for k in (1, 2, 3)]
    return sum((p.astype(F32) for p in parts), pick(t, mz).astype(F32)), made


def to_owners(x):
    return lax.all_to_all(x, "expert", split_axis=0, concat_axis=0, tiled=True)


def after(x, *others):
    return lax.optimization_barrier((x, others))[0]


def windows(length):
    for start in range(0, length, QROWS):
        yield start, max(0, start - REACH), start + QROWS


def half_masks():
    lane = lax.broadcasted_iota(jnp.int32, (1, LANES), 1)
    first = (lane < HEAD).astype(F32)
    return first, (first.astype(BF16), (1.0 - first).astype(BF16))


def attend_kernel(q_ref, k_ref, v_ref, row_ref, col_ref, out_ref, log_ref, mask_ref):
    length = q_ref.shape[0]

    @pl.when(pl.program_id(0) == 0)
    def _():
        for n, (start, low, stop) in enumerate(windows(length)):
            shape = (QROWS, stop - low)
            i = lax.broadcasted_iota(jnp.int32, shape, 0) + start
            j = lax.broadcasted_iota(jnp.int32, shape, 1) + low
            same = col_ref[start:stop, :] == row_ref[:, low:stop]
            mask_ref[n, :, : stop - low] = jnp.where((j <= i) & same, 0.0, -1e30)

    first, halves = half_masks()
    for n, (start, low, stop) in enumerate(windows(length)):
        q = q_ref[start:stop, :] * jnp.asarray(HEAD**-0.5, BF16)
        both = jnp.concatenate([q * half for half in halves])
        mask = mask_ref[n, :, : stop - low]
        s = dot_nt(both, k_ref[low:stop, :]) + jnp.concatenate([mask, mask])
        top = jnp.max(s, axis=1, keepdims=True)
        e = jnp.exp(s - top)
        sums = jnp.sum(e, axis=1, keepdims=True)
        out = dot(e.astype(BF16), v_ref[low:stop, :]) / sums
        logs = top + jnp.log(sums)
        out_ref[start:stop, :] = (out[:QROWS] * first + out[QROWS:] * (1.0 - first)).astype(BF16)
        log_ref[start:stop, :] = logs[:QROWS] * first + logs[QROWS:] * (1.0 - first)


def attend(qkv, seg_row, seg_col, width):
    length = qkv.shape[0]
    pairs = width // LANES
    spec = lambda offset: pl.BlockSpec((length, LANES), lambda p, o=offset: (0, o + p))
    whole = lambda shape: pl.BlockSpec(shape, lambda p: (0,) * len(shape))
    return pl.pallas_call(
        attend_kernel,
        grid=(pairs,),
        in_specs=[spec(0), spec(pairs), spec(2 * pairs), whole((1, length)), whole((length, 1))],
        out_specs=[spec(0), spec(0)],
        out_shape=[
            jax.ShapeDtypeStruct((length, width), BF16),
            jax.ShapeDtypeStruct((length, width), F32),
        ],
        scratch_shapes=[pltpu.VMEM((length // QROWS, QROWS, QROWS + REACH), F32)],
        compiler_params=pltpu.CompilerParams(vmem_limit_bytes=VMEM),
        cost_estimate=pl.CostEstimate(
            flops=4 * length * 512 * width, bytes_accessed=12 * length * width, transcendentals=12 * length * 512
        ),
        name="attend",
    )(qkv, qkv, qkv, seg_row, seg_col)


def attend_back_kernel(
    q_ref, k_ref, v_ref, g_ref, log_ref, row_ref, col_ref, out_ref, mask_ref, dk_ref, dv_ref
):
    length = q_ref.shape[0]

    @pl.when(pl.program_id(0) == 0)
    def _():
        for n, (start, low, stop) in enumerate(windows(length)):
            shape = (stop - low, QROWS)
            j = lax.broadcasted_iota(jnp.int32, shape, 0) + low
            i = lax.broadcasted_iota(jnp.int32, shape, 1) + start
            same = col_ref[low:stop, :] == row_ref[:, start:stop]
            mask_ref[n, : stop - low, :] = jnp.where((j <= i) & same, 0.0, -1e30)

    dk_ref[...] = jnp.zeros_like(dk_ref)
    dv_ref[...] = jnp.zeros_like(dv_ref)
    first, halves = half_masks()
    scale = HEAD**-0.5
    for n, (start, low, stop) in enumerate(windows(length)):
        q = q_ref[start:stop, :] * jnp.asarray(scale, BF16)
        g = g_ref[start:stop, :]
        k, v = k_ref[low:stop, :], v_ref[low:stop, :]
        turned = log_ref[start:stop, :].T
        logs = jnp.concatenate([turned[:1, :], turned[HEAD : HEAD + 1, :]], axis=1)
        qs = jnp.concatenate([q * half for half in halves])
        gs = jnp.concatenate([g * half for half in halves])
        mask = mask_ref[n, : stop - low, :]
        p = jnp.exp(dot_nt(k, qs) + jnp.concatenate([mask, mask], axis=1) - logs)
        dp = dot_nt(v, gs)
        centre = jnp.sum(dp * p, axis=0, keepdims=True)
        ds = (p * (dp - centre)).astype(BF16)
        dv_ref[low:stop, :] += dot(p.astype(BF16), gs)
        dk_ref[low:stop, :] += dot(ds, qs)
        dqs = dot_tn(ds, k)
        dq = dqs[:QROWS] * first + dqs[QROWS:] * (1.0 - first)
        out_ref[0, start:stop, :] = (dq * scale).astype(BF16)
    out_ref[1] = dk_ref[...].astype(BF16)
    out_ref[2] = dv_ref[...].astype(BF16)


def attend_back(qkv, grad, logs, seg_row, seg_col, width):
    length = qkv.shape[0]
    pairs = width // LANES
    spec = lambda offset: pl.BlockSpec((length, LANES), lambda p, o=offset: (0, o + p))
    whole = lambda shape: pl.BlockSpec(shape, lambda p: (0,) * len(shape))
    return pl.pallas_call(
        attend_back_kernel,
        grid=(pairs,),
        in_specs=[spec(0), spec(pairs), spec(2 * pairs), spec(0), spec(0), whole((1, length)), whole((length, 1))],
        out_specs=pl.BlockSpec((3, length, LANES), lambda p: (0, 0, p)),
        out_shape=jax.ShapeDtypeStruct((3, length, width), BF16),
        scratch_shapes=[
            pltpu.VMEM((length // QROWS, QROWS + REACH, QROWS), F32),
            pltpu.VMEM((length, LANES), F32),
            pltpu.VMEM((length, LANES), F32),
        ],
        compiler_params=pltpu.CompilerParams(vmem_limit_bytes=VMEM),
        cost_estimate=COST,
        name="attend_back",
    )(qkv, qkv, qkv, grad, logs, seg_row, seg_col)


def slot_ids(shape, axis, base, layout, first):
    groups, chunk, split, slots = layout
    at = lax.broadcasted_iota(jnp.int32, shape, axis) + base
    row, slot = at // slots, at % slots
    return (row // chunk * groups + first + row % chunk) // split * slots + slot


def dispatch_kernel(layout, first, id_ref, x_ref, out_ref):
    rows, tokens = out_ref.shape[0], x_ref.shape[0]
    ids = slot_ids((rows, 1), 0, pl.program_id(0) * rows, layout, first)
    chosen = jnp.where(ids == id_ref[...], 1.0, 0.0).astype(BF16)
    out_ref[...] = dot(chosen, x_ref[...]).astype(BF16)


def dispatch(ids, x, count, layout, first):
    tokens, width = x.shape
    block = min(count, 512)
    return pl.pallas_call(
        functools.partial(dispatch_kernel, layout, first),
        grid=(count // block,),
        in_specs=[
            pl.BlockSpec((1, tokens), lambda i: (0, 0)),
            pl.BlockSpec((tokens, width), lambda i: (0, 0)),
        ],
        out_specs=pl.BlockSpec((block, width), lambda i: (i, 0)),
        out_shape=jax.ShapeDtypeStruct((count, width), BF16),
        compiler_params=pltpu.CompilerParams(vmem_limit_bytes=VMEM),
        cost_estimate=pl.CostEstimate(
            flops=2 * count * tokens * width, bytes_accessed=4 * count * width, transcendentals=0
        ),
        name="dispatch",
    )(ids, x)


def combine_kernel(layout, firsts, id_ref, *refs):
    *x_refs, out_ref = refs
    out_ref[...] = jnp.zeros_like(out_ref)
    for first, x_ref in zip(firsts, x_refs):
        step = min(x_ref.shape[0], 512)
        for base in range(0, x_ref.shape[0], step):
            ids = slot_ids((1, step), 1, base, layout, first)
            chosen = jnp.where(id_ref[...] == ids, 1.0, 0.0).astype(BF16)
            out_ref[...] += dot(chosen, x_ref[base : base + step, :])


def combine(ids, xs, layout, firsts):
    tokens, (count, width), block = ids.shape[0], xs[0].shape, 256
    return pl.pallas_call(
        functools.partial(combine_kernel, layout, firsts),
        grid=(tokens // block,),
        in_specs=[pl.BlockSpec((block, 1), lambda i: (i, 0))]
        + [pl.BlockSpec((count, width), lambda i: (0, 0)) for _ in xs],
        out_specs=pl.BlockSpec((block, width), lambda i: (i, 0)),
        out_shape=jax.ShapeDtypeStruct((tokens, width), F32),
        compiler_params=pltpu.CompilerParams(vmem_limit_bytes=VMEM),
        cost_estimate=pl.CostEstimate(
            flops=2 * count * len(xs) * tokens * width,
            bytes_accessed=2 * count * len(xs) * width + 4 * tokens * width,
            transcendentals=0,
        ),
        name="combine",
    )(ids, *xs)


def merge_kernel(*refs):
    *parts, out_ref = refs
    owners, chunk, slots, width = out_ref.shape
    for l in range(chunk):
        both = parts[2 * l][...].astype(F32) + parts[2 * l + 1][...].astype(F32)
        out_ref[:, l] = both.astype(BF16).reshape(owners, slots, width)


def merge(pairs, owners, slots):
    rows, width = pairs[0][0].shape
    block = min(owners, 4)
    flat = [part for pair in pairs for part in pair]
    return pl.pallas_call(
        merge_kernel,
        grid=(owners // block,),
        in_specs=[pl.BlockSpec((block * slots, width), lambda i: (i, 0)) for _ in flat],
        out_specs=pl.BlockSpec((block, len(pairs), slots, width), lambda i: (i, 0, 0, 0)),
        out_shape=jax.ShapeDtypeStruct((owners, len(pairs), slots, width), BF16),
        compiler_params=pltpu.CompilerParams(vmem_limit_bytes=VMEM),
        cost_estimate=pl.CostEstimate(
            flops=len(flat) * rows * width, bytes_accessed=3 * len(flat) * rows * width, transcendentals=0
        ),
        name="merge",
    )(*flat)


def gelu_parts(x):
    size = jnp.abs(x)
    t = 1.0 / (1.0 + (0.3275911 * 0.5**0.5) * size)
    bell = jnp.exp(-0.5 * x * x)
    poly = t * (
        0.5 * 0.254829592
        + t * (0.5 * -0.284496736 + t * (0.5 * 1.421413741 + t * (0.5 * -1.453152027 + t * (0.5 * 1.061405429))))
    )
    tail = poly * bell
    return jnp.where(x < 0, tail, 1.0 - tail), bell * 0.3989422804014327


def expert_kernel(steps, experts, n, *refs):
    id_ref, h0, h1, z0, z1 = refs[:5]
    weights = refs[5:8], refs[8:11]
    wr_ref, p0, p1, d0, d1 = refs[11:16]
    own_g, got_g = refs[16 : 16 + n], refs[16 + n : 16 + 2 * n]
    refs = refs[16 + 2 * n :]
    groute, hid_a, hid_b, dpre_a, dpre_b, dexp_s, *sums = refs
    i = pl.program_id(0)
    width = wr_ref.shape[0]
    slots = h0.shape[2]
    rows = h0.shape[0] * slots
    sub = min(h0.shape[0], 4)
    hidden = hid_a.shape[1]

    def parts(w):
        if n == 1:
            return w[0].at[0, :width], w[0].at[0, width : 2 * width], w[0].at[0, 2 * width :]
        return w[0].at[0, :width], w[1].at[0], w[0].at[0, width:]

    @pl.when(i == 0)
    def _():
        groute[...] = jnp.zeros_like(groute)
        for total_ref in sums:
            total_ref[...] = jnp.zeros_like(total_ref)

    def work(h_ref, z_ref, p_ref, d_ref):
        lane = lax.broadcasted_iota(jnp.int32, (1, LANES), 1)
        own = (lane == id_ref[0]).astype(F32)

        def block(m, _):
            part = pl.ds(m * sub, sub)
            at = pl.ds(pl.multiple_of(m * sub * slots, sub * slots), sub * slots)
            h = h_ref[part, 0].reshape(sub * slots, width)
            logits = jnp.where(lane < experts, dot(h, wr_ref[...]), -1e30)
            e = jnp.exp(logits - jnp.max(logits, axis=1, keepdims=True))
            probs = e / jnp.sum(e, axis=1, keepdims=True)
            gate = jnp.sum(probs * own, axis=1, keepdims=True)
            dz = z_ref[part, 0].reshape(sub * slots, width).astype(F32)
            dexp = (gate * dz).astype(BF16)
            dexp_s[at, :] = dexp
            piece = back = None
            for (win, wout, bias), hid_s, dpre_s in zip(weights, (hid_a, hid_b), (dpre_a, dpre_b)):
                pre = dot(h, win[...]) + bias[...].astype(F32)
                phi, bell = gelu_parts(pre)
                hid = (pre * phi).astype(BF16)
                hid_s[at, :] = hid
                out = dot(hid, wout[...])
                piece = out if piece is None else piece + out
                dpre = (dot_nt(dexp, wout[...]) * (phi + pre * bell)).astype(BF16)
                dpre_s[at, :] = dpre
                out = dot_nt(dpre, win[...])
                back = out if back is None else back + out
            p_ref[at, :] = piece.astype(BF16)
            dgate = jnp.sum(dz * piece, axis=1, keepdims=True)
            dlog = (dgate * probs * (own - gate)).astype(BF16)
            d_ref[at, :] = (back + dot_nt(dlog, wr_ref[...])).astype(BF16)
            groute[...] += dot_tn(h, dlog)
            return 0

        lax.fori_loop(0, h_ref.shape[0] // sub, block, 0)
        for k, (dpre_s, hid_s) in enumerate(((dpre_a, hid_a), (dpre_b, hid_b))):
            to_win, to_bias, to_wout = sums[3 * k : 3 * k + 3]
            dpre = dpre_s[...]
            to_win[...] += dot_tn(h_ref[...].reshape(rows, width), dpre)
            to_bias[...] += jnp.broadcast_to(jnp.sum(dpre.astype(F32), axis=0, keepdims=True), to_bias.shape)
            to_wout[...] += dot_tn(hid_s[...], dexp_s[...])

    @pl.when(i < steps)
    def _():
        work(h0, z0, p0, d0)

    @pl.when(i >= steps)
    def _():
        work(h1, z1, p1, d1)

    @pl.when(i == 2 * steps - 1)
    def _():
        for k, g in enumerate((own_g, got_g)):
            win, wout, bias = parts(g)
            win[...] = sums[3 * k][...].astype(BF16)
            bias[...] = sums[3 * k + 1][...].astype(BF16)
            wout[...] = sums[3 * k + 2][...].astype(BF16)


def expert(expert_id, own_h, other_h, own_z, other_z, places, own_w, got_w, at, w_route, experts):
    sources, _, slots, width = own_h.shape
    rows = sources * slots
    hidden = own_w[0].shape[2]
    group = min(sources, 8)
    block, steps = group * slots, sources // group
    early = lambda i: jnp.minimum(i, steps - 1)
    late = lambda i: jnp.maximum(i - steps, 0)
    once = lambda shape: pl.BlockSpec(shape, lambda i: (0,) * len(shape))
    rows_spec = lambda place, when: pl.BlockSpec((group, 1, slots, width), lambda i: (when(i), place, 0, 0))
    weight = lambda w, k: pl.BlockSpec((None, *w.shape[1:]), lambda i: (k, 0, 0))
    out_first = pl.BlockSpec((block, width), lambda i: (early(i), 0))
    out_second = pl.BlockSpec((block, width), lambda i: (late(i), 0))
    shape = jax.ShapeDtypeStruct
    if hidden == width:
        grads = [shape((1, 2 * width + 16, hidden), BF16)]
    else:
        grads = [shape((1, width + 16, hidden), BF16), shape((1, hidden, width), BF16)]
    outs = [shape((rows, width), BF16)] * 4 + grads * 2 + [shape((width, LANES), F32)]
    spots = (own_h, other_h, own_z, other_z)
    return pl.pallas_call(
        functools.partial(expert_kernel, steps, experts, len(grads)),
        grid=(2 * steps,),
        in_specs=[pl.BlockSpec(memory_space=pltpu.SMEM)]
        + [rows_spec(p, w) for p, w in zip(places, (early, late, early, late))]
        + [weight(w, k) for w, k in zip((*own_w, *got_w), at)]
        + [once(w_route.shape)],
        out_specs=[out_first, out_second, out_first, out_second] + [once(o.shape) for o in outs[4:]],
        out_shape=outs,
        scratch_shapes=[
            *[pltpu.VMEM((block, hidden), BF16)] * 4,
            pltpu.VMEM((block, width), BF16),
            *[pltpu.VMEM(s, F32) for s in ((width, hidden), (16, hidden), (hidden, width))] * 2,
        ],
        compiler_params=pltpu.CompilerParams(vmem_limit_bytes=VMEM),
        cost_estimate=pl.CostEstimate(
            flops=48 * rows * hidden * width, bytes_accessed=20 * width * hidden, transcendentals=4 * rows * hidden
        ),
        name="expert",
    )(expert_id, *spots, *own_w, *got_w, w_route)


def finish_kernel(n, *refs):
    parts, (win, wout, bias) = refs[: 6 * n], refs[-3:]
    for l in range(n):
        for k, out in enumerate((win, wout, bias)):
            out[l] = parts[6 * l + k][...].astype(F32) + parts[6 * l + 3 + k][...].astype(F32)


def finish(own, got):
    n, (_, height, hidden) = len(own), own[0].shape
    width = (height - 16) // 2
    tile = 128
    steps = width // tile
    spec = lambda r, k: pl.BlockSpec((None, r, hidden), lambda i: (0, k(i), 0))
    three = [spec(tile, lambda i: i), spec(tile, lambda i: steps + i), spec(16, lambda i: 2 * width // 16)]
    flat = [x for pair in zip(own, got) for a in pair for x in (a, a, a)]
    big = pl.BlockSpec((n, tile, hidden), lambda i: (0, i, 0))
    shape = jax.ShapeDtypeStruct
    return pl.pallas_call(
        functools.partial(finish_kernel, n),
        grid=(steps,),
        in_specs=three * (2 * n),
        out_specs=[big, big, pl.BlockSpec((n, 16, hidden), lambda i: (0, 0, 0))],
        out_shape=[shape((n, width, hidden), F32), shape((n, width, hidden), F32), shape((n, 16, hidden), F32)],
        compiler_params=pltpu.CompilerParams(vmem_limit_bytes=VMEM),
        cost_estimate=pl.CostEstimate(
            flops=2 * n * height * hidden, bytes_accessed=8 * n * height * hidden, transcendentals=0
        ),
        name="finish",
    )(*flat)


def to_send_kernel(in_ref, out_ref, *refs):
    for l in range(in_ref.shape[0]):
        refs[2 * l][0] = in_ref[l]
        refs[2 * l + 1][0] = out_ref[l]


def to_send(w_in, w_out):
    groups = w_in.shape[0]
    steps = w_in.shape[1] // 128
    spec = lambda a, k: pl.BlockSpec((k, a.shape[1] // steps, a.shape[2]), lambda i: (0, i, 0))
    flat = pl.pallas_call(
        to_send_kernel,
        grid=(steps,),
        in_specs=[spec(w_in, groups), spec(w_out, groups)],
        out_specs=[spec(w_in, 1), spec(w_out, 1)] * groups,
        out_shape=[jax.ShapeDtypeStruct((1, *a.shape[1:]), BF16) for a in (w_in, w_out)] * groups,
        compiler_params=pltpu.CompilerParams(vmem_limit_bytes=VMEM),
        name="to_send",
    )(w_in, w_out)
    return [flat[2 * l : 2 * l + 2] for l in range(groups)]


def turn_kernel(x_ref, y_ref, x_out, y_out):
    x_out[...] = x_ref[...].T
    y_out[...] = y_ref[...].T


def turn(x, y):
    whole = lambda a, b: pl.BlockSpec((a, b), lambda i: (0, 0))
    tokens, width = x.shape
    return pl.pallas_call(
        turn_kernel,
        grid=(1,),
        in_specs=[whole(tokens, width)] * 2,
        out_specs=[whole(width, tokens)] * 2,
        out_shape=[jax.ShapeDtypeStruct((width, tokens), x.dtype)] * 2,
        compiler_params=pltpu.CompilerParams(vmem_limit_bytes=VMEM),
        name="turn",
    )(x, y)


def outer_kernel(h_ref, a_ref, g_ref, b_ref, rest_ref, sums_ref, out_ref):
    width = b_ref.shape[1]
    for k in range(3):
        out_ref[:, k * width : (k + 1) * width] = dot(h_ref[...], g_ref[k]).astype(BF16)
    out_ref[:, 3 * width : 4 * width] = dot(a_ref[...], b_ref[...]).astype(BF16)
    out_ref[:, 4 * width : 4 * width + LANES] = rest_ref[...]
    out_ref[:, 4 * width + LANES :] = sums_ref[...].T.astype(BF16)


def outer(h, a, g, b, rest, sums):
    width, tokens = h.shape
    tile = 256
    whole = lambda *shape: pl.BlockSpec(shape, lambda i: (0,) * len(shape))
    rows = lambda n: pl.BlockSpec((tile, n), lambda i: (i, 0))
    columns = 4 * width + 2 * LANES
    return pl.pallas_call(
        outer_kernel,
        grid=(width // tile,),
        in_specs=[
            rows(tokens), rows(tokens), whole(3, tokens, width), whole(tokens, width), rows(LANES),
            pl.BlockSpec((LANES, tile), lambda i: (0, i)),
        ],
        out_specs=rows(columns),
        out_shape=jax.ShapeDtypeStruct((width, columns), BF16),
        compiler_params=pltpu.CompilerParams(vmem_limit_bytes=VMEM),
        cost_estimate=COST,
        name="outer",
    )(h, a, g, b, rest, sums)


def input_kernel(g_ref, w_ref, x_ref, dy_ref, gain_ref, out_ref, sums_ref):
    width = x_ref.shape[1]

    @pl.when(pl.program_id(0) == 0)
    def _():
        sums_ref[...] = jnp.zeros_like(sums_ref)

    grad = dot_nt(g_ref[0], w_ref[:, :width])
    for k in (1, 2):
        grad += dot_nt(g_ref[k], w_ref[:, k * width : (k + 1) * width])
    unit, rstd = normed(x_ref[...].astype(F32))
    out_ref[...] = dy_ref[...] + norm_back(grad, gain_ref[...], unit, rstd)
    add = lambda t: jnp.sum(t, axis=0, keepdims=True)
    sums_ref[0:1, :] += add(grad * unit)
    sums_ref[1:2, :] += add(grad)
    sums_ref[2:3, :] += add(g_ref[0].astype(F32))
    sums_ref[3:4, :] += add(g_ref[2].astype(F32))


def input_back(g, wide, tokens, dy, gain):
    count, width = tokens.shape
    tile = 256
    rows = pl.BlockSpec((tile, width), lambda i: (i, 0))
    whole = lambda *shape: pl.BlockSpec(shape, lambda i: (0,) * len(shape))
    return pl.pallas_call(
        input_kernel,
        grid=(count // tile,),
        in_specs=[
            pl.BlockSpec((3, tile, width), lambda i: (0, i, 0)), whole(*wide.shape), rows, rows, whole(1, width),
        ],
        out_specs=[rows, whole(LANES, width)],
        out_shape=[jax.ShapeDtypeStruct((count, width), F32), jax.ShapeDtypeStruct((LANES, width), F32)],
        compiler_params=pltpu.CompilerParams(vmem_limit_bytes=VMEM),
        cost_estimate=COST,
        name="input_back",
    )(g, wide, tokens, dy, gain)


def normed(x):
    centred = x - jnp.mean(x, axis=-1, keepdims=True)
    rstd = lax.rsqrt(jnp.mean(centred * centred, axis=-1, keepdims=True) + EPSILON)
    return centred * rstd, rstd


def norm_back(grad, gain, unit, rstd):
    g = grad * gain
    mean = lambda t: jnp.mean(t, axis=-1, keepdims=True)
    return rstd * (g - mean(g) - unit * mean(g * unit))


def pad_columns(x, count):
    return jnp.pad(x, ((0, 0), (0, count - x.shape[1])))


def up(count):
    return -(-count // LANES) * LANES


def local(
    tokens, cotangent, segment_ids, routes, capacity, ln1_gain, ln1_bias, w_query, b_query, w_key, w_value,
    b_value, w_output, b_output, ln2_gain, ln2_bias, w_router, w_in, b_in, w_out, b_out,
):
    row_count, width = tokens.shape
    experts = capacity.shape[0]
    slots = 2 * row_count // experts
    groups = w_in.shape[0]
    owners = lax.axis_size("expert")
    split = groups * owners // experts
    share = w_query.shape[0]
    devices = lax.axis_size("batch") * owners
    me = lax.axis_index("expert")
    chunk = min(2, groups)
    layout = (groups, chunk, split, slots)
    firsts = tuple(range(0, groups, chunk))
    pair = lambda first: range(first, first + chunk)
    heavy = lambda l: 1 if l % 2 == 0 else 2
    light = lambda l: 3 - heavy(l)

    spread = -(-experts // share)
    fold = lambda x: jnp.pad(x, (0, spread * share - experts)).reshape(spread, share).T
    unfold = lambda x: x.T.reshape(-1)[:experts]

    chosen = routes[:, 0]
    picked = chosen[:, None] == jnp.arange(experts, dtype=jnp.int32)[None, :]
    picked_float = picked.astype(F32)
    position = jnp.arange(row_count, dtype=jnp.int32)
    earlier = (position[None, :] < position[:, None]).astype(BF16)
    rank = dot(earlier, picked.astype(BF16))
    slot = jnp.sum(rank * picked_float, axis=1)
    limit = jnp.sum(capacity.astype(F32)[None, :] * picked_float, axis=1)
    kept = slot < limit
    kept_float = kept.astype(F32)
    ids = jnp.where(kept, chosen * slots + slot.astype(jnp.int32), -1)
    id_row, id_col = ids[None, :], ids[:, None]
    counts = jnp.sum(picked_float, axis=0)

    def send(x, first, count):
        rows = dispatch(id_row, x, count * owners * slots, (groups, count, split, slots), first)
        return rows.reshape(owners, count, slots, width)

    grad_send = send(cotangent, 0, groups)

    small = jnp.stack([ln1_gain, ln1_bias, b_query, b_value, b_output, ln2_gain, ln2_bias], axis=1)
    tally = fold(counts).astype(BF16)
    extra = pad_columns(jnp.concatenate([small, tally], axis=1), up(7 + spread))
    wide = jnp.concatenate([w_query, w_key, w_value, extra], axis=1)
    rest = jnp.concatenate([w_router, b_out.T], axis=1)
    rest = jnp.concatenate([w_output, pad_columns(rest, up(2 * experts))], axis=1)
    if staged():
        wide, rest = gather_first(wide), gather_first(rest)
        rest_first = rest
        sent_w = to_send(*after((w_in, w_out), grad_send))
        free = gather_second(wide, (grad_send, sent_w))
        wide = gather_third(free)
        rest = after(rest, free)
    else:
        wide = lax.all_gather(wide, ALL, axis=0, tiled=True)
        rest = lax.all_gather(rest, ALL, axis=0, tiled=True)
        free = rest_first = ()
        sent_w = to_send(w_in, w_out)

    bias_rows = b_in[:, None, :]
    got_bias = [swap(after(bias_rows, free), "batch", mask) for mask in (1, 2)]
    got_w, last = [], free
    for l in range(groups):
        if l % chunk == 0:
            last = got_w[-chunk:] or free
        got_w.append([swap(w, "batch", heavy(l)) for w in after(sent_w[l], last)])

    own_z = to_owners(after(grad_send, rest_first))
    theirs = lambda rows, l, at: swap(rows[:, at : at + 1], "batch", light(l))
    other_z = [theirs(own_z, l, l) for l in range(groups)]

    vectors = wide[:, 3 * width : 3 * width + 7].astype(F32).T
    gain_one, shift_one, bias_query, bias_value, bias_output, gain_two, shift_two = vectors
    tallies = wide[:, 3 * width + 7 : 3 * width + 7 + spread].astype(F32).reshape(devices, share, spread)
    all_counts = unfold(jnp.sum(tallies, axis=0))
    token_total = float(row_count * devices)
    fraction = all_counts / token_total

    inputs = tokens.astype(F32)
    unit_one, rstd_one = normed(inputs)
    h_one = (unit_one * gain_one + shift_one).astype(BF16)
    nothing = jnp.zeros((width,), F32)
    bias = jnp.concatenate([bias_query, nothing, bias_value, jnp.zeros((wide.shape[1] - 3 * width,), F32)])
    qkv = (dot(h_one, wide) + bias).astype(BF16)
    if staged():
        rest = gather_second(rest, qkv)
    seg_row = segment_ids.reshape(1, row_count)
    seg_col = segment_ids.reshape(row_count, 1)
    attended, logs = attend(qkv, seg_row, seg_col, width)
    attended = after(attended, [w[0] for w in got_w[:chunk]])
    if staged():
        rest = gather_third(rest, attended)
    full_output = rest[:, :width]
    full_router = pad_columns(rest[:, width : width + experts], LANES)
    bias_expert = rest[:, width + experts : width + 2 * experts].T
    resid = inputs + dot(attended, full_output) + bias_output
    unit_two, rstd_two = normed(resid)
    h_two = (unit_two * gain_two + shift_two).astype(BF16)
    h_two = after(h_two, own_z, [w[1] for w in got_w[:chunk]])

    rows = [send(h_two, first, chunk) for first in firsts]
    token_rows = []
    for at in range(len(firsts)):
        if at:
            rows[at] = after(rows[at], token_rows[-1], [w[0] for w in got_w[chunk:]])
        token_rows.append(to_owners(rows[at]))
    token_rows = [after(t, rows) for t in token_rows]
    their_h = [token_rows[l // chunk][:, l % chunk : l % chunk + 1] for l in range(groups)]
    their_h = [lax.optimization_barrier(their_h[first : first + chunk]) for first in firsts]
    other_h = [swap(their_h[l // chunk][l % chunk], "batch", light(l)) for l in range(groups)]
    h_turned, att_turned = turn(h_one, attended)

    router_probs = jax.nn.softmax(dot(h_two, full_router)[:, :experts], axis=-1)
    mixing = kept_float * jnp.sum(router_probs * picked_float, axis=1)
    grad_out = cotangent.astype(F32)
    expert_bias = dot(picked.astype(BF16), bias_expert)
    gate_bias = kept_float * jnp.sum(grad_out * expert_bias, axis=1)
    grad_probs = picked_float * gate_bias[:, None] + BALANCE * experts * fraction[None, :] / token_total
    grad_logits = router_probs * (grad_probs - jnp.sum(grad_probs * router_probs, axis=1, keepdims=True))
    grad_logits = grad_logits.astype(BF16)
    mixed = picked_float * mixing[:, None]
    mixed_high = mixed.astype(BF16)
    mixed_low = (mixed - mixed_high.astype(F32)).astype(BF16)
    grad_bias_expert = dot_tn(cotangent, mixed_high) + dot_tn(cotangent, mixed_low)
    home_router = dot_tn(h_two, grad_logits)
    home_h_two = dot_nt(grad_logits, full_router[:, :experts])
    home_h_two, home_router, grad_bias_expert, probs_sum = lax.optimization_barrier(
        (home_h_two, home_router, grad_bias_expert, jnp.sum(router_probs, axis=0))
    )
    made, returned, piece_sums, got_g = [], [], [], []
    for at, first in enumerate(firsts):
        for l in pair(first):
            number = ((me * groups + l) // split).astype(jnp.int32).reshape(1)
            if l == 0:
                number = after(number, h_turned, home_h_two)
            if l == 1:
                number = after(number, made[-1], got_w[-chunk:], their_h)
            made.append(
                expert(
                    number, token_rows[at], other_h[l], own_z, other_z[l], (l - first, 0, l, 0),
                    (w_in, w_out, bias_rows), (*got_w[l], got_bias[heavy(l) - 1]), (l, l, l, 0, 0, l),
                    full_router, experts,
                )
            )
        sums = [(made[l][2], swap(after(made[l][3], other_h), "batch", light(l))) for l in pair(first)]
        rows = merge(sums, owners, slots)
        if returned:
            rows = after(rows, returned[-1], got_g)
        returned.append(to_owners(rows).reshape(-1, width))
        n = (len(made[0]) - 5) // 2
        if first + chunk == groups:
            piece_sums = [(m[0], swap(after(m[1], sums), "batch", light(l))) for l, m in enumerate(made)]
        for l in pair(first):
            grads = after(made[l][4 + n : 4 + 2 * n], sums, other_h, piece_sums)
            got_g.append([swap(g, "batch", heavy(l)) for g in grads])
    own_g = [m[4 : 4 + n] for m in made]

    grad_router = home_router + sum(m[-1] for m in made)[:, :experts]

    grad_h_two = home_h_two + combine(after(id_col, piece_sums), returned, layout, firsts)
    grad_resid = grad_out + norm_back(grad_h_two, gain_two, unit_two, rstd_two)
    grad_branch = grad_resid.astype(BF16)
    grad_att = dot_nt(grad_branch, full_output).astype(BF16)
    columns = lambda *rows: jnp.stack(rows, axis=1)
    prob_sums = jnp.tile(fold(probs_sum), (devices, 1))
    sums = columns(
        jnp.sum(grad_h_two * unit_two, axis=0), jnp.sum(grad_h_two, axis=0), jnp.sum(grad_branch.astype(F32), axis=0)
    )
    packed = jnp.concatenate([grad_router, grad_bias_expert, sums, prob_sums], axis=1)
    packed = pad_columns(packed, LANES).astype(BF16)
    merged = merge(after(piece_sums, grad_att, packed), owners, slots)
    pieces = to_owners(merged).reshape(-1, width)
    grad_att = after(grad_att, merged, packed)
    dqkv = attend_back(qkv, grad_att, logs, seg_row, seg_col, width)

    dqkv, got_g = after((dqkv, got_g), got_g)
    input_grad, sums = input_back(dqkv, wide, tokens, grad_resid, gain_one[None])
    def close(waiting):
        own, got, _ = waiting
        if n == 1:
            win, wout, bias = finish([g[0] for g in own], [g[0] for g in got])
            return win, bias[:, 0], wout
        both = [[a[0].astype(F32) + b[0].astype(F32) for a, b in zip(*pair_g)] for pair_g in zip(own, got)]
        return (
            jnp.stack([g[0][:width] for g in both]),
            jnp.stack([g[0][width] for g in both]),
            jnp.stack([g[1] for g in both]),
        )

    wide_sum, (grad_w_in, grad_b_in, grad_w_out) = scatter_rows(
        outer(h_turned, att_turned, dqkv, grad_branch, packed, sums), (own_g, got_g, pieces), close
    )
    pieces = after(pieces, grad_b_in)
    fetched = combine(id_col, [pieces], (groups, groups, split, slots), (0,))
    block_out = (resid + mixing[:, None] * (fetched + expert_bias)).astype(BF16)
    router_sum = wide_sum[:, 4 * width : 4 * width + 2 * experts]
    side = wide_sum[:, 4 * width + 2 * experts :]
    late_side = wide_sum[:, 4 * width + LANES :]
    mean_probs = unfold(side[:, 3 : 3 + spread]) / token_total
    balance_loss = experts * jnp.sum(fraction * mean_probs)
    expert_shares = jnp.stack([experts * fraction, experts * mean_probs])

    return (
        block_out,
        balance_loss,
        expert_shares,
        input_grad,
        late_side[:, 0],
        late_side[:, 1],
        wide_sum[:, :width],
        late_side[:, 2],
        wide_sum[:, width : 2 * width],
        wide_sum[:, 2 * width : 3 * width],
        late_side[:, 3],
        wide_sum[:, 3 * width : 4 * width],
        side[:, 2],
        side[:, 0],
        side[:, 1],
        router_sum[:, :experts],
        grad_w_in,
        grad_b_in,
        grad_w_out,
        router_sum[:, experts:].T,
    )


def solution(mesh):
    rows, split = P(ALL, None), P(ALL)
    experts = (P("expert", None, "batch"), P("expert", "batch"), P("expert", "batch", None), P(None, ALL))
    return jax.shard_map(
        local,
        mesh=mesh,
        in_specs=(
            rows, rows, rows, rows, P(), split, split, rows, split, rows, rows, split, rows, split, split, split,
            rows, *experts,
        ),
        out_specs=(
            rows, P(), P(), rows, split, split, rows, split, rows, rows, split, rows, split, split, split, rows,
            *experts,
        ),
        check_vma=False,
    )
```

```python
import functools

import jax
import jax.numpy as jnp
from jax import lax
from jax.experimental import pallas as pl
from jax.experimental.pallas import tpu as pltpu
from jax.sharding import PartitionSpec as P

HEAD = 64
LANES = 128
REACH = 384
QROWS = 256
EPSILON = 1e-05
BALANCE = 0.01
ALL = ("batch", "expert")
VMEM = 60 * 1024 * 1024
COST = pl.CostEstimate(flops=1, bytes_accessed=1, transcendentals=0)
F32 = jnp.float32
BF16 = jnp.bfloat16


def dot(a, b):
    return jnp.dot(a, b, preferred_element_type=F32)


def dot_nt(a, b):
    return lax.dot_general(a, b, (((1,), (1,)), ((), ())), preferred_element_type=F32)


def dot_tn(a, b):
    return lax.dot_general(a, b, (((0,), (0,)), ((), ())), preferred_element_type=F32)


def swap(x, axis, mask):
    return lax.ppermute(x, axis, [(i, i ^ mask) for i in range(lax.axis_size(axis))])


def shift(x, step):
    size = lax.axis_size("expert")
    return lax.ppermute(x, "expert", [(i, (i + step) % size) for i in range(size)])


def staged():
    return lax.axis_size("batch") == 4 and lax.axis_size("expert") == 8


def gather_first(x):
    mz = lax.axis_index("expert") // 2
    ring = [shift(x, 2 * k) for k in (3, 2, 1)] + [x]
    ring = jnp.stack(ring + ring[:3])
    return lax.dynamic_slice_in_dim(ring, 3 - mz, 4, 0)


def gather_second(zs, beside):
    mb = lax.axis_index("batch")
    b = after([zs] + [swap(zs, "batch", k) for k in (1, 2, 3)], beside)
    odd, high = (mb & 1) == 1, (mb & 2) == 2
    u = [jnp.where(odd, b[i ^ 1], b[i]) for i in range(4)]
    return jnp.stack([jnp.where(high, u[i ^ 2], u[i]) for i in range(4)])


def gather_third(rows, beside=()):
    mc = lax.axis_index("expert") % 2
    other = after(swap(rows, "expert", 1), beside)
    both = jnp.stack(
        [jnp.where(mc == 0, rows, other), jnp.where(mc == 0, other, rows)], axis=2
    )
    return both.reshape(-1, rows.shape[-1])


def scatter_rows(g, before, beside):
    if not staged():
        return lax.psum_scatter(g, ALL, scatter_dimension=0, tiled=True).astype(F32), beside(before)
    mb, me = lax.axis_index("batch"), lax.axis_index("expert")
    mz, mc = me // 2, me % 2
    r, c = g.shape[0] // 32, g.shape[1]
    g = g.reshape(4, 4, 2, r, c)
    mine = jnp.where(mc == 0, g[:, :, 0], g[:, :, 1])
    other = swap(jnp.where(mc == 0, g[:, :, 1], g[:, :, 0]), "expert", 1)
    s = (mine.astype(F32) + other.astype(F32)).astype(BF16)
    made = beside(after(before, s))
    pick = lambda t, i: lax.dynamic_index_in_dim(t, i, 0, keepdims=False)
    parts = after([swap(pick(s, mb ^ k), "batch", k) for k in (1, 2, 3)], made, before)
    t = sum((p.astype(F32) for p in parts), pick(s, mb).astype(F32)).astype(BF16)
    parts = [shift(pick(t, (mz + k) % 4), 2 * k) for k in (1, 2, 3)]
    return sum((p.astype(F32) for p in parts), pick(t, mz).astype(F32)), made


def to_owners(x):
    return lax.all_to_all(x, "expert", split_axis=0, concat_axis=0, tiled=True)


def after(x, *others):
    return lax.optimization_barrier((x, others))[0]


def windows(length):
    for start in range(0, length, QROWS):
        yield start, max(0, start - REACH), start + QROWS


def half_masks():
    lane = lax.broadcasted_iota(jnp.int32, (1, LANES), 1)
    first = (lane < HEAD).astype(F32)
    return first, (first.astype(BF16), (1.0 - first).astype(BF16))


def attend_kernel(q_ref, k_ref, v_ref, row_ref, col_ref, out_ref, log_ref, mask_ref):
    length = q_ref.shape[0]

    @pl.when(pl.program_id(0) == 0)
    def _():
        for n, (start, low, stop) in enumerate(windows(length)):
            shape = (QROWS, stop - low)
            i = lax.broadcasted_iota(jnp.int32, shape, 0) + start
            j = lax.broadcasted_iota(jnp.int32, shape, 1) + low
            same = col_ref[start:stop, :] == row_ref[:, low:stop]
            mask_ref[n, :, : stop - low] = jnp.where((j <= i) & same, 0.0, -1e30)

    first, halves = half_masks()
    for n, (start, low, stop) in enumerate(windows(length)):
        q = q_ref[start:stop, :] * jnp.asarray(HEAD**-0.5, BF16)
        both = jnp.concatenate([q * half for half in halves])
        mask = mask_ref[n, :, : stop - low]
        s = dot_nt(both, k_ref[low:stop, :]) + jnp.concatenate([mask, mask])
        top = jnp.max(s, axis=1, keepdims=True)
        e = jnp.exp(s - top)
        sums = jnp.sum(e, axis=1, keepdims=True)
        out = dot(e.astype(BF16), v_ref[low:stop, :]) / sums
        logs = top + jnp.log(sums)
        out_ref[start:stop, :] = (out[:QROWS] * first + out[QROWS:] * (1.0 - first)).astype(BF16)
        log_ref[start:stop, :] = logs[:QROWS] * first + logs[QROWS:] * (1.0 - first)


def attend(qkv, seg_row, seg_col, width):
    length = qkv.shape[0]
    pairs = width // LANES
    spec = lambda offset: pl.BlockSpec((length, LANES), lambda p, o=offset: (0, o + p))
    whole = lambda shape: pl.BlockSpec(shape, lambda p: (0,) * len(shape))
    return pl.pallas_call(
        attend_kernel,
        grid=(pairs,),
        in_specs=[spec(0), spec(pairs), spec(2 * pairs), whole((1, length)), whole((length, 1))],
        out_specs=[spec(0), spec(0)],
        out_shape=[
            jax.ShapeDtypeStruct((length, width), BF16),
            jax.ShapeDtypeStruct((length, width), F32),
        ],
        scratch_shapes=[pltpu.VMEM((length // QROWS, QROWS, QROWS + REACH), F32)],
        compiler_params=pltpu.CompilerParams(vmem_limit_bytes=VMEM),
        cost_estimate=COST,
        name="attend",
    )(qkv, qkv, qkv, seg_row, seg_col)


def attend_back_kernel(
    q_ref, k_ref, v_ref, g_ref, log_ref, row_ref, col_ref, out_ref, mask_ref, dk_ref, dv_ref
):
    length = q_ref.shape[0]

    @pl.when(pl.program_id(0) == 0)
    def _():
        for n, (start, low, stop) in enumerate(windows(length)):
            shape = (stop - low, QROWS)
            j = lax.broadcasted_iota(jnp.int32, shape, 0) + low
            i = lax.broadcasted_iota(jnp.int32, shape, 1) + start
            same = col_ref[low:stop, :] == row_ref[:, start:stop]
            mask_ref[n, : stop - low, :] = jnp.where((j <= i) & same, 0.0, -1e30)

    dk_ref[...] = jnp.zeros_like(dk_ref)
    dv_ref[...] = jnp.zeros_like(dv_ref)
    first, halves = half_masks()
    scale = HEAD**-0.5
    for n, (start, low, stop) in enumerate(windows(length)):
        q = q_ref[start:stop, :] * jnp.asarray(scale, BF16)
        g = g_ref[start:stop, :]
        k, v = k_ref[low:stop, :], v_ref[low:stop, :]
        turned = log_ref[start:stop, :].T
        logs = jnp.concatenate([turned[:1, :], turned[HEAD : HEAD + 1, :]], axis=1)
        qs = jnp.concatenate([q * half for half in halves])
        gs = jnp.concatenate([g * half for half in halves])
        mask = mask_ref[n, : stop - low, :]
        p = jnp.exp(dot_nt(k, qs) + jnp.concatenate([mask, mask], axis=1) - logs)
        dp = dot_nt(v, gs)
        centre = jnp.sum(dp * p, axis=0, keepdims=True)
        ds = (p * (dp - centre)).astype(BF16)
        dv_ref[low:stop, :] += dot(p.astype(BF16), gs)
        dk_ref[low:stop, :] += dot(ds, qs)
        dqs = dot_tn(ds, k)
        dq = dqs[:QROWS] * first + dqs[QROWS:] * (1.0 - first)
        out_ref[0, start:stop, :] = (dq * scale).astype(BF16)
    out_ref[1] = dk_ref[...].astype(BF16)
    out_ref[2] = dv_ref[...].astype(BF16)


def attend_back(qkv, grad, logs, seg_row, seg_col, width):
    length = qkv.shape[0]
    pairs = width // LANES
    spec = lambda offset: pl.BlockSpec((length, LANES), lambda p, o=offset: (0, o + p))
    whole = lambda shape: pl.BlockSpec(shape, lambda p: (0,) * len(shape))
    return pl.pallas_call(
        attend_back_kernel,
        grid=(pairs,),
        in_specs=[spec(0), spec(pairs), spec(2 * pairs), spec(0), spec(0), whole((1, length)), whole((length, 1))],
        out_specs=pl.BlockSpec((3, length, LANES), lambda p: (0, 0, p)),
        out_shape=jax.ShapeDtypeStruct((3, length, width), BF16),
        scratch_shapes=[
            pltpu.VMEM((length // QROWS, QROWS + REACH, QROWS), F32),
            pltpu.VMEM((length, LANES), F32),
            pltpu.VMEM((length, LANES), F32),
        ],
        compiler_params=pltpu.CompilerParams(vmem_limit_bytes=VMEM),
        cost_estimate=COST,
        name="attend_back",
    )(qkv, qkv, qkv, grad, logs, seg_row, seg_col)


def slot_ids(shape, axis, base, layout, first):
    groups, chunk, split, slots = layout
    at = lax.broadcasted_iota(jnp.int32, shape, axis) + base
    row, slot = at // slots, at % slots
    return (row // chunk * groups + first + row % chunk) // split * slots + slot


def dispatch_kernel(layout, first, id_ref, x_ref, out_ref):
    rows, tokens = out_ref.shape[0], x_ref.shape[0]
    ids = slot_ids((rows, 1), 0, pl.program_id(0) * rows, layout, first)
    chosen = jnp.where(ids == id_ref[...], 1.0, 0.0).astype(BF16)
    out_ref[...] = dot(chosen, x_ref[...]).astype(BF16)


def dispatch(ids, x, count, layout, first):
    tokens, width = x.shape
    block = min(count, 512)
    return pl.pallas_call(
        functools.partial(dispatch_kernel, layout, first),
        grid=(count // block,),
        in_specs=[
            pl.BlockSpec((1, tokens), lambda i: (0, 0)),
            pl.BlockSpec((tokens, width), lambda i: (0, 0)),
        ],
        out_specs=pl.BlockSpec((block, width), lambda i: (i, 0)),
        out_shape=jax.ShapeDtypeStruct((count, width), BF16),
        compiler_params=pltpu.CompilerParams(vmem_limit_bytes=VMEM),
        cost_estimate=pl.CostEstimate(
            flops=2 * count * tokens * width, bytes_accessed=4 * count * width, transcendentals=0
        ),
        name="dispatch",
    )(ids, x)


def combine_kernel(layout, firsts, id_ref, *refs):
    *x_refs, out_ref = refs
    out_ref[...] = jnp.zeros_like(out_ref)
    for first, x_ref in zip(firsts, x_refs):
        step = min(x_ref.shape[0], 512)
        for base in range(0, x_ref.shape[0], step):
            ids = slot_ids((1, step), 1, base, layout, first)
            chosen = jnp.where(id_ref[...] == ids, 1.0, 0.0).astype(BF16)
            out_ref[...] += dot(chosen, x_ref[base : base + step, :])


def combine(ids, xs, layout, firsts):
    tokens, (count, width), block = ids.shape[0], xs[0].shape, 256
    return pl.pallas_call(
        functools.partial(combine_kernel, layout, firsts),
        grid=(tokens // block,),
        in_specs=[pl.BlockSpec((block, 1), lambda i: (i, 0))]
        + [pl.BlockSpec((count, width), lambda i: (0, 0)) for _ in xs],
        out_specs=pl.BlockSpec((block, width), lambda i: (i, 0)),
        out_shape=jax.ShapeDtypeStruct((tokens, width), F32),
        compiler_params=pltpu.CompilerParams(vmem_limit_bytes=VMEM),
        cost_estimate=pl.CostEstimate(
            flops=2 * count * len(xs) * tokens * width,
            bytes_accessed=2 * count * len(xs) * width + 4 * tokens * width,
            transcendentals=0,
        ),
        name="combine",
    )(ids, *xs)


def merge_kernel(*refs):
    *parts, out_ref = refs
    owners, chunk, slots, width = out_ref.shape
    for l in range(chunk):
        both = parts[2 * l][...].astype(F32) + parts[2 * l + 1][...].astype(F32)
        out_ref[:, l] = both.astype(BF16).reshape(owners, slots, width)


def merge(pairs, owners, slots):
    rows, width = pairs[0][0].shape
    block = min(owners, 4)
    flat = [part for pair in pairs for part in pair]
    return pl.pallas_call(
        merge_kernel,
        grid=(owners // block,),
        in_specs=[pl.BlockSpec((block * slots, width), lambda i: (i, 0)) for _ in flat],
        out_specs=pl.BlockSpec((block, len(pairs), slots, width), lambda i: (i, 0, 0, 0)),
        out_shape=jax.ShapeDtypeStruct((owners, len(pairs), slots, width), BF16),
        compiler_params=pltpu.CompilerParams(vmem_limit_bytes=VMEM),
        cost_estimate=pl.CostEstimate(
            flops=len(flat) * rows * width, bytes_accessed=3 * len(flat) * rows * width, transcendentals=0
        ),
        name="merge",
    )(*flat)


def gelu_parts(x):
    size = jnp.abs(x)
    t = 1.0 / (1.0 + (0.3275911 * 0.5**0.5) * size)
    bell = jnp.exp(-0.5 * x * x)
    poly = t * (
        0.5 * 0.254829592
        + t * (0.5 * -0.284496736 + t * (0.5 * 1.421413741 + t * (0.5 * -1.453152027 + t * (0.5 * 1.061405429))))
    )
    tail = poly * bell
    return jnp.where(x < 0, tail, 1.0 - tail), bell * 0.3989422804014327


def expert_kernel(steps, experts, n, *refs):
    id_ref, h0, h1, z0, z1 = refs[:5]
    weights = refs[5:8], refs[8:11]
    wr_ref, p0, p1, d0, d1 = refs[11:16]
    own_g, got_g = refs[16 : 16 + n], refs[16 + n : 16 + 2 * n]
    refs = refs[16 + 2 * n :]
    groute, hid_a, hid_b, dpre_a, dpre_b, dexp_s, *sums = refs
    i = pl.program_id(0)
    width = wr_ref.shape[0]
    slots = h0.shape[2]
    rows = h0.shape[0] * slots
    sub = min(h0.shape[0], 4)
    hidden = hid_a.shape[1]

    def parts(w):
        if n == 1:
            return w[0].at[0, :width], w[0].at[0, width : 2 * width], w[0].at[0, 2 * width :]
        return w[0].at[0, :width], w[1].at[0], w[0].at[0, width:]

    @pl.when(i == 0)
    def _():
        groute[...] = jnp.zeros_like(groute)
        for total_ref in sums:
            total_ref[...] = jnp.zeros_like(total_ref)

    def work(h_ref, z_ref, p_ref, d_ref):
        lane = lax.broadcasted_iota(jnp.int32, (1, LANES), 1)
        own = (lane == id_ref[0]).astype(F32)

        def block(m, _):
            part = pl.ds(m * sub, sub)
            at = pl.ds(pl.multiple_of(m * sub * slots, sub * slots), sub * slots)
            h = h_ref[part, 0].reshape(sub * slots, width)
            logits = jnp.where(lane < experts, dot(h, wr_ref[...]), -1e30)
            e = jnp.exp(logits - jnp.max(logits, axis=1, keepdims=True))
            probs = e / jnp.sum(e, axis=1, keepdims=True)
            gate = jnp.sum(probs * own, axis=1, keepdims=True)
            dz = z_ref[part, 0].reshape(sub * slots, width).astype(F32)
            dexp = (gate * dz).astype(BF16)
            dexp_s[at, :] = dexp
            piece = back = None
            for (win, wout, bias), hid_s, dpre_s in zip(weights, (hid_a, hid_b), (dpre_a, dpre_b)):
                pre = dot(h, win[...]) + bias[...].astype(F32)
                phi, bell = gelu_parts(pre)
                hid = (pre * phi).astype(BF16)
                hid_s[at, :] = hid
                out = dot(hid, wout[...])
                piece = out if piece is None else piece + out
                dpre = (dot_nt(dexp, wout[...]) * (phi + pre * bell)).astype(BF16)
                dpre_s[at, :] = dpre
                out = dot_nt(dpre, win[...])
                back = out if back is None else back + out
            p_ref[at, :] = piece.astype(BF16)
            dgate = jnp.sum(dz * piece, axis=1, keepdims=True)
            dlog = (dgate * probs * (own - gate)).astype(BF16)
            d_ref[at, :] = (back + dot_nt(dlog, wr_ref[...])).astype(BF16)
            groute[...] += dot_tn(h, dlog)
            return 0

        lax.fori_loop(0, h_ref.shape[0] // sub, block, 0)
        for k, (dpre_s, hid_s) in enumerate(((dpre_a, hid_a), (dpre_b, hid_b))):
            to_win, to_bias, to_wout = sums[3 * k : 3 * k + 3]
            dpre = dpre_s[...]
            to_win[...] += dot_tn(h_ref[...].reshape(rows, width), dpre)
            to_bias[...] += jnp.broadcast_to(jnp.sum(dpre.astype(F32), axis=0, keepdims=True), to_bias.shape)
            to_wout[...] += dot_tn(hid_s[...], dexp_s[...])

    @pl.when(i < steps)
    def _():
        work(h0, z0, p0, d0)

    @pl.when(i >= steps)
    def _():
        work(h1, z1, p1, d1)

    @pl.when(i == 2 * steps - 1)
    def _():
        for k, g in enumerate((own_g, got_g)):
            win, wout, bias = parts(g)
            win[...] = sums[3 * k][...].astype(BF16)
            bias[...] = sums[3 * k + 1][...].astype(BF16)
            wout[...] = sums[3 * k + 2][...].astype(BF16)


def expert(expert_id, own_h, other_h, own_z, other_z, places, own_w, got_w, at, w_route, experts):
    sources, _, slots, width = own_h.shape
    rows = sources * slots
    hidden = own_w[0].shape[2]
    group = min(sources, 8)
    block, steps = group * slots, sources // group
    early = lambda i: jnp.minimum(i, steps - 1)
    late = lambda i: jnp.maximum(i - steps, 0)
    once = lambda shape: pl.BlockSpec(shape, lambda i: (0,) * len(shape))
    rows_spec = lambda place, when: pl.BlockSpec((group, 1, slots, width), lambda i: (when(i), place, 0, 0))
    weight = lambda w, k: pl.BlockSpec((None, *w.shape[1:]), lambda i: (k, 0, 0))
    out_first = pl.BlockSpec((block, width), lambda i: (early(i), 0))
    out_second = pl.BlockSpec((block, width), lambda i: (late(i), 0))
    shape = jax.ShapeDtypeStruct
    if hidden == width:
        grads = [shape((1, 2 * width + 16, hidden), BF16)]
    else:
        grads = [shape((1, width + 16, hidden), BF16), shape((1, hidden, width), BF16)]
    outs = [shape((rows, width), BF16)] * 4 + grads * 2 + [shape((width, LANES), F32)]
    spots = (own_h, other_h, own_z, other_z)
    return pl.pallas_call(
        functools.partial(expert_kernel, steps, experts, len(grads)),
        grid=(2 * steps,),
        in_specs=[pl.BlockSpec(memory_space=pltpu.SMEM)]
        + [rows_spec(p, w) for p, w in zip(places, (early, late, early, late))]
        + [weight(w, k) for w, k in zip((*own_w, *got_w), at)]
        + [once(w_route.shape)],
        out_specs=[out_first, out_second, out_first, out_second] + [once(o.shape) for o in outs[4:]],
        out_shape=outs,
        scratch_shapes=[
            *[pltpu.VMEM((block, hidden), BF16)] * 4,
            pltpu.VMEM((block, width), BF16),
            *[pltpu.VMEM(s, F32) for s in ((width, hidden), (16, hidden), (hidden, width))] * 2,
        ],
        compiler_params=pltpu.CompilerParams(vmem_limit_bytes=VMEM),
        cost_estimate=pl.CostEstimate(
            flops=48 * rows * hidden * width, bytes_accessed=20 * width * hidden, transcendentals=4 * rows * hidden
        ),
        name="expert",
    )(expert_id, *spots, *own_w, *got_w, w_route)


def finish_kernel(n, *refs):
    parts, (win, wout, bias) = refs[: 6 * n], refs[-3:]
    for l in range(n):
        for k, out in enumerate((win, wout, bias)):
            out[l] = parts[6 * l + k][...].astype(F32) + parts[6 * l + 3 + k][...].astype(F32)


def finish(own, got):
    n, (_, height, hidden) = len(own), own[0].shape
    width = (height - 16) // 2
    tile = 128
    steps = width // tile
    spec = lambda r, k: pl.BlockSpec((None, r, hidden), lambda i: (0, k(i), 0))
    three = [spec(tile, lambda i: i), spec(tile, lambda i: steps + i), spec(16, lambda i: 2 * width // 16)]
    flat = [x for pair in zip(own, got) for a in pair for x in (a, a, a)]
    big = pl.BlockSpec((n, tile, hidden), lambda i: (0, i, 0))
    shape = jax.ShapeDtypeStruct
    return pl.pallas_call(
        functools.partial(finish_kernel, n),
        grid=(steps,),
        in_specs=three * (2 * n),
        out_specs=[big, big, pl.BlockSpec((n, 16, hidden), lambda i: (0, 0, 0))],
        out_shape=[shape((n, width, hidden), F32), shape((n, width, hidden), F32), shape((n, 16, hidden), F32)],
        compiler_params=pltpu.CompilerParams(vmem_limit_bytes=VMEM),
        cost_estimate=pl.CostEstimate(
            flops=2 * n * height * hidden, bytes_accessed=8 * n * height * hidden, transcendentals=0
        ),
        name="finish",
    )(*flat)


def to_send_kernel(in_ref, out_ref, *refs):
    for l in range(in_ref.shape[0]):
        refs[2 * l][0] = in_ref[l]
        refs[2 * l + 1][0] = out_ref[l]


def to_send(w_in, w_out):
    groups = w_in.shape[0]
    steps = w_in.shape[1] // 128
    spec = lambda a, k: pl.BlockSpec((k, a.shape[1] // steps, a.shape[2]), lambda i: (0, i, 0))
    flat = pl.pallas_call(
        to_send_kernel,
        grid=(steps,),
        in_specs=[spec(w_in, groups), spec(w_out, groups)],
        out_specs=[spec(w_in, 1), spec(w_out, 1)] * groups,
        out_shape=[jax.ShapeDtypeStruct((1, *a.shape[1:]), BF16) for a in (w_in, w_out)] * groups,
        compiler_params=pltpu.CompilerParams(vmem_limit_bytes=VMEM),
        cost_estimate=COST,
        name="to_send",
    )(w_in, w_out)
    return [flat[2 * l : 2 * l + 2] for l in range(groups)]


def turn_kernel(x_ref, y_ref, x_out, y_out):
    x_out[...] = x_ref[...].T
    y_out[...] = y_ref[...].T


def turn(x, y):
    whole = lambda a, b: pl.BlockSpec((a, b), lambda i: (0, 0))
    tokens, width = x.shape
    return pl.pallas_call(
        turn_kernel,
        grid=(1,),
        in_specs=[whole(tokens, width)] * 2,
        out_specs=[whole(width, tokens)] * 2,
        out_shape=[jax.ShapeDtypeStruct((width, tokens), x.dtype)] * 2,
        compiler_params=pltpu.CompilerParams(vmem_limit_bytes=VMEM),
        name="turn",
    )(x, y)


def outer_kernel(h_ref, a_ref, g_ref, b_ref, rest_ref, sums_ref, out_ref):
    width = b_ref.shape[1]
    for k in range(3):
        out_ref[:, k * width : (k + 1) * width] = dot(h_ref[...], g_ref[k]).astype(BF16)
    out_ref[:, 3 * width : 4 * width] = dot(a_ref[...], b_ref[...]).astype(BF16)
    out_ref[:, 4 * width : 4 * width + LANES] = rest_ref[...]
    out_ref[:, 4 * width + LANES :] = sums_ref[...].T.astype(BF16)


def outer(h, a, g, b, rest, sums):
    width, tokens = h.shape
    tile = 256
    whole = lambda *shape: pl.BlockSpec(shape, lambda i: (0,) * len(shape))
    rows = lambda n: pl.BlockSpec((tile, n), lambda i: (i, 0))
    columns = 4 * width + 2 * LANES
    return pl.pallas_call(
        outer_kernel,
        grid=(width // tile,),
        in_specs=[
            rows(tokens), rows(tokens), whole(3, tokens, width), whole(tokens, width), rows(LANES),
            pl.BlockSpec((LANES, tile), lambda i: (0, i)),
        ],
        out_specs=rows(columns),
        out_shape=jax.ShapeDtypeStruct((width, columns), BF16),
        compiler_params=pltpu.CompilerParams(vmem_limit_bytes=VMEM),
        cost_estimate=COST,
        name="outer",
    )(h, a, g, b, rest, sums)


def input_kernel(g_ref, w_ref, x_ref, dy_ref, gain_ref, out_ref, sums_ref):
    width = x_ref.shape[1]

    @pl.when(pl.program_id(0) == 0)
    def _():
        sums_ref[...] = jnp.zeros_like(sums_ref)

    grad = dot_nt(g_ref[0], w_ref[:, :width])
    for k in (1, 2):
        grad += dot_nt(g_ref[k], w_ref[:, k * width : (k + 1) * width])
    unit, rstd = normed(x_ref[...].astype(F32))
    out_ref[...] = dy_ref[...] + norm_back(grad, gain_ref[...], unit, rstd)
    add = lambda t: jnp.sum(t, axis=0, keepdims=True)
    sums_ref[0:1, :] += add(grad * unit)
    sums_ref[1:2, :] += add(grad)
    sums_ref[2:3, :] += add(g_ref[0].astype(F32))
    sums_ref[3:4, :] += add(g_ref[2].astype(F32))


def input_back(g, wide, tokens, dy, gain):
    count, width = tokens.shape
    tile = 256
    rows = pl.BlockSpec((tile, width), lambda i: (i, 0))
    whole = lambda *shape: pl.BlockSpec(shape, lambda i: (0,) * len(shape))
    return pl.pallas_call(
        input_kernel,
        grid=(count // tile,),
        in_specs=[
            pl.BlockSpec((3, tile, width), lambda i: (0, i, 0)), whole(*wide.shape), rows, rows, whole(1, width),
        ],
        out_specs=[rows, whole(LANES, width)],
        out_shape=[jax.ShapeDtypeStruct((count, width), F32), jax.ShapeDtypeStruct((LANES, width), F32)],
        compiler_params=pltpu.CompilerParams(vmem_limit_bytes=VMEM),
        cost_estimate=COST,
        name="input_back",
    )(g, wide, tokens, dy, gain)


def normed(x):
    centred = x - jnp.mean(x, axis=-1, keepdims=True)
    rstd = lax.rsqrt(jnp.mean(centred * centred, axis=-1, keepdims=True) + EPSILON)
    return centred * rstd, rstd


def norm_back(grad, gain, unit, rstd):
    g = grad * gain
    mean = lambda t: jnp.mean(t, axis=-1, keepdims=True)
    return rstd * (g - mean(g) - unit * mean(g * unit))


def pad_columns(x, count):
    return jnp.pad(x, ((0, 0), (0, count - x.shape[1])))


def up(count):
    return -(-count // LANES) * LANES


def local(
    tokens, cotangent, segment_ids, routes, capacity, ln1_gain, ln1_bias, w_query, b_query, w_key, w_value,
    b_value, w_output, b_output, ln2_gain, ln2_bias, w_router, w_in, b_in, w_out, b_out,
):
    row_count, width = tokens.shape
    experts = capacity.shape[0]
    slots = 2 * row_count // experts
    groups = w_in.shape[0]
    owners = lax.axis_size("expert")
    split = groups * owners // experts
    share = w_query.shape[0]
    devices = lax.axis_size("batch") * owners
    me = lax.axis_index("expert")
    chunk = min(2, groups)
    layout = (groups, chunk, split, slots)
    firsts = tuple(range(0, groups, chunk))
    pair = lambda first: range(first, first + chunk)
    heavy = lambda l: 1 if l % 2 == 0 else 2
    light = lambda l: 3 - heavy(l)

    spread = -(-experts // share)
    fold = lambda x: jnp.pad(x, (0, spread * share - experts)).reshape(spread, share).T
    unfold = lambda x: x.T.reshape(-1)[:experts]

    chosen = routes[:, 0]
    picked = chosen[:, None] == jnp.arange(experts, dtype=jnp.int32)[None, :]
    picked_float = picked.astype(F32)
    position = jnp.arange(row_count, dtype=jnp.int32)
    earlier = (position[None, :] < position[:, None]).astype(BF16)
    rank = dot(earlier, picked.astype(BF16))
    slot = jnp.sum(rank * picked_float, axis=1)
    limit = jnp.sum(capacity.astype(F32)[None, :] * picked_float, axis=1)
    kept = slot < limit
    kept_float = kept.astype(F32)
    ids = jnp.where(kept, chosen * slots + slot.astype(jnp.int32), -1)
    id_row, id_col = ids[None, :], ids[:, None]
    counts = jnp.sum(picked_float, axis=0)

    def send(x, first, count):
        rows = dispatch(id_row, x, count * owners * slots, (groups, count, split, slots), first)
        return rows.reshape(owners, count, slots, width)

    grad_send = send(cotangent, 0, groups)

    small = jnp.stack([ln1_gain, ln1_bias, b_query, b_value, b_output, ln2_gain, ln2_bias], axis=1)
    tally = fold(counts).astype(BF16)
    extra = pad_columns(jnp.concatenate([small, tally], axis=1), up(7 + spread))
    wide = jnp.concatenate([w_query, w_key, w_value, extra], axis=1)
    rest = jnp.concatenate([w_router, b_out.T], axis=1)
    rest = jnp.concatenate([w_output, pad_columns(rest, up(2 * experts))], axis=1)
    if staged():
        wide, rest = gather_first(wide), gather_first(rest)
        rest_first = rest
        sent_w = to_send(*after((w_in, w_out), grad_send))
        free = gather_second(wide, (grad_send, sent_w))
        wide = gather_third(free)
        rest = after(rest, free)
    else:
        wide = lax.all_gather(wide, ALL, axis=0, tiled=True)
        rest = lax.all_gather(rest, ALL, axis=0, tiled=True)
        free = rest_first = ()
        sent_w = to_send(w_in, w_out)

    bias_rows = b_in[:, None, :]
    got_bias = [swap(after(bias_rows, free), "batch", mask) for mask in (1, 2)]
    got_w, last = [], free
    for l in range(groups):
        if l % chunk == 0:
            last = got_w[-chunk:] or free
        got_w.append([swap(w, "batch", heavy(l)) for w in after(sent_w[l], last)])

    own_z = to_owners(after(grad_send, rest_first))
    theirs = lambda rows, l, at: swap(rows[:, at : at + 1], "batch", light(l))
    other_z = [theirs(own_z, l, l) for l in range(groups)]

    vectors = wide[:, 3 * width : 3 * width + 7].astype(F32).T
    gain_one, shift_one, bias_query, bias_value, bias_output, gain_two, shift_two = vectors
    tallies = wide[:, 3 * width + 7 : 3 * width + 7 + spread].astype(F32).reshape(devices, share, spread)
    all_counts = unfold(jnp.sum(tallies, axis=0))
    token_total = float(row_count * devices)
    fraction = all_counts / token_total

    inputs = tokens.astype(F32)
    unit_one, rstd_one = normed(inputs)
    h_one = (unit_one * gain_one + shift_one).astype(BF16)
    nothing = jnp.zeros((width,), F32)
    bias = jnp.concatenate([bias_query, nothing, bias_value, jnp.zeros((wide.shape[1] - 3 * width,), F32)])
    qkv = after((dot(h_one, wide) + bias).astype(BF16), [w[0] for w in got_w[:chunk]])
    if staged():
        rest = gather_second(rest, qkv)
    seg_row = segment_ids.reshape(1, row_count)
    seg_col = segment_ids.reshape(row_count, 1)
    attended, logs = attend(qkv, seg_row, seg_col, width)
    if staged():
        rest = gather_third(rest, attended)
    full_output = rest[:, :width]
    full_router = pad_columns(rest[:, width : width + experts], LANES)
    bias_expert = rest[:, width + experts : width + 2 * experts].T
    resid = inputs + dot(attended, full_output) + bias_output
    unit_two, rstd_two = normed(resid)
    h_two = (unit_two * gain_two + shift_two).astype(BF16)
    h_two = after(h_two, own_z, [w[1] for w in got_w[:chunk]])

    rows = [send(h_two, first, chunk) for first in firsts]
    token_rows = []
    for at in range(len(firsts)):
        if at:
            rows[at] = after(rows[at], token_rows[-1], [w[0] for w in got_w[chunk:]])
        token_rows.append(to_owners(rows[at]))
    token_rows = [after(t, rows) for t in token_rows]
    their_h = [token_rows[l // chunk][:, l % chunk : l % chunk + 1] for l in range(groups)]
    their_h = [lax.optimization_barrier(their_h[first : first + chunk]) for first in firsts]
    other_h = [swap(their_h[l // chunk][l % chunk], "batch", light(l)) for l in range(groups)]
    h_turned, att_turned = turn(h_one, attended)

    router_probs = jax.nn.softmax(dot(h_two, full_router)[:, :experts], axis=-1)
    mixing = kept_float * jnp.sum(router_probs * picked_float, axis=1)
    grad_out = cotangent.astype(F32)
    expert_bias = dot(picked.astype(BF16), bias_expert)
    gate_bias = kept_float * jnp.sum(grad_out * expert_bias, axis=1)
    grad_probs = picked_float * gate_bias[:, None] + BALANCE * experts * fraction[None, :] / token_total
    grad_logits = router_probs * (grad_probs - jnp.sum(grad_probs * router_probs, axis=1, keepdims=True))
    grad_logits = grad_logits.astype(BF16)
    mixed = picked_float * mixing[:, None]
    mixed_high = mixed.astype(BF16)
    mixed_low = (mixed - mixed_high.astype(F32)).astype(BF16)
    grad_bias_expert = dot_tn(cotangent, mixed_high) + dot_tn(cotangent, mixed_low)
    home_router = dot_tn(h_two, grad_logits)
    home_h_two = dot_nt(grad_logits, full_router[:, :experts])
    home_h_two, home_router, grad_bias_expert, probs_sum = lax.optimization_barrier(
        (home_h_two, home_router, grad_bias_expert, jnp.sum(router_probs, axis=0))
    )
    made, returned, piece_sums, got_g = [], [], [], []
    for at, first in enumerate(firsts):
        for l in pair(first):
            number = ((me * groups + l) // split).astype(jnp.int32).reshape(1)
            if l == 0:
                number = after(number, h_turned, home_h_two)
            if l == 1:
                number = after(number, made[-1], got_w[-chunk:], their_h)
            made.append(
                expert(
                    number, token_rows[at], other_h[l], own_z, other_z[l], (l - first, 0, l, 0),
                    (w_in, w_out, bias_rows), (*got_w[l], got_bias[heavy(l) - 1]), (l, l, l, 0, 0, l),
                    full_router, experts,
                )
            )
        sums = [(made[l][2], swap(after(made[l][3], other_h), "batch", light(l))) for l in pair(first)]
        rows = merge(sums, owners, slots)
        if returned:
            rows = after(rows, returned[-1], got_g)
        returned.append(to_owners(rows).reshape(-1, width))
        n = (len(made[0]) - 5) // 2
        if first + chunk == groups:
            piece_sums = [(m[0], swap(after(m[1], sums), "batch", light(l))) for l, m in enumerate(made)]
        for l in pair(first):
            grads = after(made[l][4 + n : 4 + 2 * n], sums, other_h, piece_sums)
            got_g.append([swap(g, "batch", heavy(l)) for g in grads])
    own_g = [m[4 : 4 + n] for m in made]

    grad_router = home_router + sum(m[-1] for m in made)[:, :experts]

    grad_h_two = home_h_two + combine(after(id_col, piece_sums), returned, layout, firsts)
    grad_resid = grad_out + norm_back(grad_h_two, gain_two, unit_two, rstd_two)
    grad_branch = grad_resid.astype(BF16)
    grad_att = dot_nt(grad_branch, full_output).astype(BF16)
    columns = lambda *rows: jnp.stack(rows, axis=1)
    prob_sums = jnp.tile(fold(probs_sum), (devices, 1))
    sums = columns(
        jnp.sum(grad_h_two * unit_two, axis=0), jnp.sum(grad_h_two, axis=0), jnp.sum(grad_branch.astype(F32), axis=0)
    )
    packed = jnp.concatenate([grad_router, grad_bias_expert, sums, prob_sums], axis=1)
    packed = pad_columns(packed, LANES).astype(BF16)
    merged = merge(after(piece_sums, grad_att, packed), owners, slots)
    pieces = to_owners(merged).reshape(-1, width)
    grad_att = after(grad_att, merged, packed)
    dqkv = attend_back(qkv, grad_att, logs, seg_row, seg_col, width)

    dqkv, got_g = after((dqkv, got_g), got_g)
    input_grad, sums = input_back(dqkv, wide, tokens, grad_resid, gain_one[None])
    def close(waiting):
        own, got, _ = waiting
        if n == 1:
            win, wout, bias = finish([g[0] for g in own], [g[0] for g in got])
            return win, bias[:, 0], wout
        both = [[a[0].astype(F32) + b[0].astype(F32) for a, b in zip(*pair_g)] for pair_g in zip(own, got)]
        return (
            jnp.stack([g[0][:width] for g in both]),
            jnp.stack([g[0][width] for g in both]),
            jnp.stack([g[1] for g in both]),
        )

    wide_sum, (grad_w_in, grad_b_in, grad_w_out) = scatter_rows(
        outer(h_turned, att_turned, dqkv, grad_branch, packed, sums), (own_g, got_g, pieces), close
    )
    pieces = after(pieces, grad_b_in)
    fetched = combine(id_col, [pieces], (groups, groups, split, slots), (0,))
    block_out = (resid + mixing[:, None] * (fetched + expert_bias)).astype(BF16)
    router_sum = wide_sum[:, 4 * width : 4 * width + 2 * experts]
    side = wide_sum[:, 4 * width + 2 * experts :]
    late_side = wide_sum[:, 4 * width + LANES :]
    mean_probs = unfold(side[:, 3 : 3 + spread]) / token_total
    balance_loss = experts * jnp.sum(fraction * mean_probs)
    expert_shares = jnp.stack([experts * fraction, experts * mean_probs])

    return (
        block_out,
        balance_loss,
        expert_shares,
        input_grad,
        late_side[:, 0],
        late_side[:, 1],
        wide_sum[:, :width],
        late_side[:, 2],
        wide_sum[:, width : 2 * width],
        wide_sum[:, 2 * width : 3 * width],
        late_side[:, 3],
        wide_sum[:, 3 * width : 4 * width],
        side[:, 2],
        side[:, 0],
        side[:, 1],
        router_sum[:, :experts],
        grad_w_in,
        grad_b_in,
        grad_w_out,
        router_sum[:, experts:].T,
    )


def solution(mesh):
    rows, split = P(ALL, None), P(ALL)
    experts = (P("expert", None, "batch"), P("expert", "batch"), P("expert", "batch", None), P(None, ALL))
    return jax.shard_map(
        local,
        mesh=mesh,
        in_specs=(
            rows, rows, rows, rows, P(), split, split, rows, split, rows, rows, split, rows, split, split, split,
            rows, *experts,
        ),
        out_specs=(
            rows, P(), P(), rows, split, split, rows, split, rows, rows, split, rows, split, split, split, rows,
            *experts,
        ),
        check_vma=False,
    )
```

```python
import functools

import jax
import jax.numpy as jnp
from jax import lax
from jax.experimental import pallas as pl
from jax.experimental.pallas import tpu as pltpu
from jax.sharding import PartitionSpec as P

HEAD = 64
LANES = 128
REACH = 384
QROWS = 256
EPSILON = 1e-05
BALANCE = 0.01
ALL = ("batch", "expert")
VMEM = 60 * 1024 * 1024
COST = pl.CostEstimate(flops=1, bytes_accessed=1, transcendentals=0)
F32 = jnp.float32
BF16 = jnp.bfloat16


def dot(a, b):
    return jnp.dot(a, b, preferred_element_type=F32)


def dot_nt(a, b):
    return lax.dot_general(a, b, (((1,), (1,)), ((), ())), preferred_element_type=F32)


def dot_tn(a, b):
    return lax.dot_general(a, b, (((0,), (0,)), ((), ())), preferred_element_type=F32)


def swap(x, axis, mask):
    return lax.ppermute(x, axis, [(i, i ^ mask) for i in range(lax.axis_size(axis))])


def shift(x, step):
    size = lax.axis_size("expert")
    return lax.ppermute(x, "expert", [(i, (i + step) % size) for i in range(size)])


def staged():
    return lax.axis_size("batch") == 4 and lax.axis_size("expert") == 8


def gather_first(x):
    mz = lax.axis_index("expert") // 2
    ring = [shift(x, 2 * k) for k in (3, 2, 1)] + [x]
    ring = jnp.stack(ring + ring[:3])
    return lax.dynamic_slice_in_dim(ring, 3 - mz, 4, 0)


def gather_second(zs, beside):
    mb = lax.axis_index("batch")
    b = after([zs] + [swap(zs, "batch", k) for k in (1, 2, 3)], beside)
    odd, high = (mb & 1) == 1, (mb & 2) == 2
    u = [jnp.where(odd, b[i ^ 1], b[i]) for i in range(4)]
    return jnp.stack([jnp.where(high, u[i ^ 2], u[i]) for i in range(4)])


def gather_third(rows, beside=()):
    mc = lax.axis_index("expert") % 2
    other = after(swap(rows, "expert", 1), beside)
    both = jnp.stack(
        [jnp.where(mc == 0, rows, other), jnp.where(mc == 0, other, rows)], axis=2
    )
    return both.reshape(-1, rows.shape[-1])


def scatter_rows(g, before, beside):
    if not staged():
        return lax.psum_scatter(g, ALL, scatter_dimension=0, tiled=True).astype(F32), beside(before)
    mb, me = lax.axis_index("batch"), lax.axis_index("expert")
    mz, mc = me // 2, me % 2
    r, c = g.shape[0] // 32, g.shape[1]
    g = g.reshape(4, 4, 2, r, c)
    mine = jnp.where(mc == 0, g[:, :, 0], g[:, :, 1])
    other = swap(jnp.where(mc == 0, g[:, :, 1], g[:, :, 0]), "expert", 1)
    s = (mine.astype(F32) + other.astype(F32)).astype(BF16)
    made = beside(after(before, s))
    pick = lambda t, i: lax.dynamic_index_in_dim(t, i, 0, keepdims=False)
    parts = after([swap(pick(s, mb ^ k), "batch", k) for k in (1, 2, 3)], made, before)
    t = sum((p.astype(F32) for p in parts), pick(s, mb).astype(F32)).astype(BF16)
    parts = [shift(pick(t, (mz + k) % 4), 2 * k) for k in (1, 2, 3)]
    return sum((p.astype(F32) for p in parts), pick(t, mz).astype(F32)), made


def to_owners(x):
    return lax.all_to_all(x, "expert", split_axis=0, concat_axis=0, tiled=True)


def after(x, *others):
    return lax.optimization_barrier((x, others))[0]


def windows(length):
    for start in range(0, length, QROWS):
        yield start, max(0, start - REACH), start + QROWS


def half_masks():
    lane = lax.broadcasted_iota(jnp.int32, (1, LANES), 1)
    first = (lane < HEAD).astype(F32)
    return first, (first.astype(BF16), (1.0 - first).astype(BF16))


def attend_kernel(q_ref, k_ref, v_ref, row_ref, col_ref, out_ref, log_ref, mask_ref):
    length = q_ref.shape[0]

    @pl.when(pl.program_id(0) == 0)
    def _():
        for n, (start, low, stop) in enumerate(windows(length)):
            shape = (QROWS, stop - low)
            i = lax.broadcasted_iota(jnp.int32, shape, 0) + start
            j = lax.broadcasted_iota(jnp.int32, shape, 1) + low
            same = col_ref[start:stop, :] == row_ref[:, low:stop]
            mask_ref[n, :, : stop - low] = jnp.where((j <= i) & same, 0.0, -1e30)

    first, halves = half_masks()
    for n, (start, low, stop) in enumerate(windows(length)):
        q = q_ref[start:stop, :] * jnp.asarray(HEAD**-0.5, BF16)
        both = jnp.concatenate([q * half for half in halves])
        mask = mask_ref[n, :, : stop - low]
        s = dot_nt(both, k_ref[low:stop, :]) + jnp.concatenate([mask, mask])
        top = jnp.max(s, axis=1, keepdims=True)
        e = jnp.exp(s - top)
        sums = jnp.sum(e, axis=1, keepdims=True)
        out = dot(e.astype(BF16), v_ref[low:stop, :]) / sums
        logs = top + jnp.log(sums)
        out_ref[start:stop, :] = (out[:QROWS] * first + out[QROWS:] * (1.0 - first)).astype(BF16)
        log_ref[start:stop, :] = logs[:QROWS] * first + logs[QROWS:] * (1.0 - first)


def attend(qkv, seg_row, seg_col, width):
    length = qkv.shape[0]
    pairs = width // LANES
    spec = lambda offset: pl.BlockSpec((length, LANES), lambda p, o=offset: (0, o + p))
    whole = lambda shape: pl.BlockSpec(shape, lambda p: (0,) * len(shape))
    return pl.pallas_call(
        attend_kernel,
        grid=(pairs,),
        in_specs=[spec(0), spec(pairs), spec(2 * pairs), whole((1, length)), whole((length, 1))],
        out_specs=[spec(0), spec(0)],
        out_shape=[
            jax.ShapeDtypeStruct((length, width), BF16),
            jax.ShapeDtypeStruct((length, width), F32),
        ],
        scratch_shapes=[pltpu.VMEM((length // QROWS, QROWS, QROWS + REACH), F32)],
        compiler_params=pltpu.CompilerParams(vmem_limit_bytes=VMEM),
        cost_estimate=COST,
        name="attend",
    )(qkv, qkv, qkv, seg_row, seg_col)


def attend_back_kernel(
    q_ref, k_ref, v_ref, g_ref, log_ref, row_ref, col_ref, out_ref, mask_ref, dk_ref, dv_ref
):
    length = q_ref.shape[0]

    @pl.when(pl.program_id(0) == 0)
    def _():
        for n, (start, low, stop) in enumerate(windows(length)):
            shape = (stop - low, QROWS)
            j = lax.broadcasted_iota(jnp.int32, shape, 0) + low
            i = lax.broadcasted_iota(jnp.int32, shape, 1) + start
            same = col_ref[low:stop, :] == row_ref[:, start:stop]
            mask_ref[n, : stop - low, :] = jnp.where((j <= i) & same, 0.0, -1e30)

    dk_ref[...] = jnp.zeros_like(dk_ref)
    dv_ref[...] = jnp.zeros_like(dv_ref)
    first, halves = half_masks()
    scale = HEAD**-0.5
    for n, (start, low, stop) in enumerate(windows(length)):
        q = q_ref[start:stop, :] * jnp.asarray(scale, BF16)
        g = g_ref[start:stop, :]
        k, v = k_ref[low:stop, :], v_ref[low:stop, :]
        turned = log_ref[start:stop, :].T
        logs = jnp.concatenate([turned[:1, :], turned[HEAD : HEAD + 1, :]], axis=1)
        qs = jnp.concatenate([q * half for half in halves])
        gs = jnp.concatenate([g * half for half in halves])
        mask = mask_ref[n, : stop - low, :]
        p = jnp.exp(dot_nt(k, qs) + jnp.concatenate([mask, mask], axis=1) - logs)
        dp = dot_nt(v, gs)
        centre = jnp.sum(dp * p, axis=0, keepdims=True)
        ds = (p * (dp - centre)).astype(BF16)
        dv_ref[low:stop, :] += dot(p.astype(BF16), gs)
        dk_ref[low:stop, :] += dot(ds, qs)
        dqs = dot_tn(ds, k)
        dq = dqs[:QROWS] * first + dqs[QROWS:] * (1.0 - first)
        out_ref[0, start:stop, :] = (dq * scale).astype(BF16)
    out_ref[1] = dk_ref[...].astype(BF16)
    out_ref[2] = dv_ref[...].astype(BF16)


def attend_back(qkv, grad, logs, seg_row, seg_col, width):
    length = qkv.shape[0]
    pairs = width // LANES
    spec = lambda offset: pl.BlockSpec((length, LANES), lambda p, o=offset: (0, o + p))
    whole = lambda shape: pl.BlockSpec(shape, lambda p: (0,) * len(shape))
    return pl.pallas_call(
        attend_back_kernel,
        grid=(pairs,),
        in_specs=[spec(0), spec(pairs), spec(2 * pairs), spec(0), spec(0), whole((1, length)), whole((length, 1))],
        out_specs=pl.BlockSpec((3, length, LANES), lambda p: (0, 0, p)),
        out_shape=jax.ShapeDtypeStruct((3, length, width), BF16),
        scratch_shapes=[
            pltpu.VMEM((length // QROWS, QROWS + REACH, QROWS), F32),
            pltpu.VMEM((length, LANES), F32),
            pltpu.VMEM((length, LANES), F32),
        ],
        compiler_params=pltpu.CompilerParams(vmem_limit_bytes=VMEM),
        cost_estimate=COST,
        name="attend_back",
    )(qkv, qkv, qkv, grad, logs, seg_row, seg_col)


def slot_ids(shape, axis, base, layout, first):
    groups, chunk, split, slots = layout
    at = lax.broadcasted_iota(jnp.int32, shape, axis) + base
    row, slot = at // slots, at % slots
    return (row // chunk * groups + first + row % chunk) // split * slots + slot


def dispatch_kernel(layout, first, id_ref, x_ref, out_ref):
    rows, tokens = out_ref.shape[0], x_ref.shape[0]
    ids = slot_ids((rows, 1), 0, pl.program_id(0) * rows, layout, first)
    chosen = jnp.where(ids == id_ref[...], 1.0, 0.0).astype(BF16)
    out_ref[...] = dot(chosen, x_ref[...]).astype(BF16)


def dispatch(ids, x, count, layout, first):
    tokens, width = x.shape
    block = min(count, 512)
    return pl.pallas_call(
        functools.partial(dispatch_kernel, layout, first),
        grid=(count // block,),
        in_specs=[
            pl.BlockSpec((1, tokens), lambda i: (0, 0)),
            pl.BlockSpec((tokens, width), lambda i: (0, 0)),
        ],
        out_specs=pl.BlockSpec((block, width), lambda i: (i, 0)),
        out_shape=jax.ShapeDtypeStruct((count, width), BF16),
        compiler_params=pltpu.CompilerParams(vmem_limit_bytes=VMEM),
        cost_estimate=pl.CostEstimate(
            flops=2 * count * tokens * width, bytes_accessed=4 * count * width, transcendentals=0
        ),
        name="dispatch",
    )(ids, x)


def combine_kernel(layout, firsts, id_ref, *refs):
    *x_refs, out_ref = refs
    out_ref[...] = jnp.zeros_like(out_ref)
    for first, x_ref in zip(firsts, x_refs):
        step = min(x_ref.shape[0], 512)
        for base in range(0, x_ref.shape[0], step):
            ids = slot_ids((1, step), 1, base, layout, first)
            chosen = jnp.where(id_ref[...] == ids, 1.0, 0.0).astype(BF16)
            out_ref[...] += dot(chosen, x_ref[base : base + step, :])


def combine(ids, xs, layout, firsts):
    tokens, (count, width), block = ids.shape[0], xs[0].shape, 256
    return pl.pallas_call(
        functools.partial(combine_kernel, layout, firsts),
        grid=(tokens // block,),
        in_specs=[pl.BlockSpec((block, 1), lambda i: (i, 0))]
        + [pl.BlockSpec((count, width), lambda i: (0, 0)) for _ in xs],
        out_specs=pl.BlockSpec((block, width), lambda i: (i, 0)),
        out_shape=jax.ShapeDtypeStruct((tokens, width), F32),
        compiler_params=pltpu.CompilerParams(vmem_limit_bytes=VMEM),
        cost_estimate=pl.CostEstimate(
            flops=2 * count * len(xs) * tokens * width,
            bytes_accessed=2 * count * len(xs) * width + 4 * tokens * width,
            transcendentals=0,
        ),
        name="combine",
    )(ids, *xs)


def merge_kernel(*refs):
    *parts, out_ref = refs
    owners, chunk, slots, width = out_ref.shape
    for l in range(chunk):
        both = parts[2 * l][...].astype(F32) + parts[2 * l + 1][...].astype(F32)
        out_ref[:, l] = both.astype(BF16).reshape(owners, slots, width)


def merge(pairs, owners, slots):
    rows, width = pairs[0][0].shape
    block = min(owners, 4)
    flat = [part for pair in pairs for part in pair]
    return pl.pallas_call(
        merge_kernel,
        grid=(owners // block,),
        in_specs=[pl.BlockSpec((block * slots, width), lambda i: (i, 0)) for _ in flat],
        out_specs=pl.BlockSpec((block, len(pairs), slots, width), lambda i: (i, 0, 0, 0)),
        out_shape=jax.ShapeDtypeStruct((owners, len(pairs), slots, width), BF16),
        compiler_params=pltpu.CompilerParams(vmem_limit_bytes=VMEM),
        cost_estimate=pl.CostEstimate(
            flops=len(flat) * rows * width, bytes_accessed=3 * len(flat) * rows * width, transcendentals=0
        ),
        name="merge",
    )(*flat)


def gelu_parts(x):
    size = jnp.abs(x)
    t = 1.0 / (1.0 + (0.3275911 * 0.5**0.5) * size)
    bell = jnp.exp(-0.5 * x * x)
    poly = t * (
        0.5 * 0.254829592
        + t * (0.5 * -0.284496736 + t * (0.5 * 1.421413741 + t * (0.5 * -1.453152027 + t * (0.5 * 1.061405429))))
    )
    tail = poly * bell
    return jnp.where(x < 0, tail, 1.0 - tail), bell * 0.3989422804014327


def expert_kernel(steps, experts, n, *refs):
    id_ref, h0, h1, z0, z1 = refs[:5]
    weights = refs[5:8], refs[8:11]
    wr_ref, p0, p1, d0, d1 = refs[11:16]
    own_g, got_g = refs[16 : 16 + n], refs[16 + n : 16 + 2 * n]
    refs = refs[16 + 2 * n :]
    groute, hid_a, hid_b, dpre_a, dpre_b, dexp_s, *sums = refs
    i = pl.program_id(0)
    width = wr_ref.shape[0]
    slots = h0.shape[2]
    rows = h0.shape[0] * slots
    sub = min(h0.shape[0], 4)
    hidden = hid_a.shape[1]

    def parts(w):
        if n == 1:
            return w[0].at[0, :width], w[0].at[0, width : 2 * width], w[0].at[0, 2 * width :]
        return w[0].at[0, :width], w[1].at[0], w[0].at[0, width:]

    @pl.when(i == 0)
    def _():
        groute[...] = jnp.zeros_like(groute)
        for total_ref in sums:
            total_ref[...] = jnp.zeros_like(total_ref)

    def work(h_ref, z_ref, p_ref, d_ref):
        lane = lax.broadcasted_iota(jnp.int32, (1, LANES), 1)
        own = (lane == id_ref[0]).astype(F32)

        def block(m, _):
            part = pl.ds(m * sub, sub)
            at = pl.ds(pl.multiple_of(m * sub * slots, sub * slots), sub * slots)
            h = h_ref[part, 0].reshape(sub * slots, width)
            logits = jnp.where(lane < experts, dot(h, wr_ref[...]), -1e30)
            e = jnp.exp(logits - jnp.max(logits, axis=1, keepdims=True))
            probs = e / jnp.sum(e, axis=1, keepdims=True)
            gate = jnp.sum(probs * own, axis=1, keepdims=True)
            dz = z_ref[part, 0].reshape(sub * slots, width).astype(F32)
            dexp = (gate * dz).astype(BF16)
            dexp_s[at, :] = dexp
            piece = back = None
            for (win, wout, bias), hid_s, dpre_s in zip(weights, (hid_a, hid_b), (dpre_a, dpre_b)):
                pre = dot(h, win[...]) + bias[...].astype(F32)
                phi, bell = gelu_parts(pre)
                hid = (pre * phi).astype(BF16)
                hid_s[at, :] = hid
                out = dot(hid, wout[...])
                piece = out if piece is None else piece + out
                dpre = (dot_nt(dexp, wout[...]) * (phi + pre * bell)).astype(BF16)
                dpre_s[at, :] = dpre
                out = dot_nt(dpre, win[...])
                back = out if back is None else back + out
            p_ref[at, :] = piece.astype(BF16)
            dgate = jnp.sum(dz * piece, axis=1, keepdims=True)
            dlog = (dgate * probs * (own - gate)).astype(BF16)
            d_ref[at, :] = (back + dot_nt(dlog, wr_ref[...])).astype(BF16)
            groute[...] += dot_tn(h, dlog)
            return 0

        lax.fori_loop(0, h_ref.shape[0] // sub, block, 0)
        for k, (dpre_s, hid_s) in enumerate(((dpre_a, hid_a), (dpre_b, hid_b))):
            to_win, to_bias, to_wout = sums[3 * k : 3 * k + 3]
            dpre = dpre_s[...]
            to_win[...] += dot_tn(h_ref[...].reshape(rows, width), dpre)
            to_bias[...] += jnp.broadcast_to(jnp.sum(dpre.astype(F32), axis=0, keepdims=True), to_bias.shape)
            to_wout[...] += dot_tn(hid_s[...], dexp_s[...])

    @pl.when(i < steps)
    def _():
        work(h0, z0, p0, d0)

    @pl.when(i >= steps)
    def _():
        work(h1, z1, p1, d1)

    @pl.when(i == 2 * steps - 1)
    def _():
        for k, g in enumerate((own_g, got_g)):
            win, wout, bias = parts(g)
            win[...] = sums[3 * k][...].astype(BF16)
            bias[...] = sums[3 * k + 1][...].astype(BF16)
            wout[...] = sums[3 * k + 2][...].astype(BF16)


def expert(expert_id, own_h, other_h, own_z, other_z, places, own_w, got_w, at, w_route, experts):
    sources, _, slots, width = own_h.shape
    rows = sources * slots
    hidden = own_w[0].shape[2]
    group = min(sources, 8)
    block, steps = group * slots, sources // group
    early = lambda i: jnp.minimum(i, steps - 1)
    late = lambda i: jnp.maximum(i - steps, 0)
    once = lambda shape: pl.BlockSpec(shape, lambda i: (0,) * len(shape))
    rows_spec = lambda place, when: pl.BlockSpec((group, 1, slots, width), lambda i: (when(i), place, 0, 0))
    weight = lambda w, k: pl.BlockSpec((None, *w.shape[1:]), lambda i: (k, 0, 0))
    out_first = pl.BlockSpec((block, width), lambda i: (early(i), 0))
    out_second = pl.BlockSpec((block, width), lambda i: (late(i), 0))
    shape = jax.ShapeDtypeStruct
    if hidden == width:
        grads = [shape((1, 2 * width + 16, hidden), BF16)]
    else:
        grads = [shape((1, width + 16, hidden), BF16), shape((1, hidden, width), BF16)]
    outs = [shape((rows, width), BF16)] * 4 + grads * 2 + [shape((width, LANES), F32)]
    spots = (own_h, other_h, own_z, other_z)
    return pl.pallas_call(
        functools.partial(expert_kernel, steps, experts, len(grads)),
        grid=(2 * steps,),
        in_specs=[pl.BlockSpec(memory_space=pltpu.SMEM)]
        + [rows_spec(p, w) for p, w in zip(places, (early, late, early, late))]
        + [weight(w, k) for w, k in zip((*own_w, *got_w), at)]
        + [once(w_route.shape)],
        out_specs=[out_first, out_second, out_first, out_second] + [once(o.shape) for o in outs[4:]],
        out_shape=outs,
        scratch_shapes=[
            *[pltpu.VMEM((block, hidden), BF16)] * 4,
            pltpu.VMEM((block, width), BF16),
            *[pltpu.VMEM(s, F32) for s in ((width, hidden), (16, hidden), (hidden, width))] * 2,
        ],
        compiler_params=pltpu.CompilerParams(vmem_limit_bytes=VMEM),
        cost_estimate=pl.CostEstimate(
            flops=48 * rows * hidden * width, bytes_accessed=20 * width * hidden, transcendentals=4 * rows * hidden
        ),
        name="expert",
    )(expert_id, *spots, *own_w, *got_w, w_route)


def finish_kernel(n, *refs):
    parts, (win, wout, bias) = refs[: 6 * n], refs[-3:]
    for l in range(n):
        for k, out in enumerate((win, wout, bias)):
            out[l] = parts[6 * l + k][...].astype(F32) + parts[6 * l + 3 + k][...].astype(F32)


def finish(own, got):
    n, (_, height, hidden) = len(own), own[0].shape
    width = (height - 16) // 2
    tile = 128
    steps = width // tile
    spec = lambda r, k: pl.BlockSpec((None, r, hidden), lambda i: (0, k(i), 0))
    three = [spec(tile, lambda i: i), spec(tile, lambda i: steps + i), spec(16, lambda i: 2 * width // 16)]
    flat = [x for pair in zip(own, got) for a in pair for x in (a, a, a)]
    big = pl.BlockSpec((n, tile, hidden), lambda i: (0, i, 0))
    shape = jax.ShapeDtypeStruct
    return pl.pallas_call(
        functools.partial(finish_kernel, n),
        grid=(steps,),
        in_specs=three * (2 * n),
        out_specs=[big, big, pl.BlockSpec((n, 16, hidden), lambda i: (0, 0, 0))],
        out_shape=[shape((n, width, hidden), F32), shape((n, width, hidden), F32), shape((n, 16, hidden), F32)],
        compiler_params=pltpu.CompilerParams(vmem_limit_bytes=VMEM),
        cost_estimate=pl.CostEstimate(
            flops=2 * n * height * hidden, bytes_accessed=8 * n * height * hidden, transcendentals=0
        ),
        name="finish",
    )(*flat)


def to_send_kernel(in_ref, out_ref, *refs):
    for l in range(in_ref.shape[0]):
        refs[2 * l][0] = in_ref[l]
        refs[2 * l + 1][0] = out_ref[l]


def to_send(w_in, w_out):
    groups = w_in.shape[0]
    steps = w_in.shape[1] // 128
    spec = lambda a, k: pl.BlockSpec((k, a.shape[1] // steps, a.shape[2]), lambda i: (0, i, 0))
    flat = pl.pallas_call(
        to_send_kernel,
        grid=(steps,),
        in_specs=[spec(w_in, groups), spec(w_out, groups)],
        out_specs=[spec(w_in, 1), spec(w_out, 1)] * groups,
        out_shape=[jax.ShapeDtypeStruct((1, *a.shape[1:]), BF16) for a in (w_in, w_out)] * groups,
        compiler_params=pltpu.CompilerParams(vmem_limit_bytes=VMEM),
        cost_estimate=COST,
        name="to_send",
    )(w_in, w_out)
    return [flat[2 * l : 2 * l + 2] for l in range(groups)]


def turn_kernel(x_ref, y_ref, x_out, y_out):
    x_out[...] = x_ref[...].T
    y_out[...] = y_ref[...].T


def turn(x, y):
    whole = lambda a, b: pl.BlockSpec((a, b), lambda i: (0, 0))
    tokens, width = x.shape
    return pl.pallas_call(
        turn_kernel,
        grid=(1,),
        in_specs=[whole(tokens, width)] * 2,
        out_specs=[whole(width, tokens)] * 2,
        out_shape=[jax.ShapeDtypeStruct((width, tokens), x.dtype)] * 2,
        compiler_params=pltpu.CompilerParams(vmem_limit_bytes=VMEM),
        name="turn",
    )(x, y)


def outer_kernel(h_ref, a_ref, g_ref, b_ref, rest_ref, sums_ref, out_ref):
    width = b_ref.shape[1]
    for k in range(3):
        out_ref[:, k * width : (k + 1) * width] = dot(h_ref[...], g_ref[k]).astype(BF16)
    out_ref[:, 3 * width : 4 * width] = dot(a_ref[...], b_ref[...]).astype(BF16)
    out_ref[:, 4 * width : 4 * width + LANES] = rest_ref[...]
    out_ref[:, 4 * width + LANES :] = sums_ref[...].T.astype(BF16)


def outer(h, a, g, b, rest, sums):
    width, tokens = h.shape
    tile = 256
    whole = lambda *shape: pl.BlockSpec(shape, lambda i: (0,) * len(shape))
    rows = lambda n: pl.BlockSpec((tile, n), lambda i: (i, 0))
    columns = 4 * width + 2 * LANES
    return pl.pallas_call(
        outer_kernel,
        grid=(width // tile,),
        in_specs=[
            rows(tokens), rows(tokens), whole(3, tokens, width), whole(tokens, width), rows(LANES),
            pl.BlockSpec((LANES, tile), lambda i: (0, i)),
        ],
        out_specs=rows(columns),
        out_shape=jax.ShapeDtypeStruct((width, columns), BF16),
        compiler_params=pltpu.CompilerParams(vmem_limit_bytes=VMEM),
        cost_estimate=COST,
        name="outer",
    )(h, a, g, b, rest, sums)


def input_kernel(g_ref, w_ref, x_ref, dy_ref, gain_ref, out_ref, sums_ref):
    width = x_ref.shape[1]

    @pl.when(pl.program_id(0) == 0)
    def _():
        sums_ref[...] = jnp.zeros_like(sums_ref)

    grad = dot_nt(g_ref[0], w_ref[:, :width])
    for k in (1, 2):
        grad += dot_nt(g_ref[k], w_ref[:, k * width : (k + 1) * width])
    unit, rstd = normed(x_ref[...].astype(F32))
    out_ref[...] = dy_ref[...] + norm_back(grad, gain_ref[...], unit, rstd)
    add = lambda t: jnp.sum(t, axis=0, keepdims=True)
    sums_ref[0:1, :] += add(grad * unit)
    sums_ref[1:2, :] += add(grad)
    sums_ref[2:3, :] += add(g_ref[0].astype(F32))
    sums_ref[3:4, :] += add(g_ref[2].astype(F32))


def input_back(g, wide, tokens, dy, gain):
    count, width = tokens.shape
    tile = 256
    rows = pl.BlockSpec((tile, width), lambda i: (i, 0))
    whole = lambda *shape: pl.BlockSpec(shape, lambda i: (0,) * len(shape))
    return pl.pallas_call(
        input_kernel,
        grid=(count // tile,),
        in_specs=[
            pl.BlockSpec((3, tile, width), lambda i: (0, i, 0)), whole(*wide.shape), rows, rows, whole(1, width),
        ],
        out_specs=[rows, whole(LANES, width)],
        out_shape=[jax.ShapeDtypeStruct((count, width), F32), jax.ShapeDtypeStruct((LANES, width), F32)],
        compiler_params=pltpu.CompilerParams(vmem_limit_bytes=VMEM),
        cost_estimate=COST,
        name="input_back",
    )(g, wide, tokens, dy, gain)


def normed(x):
    centred = x - jnp.mean(x, axis=-1, keepdims=True)
    rstd = lax.rsqrt(jnp.mean(centred * centred, axis=-1, keepdims=True) + EPSILON)
    return centred * rstd, rstd


def norm_back(grad, gain, unit, rstd):
    g = grad * gain
    mean = lambda t: jnp.mean(t, axis=-1, keepdims=True)
    return rstd * (g - mean(g) - unit * mean(g * unit))


def pad_columns(x, count):
    return jnp.pad(x, ((0, 0), (0, count - x.shape[1])))


def up(count):
    return -(-count // LANES) * LANES


def local(
    tokens, cotangent, segment_ids, routes, capacity, ln1_gain, ln1_bias, w_query, b_query, w_key, w_value,
    b_value, w_output, b_output, ln2_gain, ln2_bias, w_router, w_in, b_in, w_out, b_out,
):
    row_count, width = tokens.shape
    experts = capacity.shape[0]
    slots = 2 * row_count // experts
    groups = w_in.shape[0]
    owners = lax.axis_size("expert")
    split = groups * owners // experts
    share = w_query.shape[0]
    devices = lax.axis_size("batch") * owners
    me = lax.axis_index("expert")
    chunk = min(2, groups)
    layout = (groups, chunk, split, slots)
    firsts = tuple(range(0, groups, chunk))
    pair = lambda first: range(first, first + chunk)
    heavy = lambda l: 1 if l % 2 == 0 else 2
    light = lambda l: 3 - heavy(l)

    spread = -(-experts // share)
    fold = lambda x: jnp.pad(x, (0, spread * share - experts)).reshape(spread, share).T
    unfold = lambda x: x.T.reshape(-1)[:experts]

    chosen = routes[:, 0]
    picked = chosen[:, None] == jnp.arange(experts, dtype=jnp.int32)[None, :]
    picked_float = picked.astype(F32)
    position = jnp.arange(row_count, dtype=jnp.int32)
    earlier = (position[None, :] < position[:, None]).astype(BF16)
    rank = dot(earlier, picked.astype(BF16))
    slot = jnp.sum(rank * picked_float, axis=1)
    limit = jnp.sum(capacity.astype(F32)[None, :] * picked_float, axis=1)
    kept = slot < limit
    kept_float = kept.astype(F32)
    ids = jnp.where(kept, chosen * slots + slot.astype(jnp.int32), -1)
    id_row, id_col = ids[None, :], ids[:, None]
    counts = jnp.sum(picked_float, axis=0)

    def send(x, first, count):
        rows = dispatch(id_row, x, count * owners * slots, (groups, count, split, slots), first)
        return rows.reshape(owners, count, slots, width)

    grad_send = send(cotangent, 0, groups)

    small = jnp.stack([ln1_gain, ln1_bias, b_query, b_value, b_output, ln2_gain, ln2_bias], axis=1)
    tally = fold(counts).astype(BF16)
    extra = pad_columns(jnp.concatenate([small, tally], axis=1), up(7 + spread))
    wide = jnp.concatenate([w_query, w_key, w_value, extra], axis=1)
    rest = jnp.concatenate([w_router, b_out.T], axis=1)
    rest = jnp.concatenate([w_output, pad_columns(rest, up(2 * experts))], axis=1)
    if staged():
        wide, rest = gather_first(wide), gather_first(rest)
        rest_first = rest
        sent_w = to_send(*after((w_in, w_out), grad_send))
        free = gather_second(wide, (grad_send, sent_w))
        wide = gather_third(free)
        rest = after(rest, free)
    else:
        wide = lax.all_gather(wide, ALL, axis=0, tiled=True)
        rest = lax.all_gather(rest, ALL, axis=0, tiled=True)
        free = rest_first = ()
        sent_w = to_send(w_in, w_out)

    bias_rows = b_in[:, None, :]
    got_bias = [swap(after(bias_rows, free), "batch", mask) for mask in (1, 2)]
    got_w, last = [], free
    for l in range(groups):
        if l % chunk == 0:
            last = got_w[-chunk:] or free
        got_w.append([swap(w, "batch", heavy(l)) for w in after(sent_w[l], last)])

    own_z = to_owners(after(grad_send, rest_first))
    theirs = lambda rows, l, at: swap(rows[:, at : at + 1], "batch", light(l))
    other_z = [theirs(own_z, l, l) for l in range(groups)]

    vectors = wide[:, 3 * width : 3 * width + 7].astype(F32).T
    gain_one, shift_one, bias_query, bias_value, bias_output, gain_two, shift_two = vectors
    tallies = wide[:, 3 * width + 7 : 3 * width + 7 + spread].astype(F32).reshape(devices, share, spread)
    all_counts = unfold(jnp.sum(tallies, axis=0))
    token_total = float(row_count * devices)
    fraction = all_counts / token_total

    inputs = tokens.astype(F32)
    unit_one, rstd_one = normed(inputs)
    h_one = (unit_one * gain_one + shift_one).astype(BF16)
    nothing = jnp.zeros((width,), F32)
    bias = jnp.concatenate([bias_query, nothing, bias_value, jnp.zeros((wide.shape[1] - 3 * width,), F32)])
    qkv = (dot(h_one, wide) + bias).astype(BF16)
    if staged():
        rest = gather_second(rest, qkv)
    seg_row = segment_ids.reshape(1, row_count)
    seg_col = segment_ids.reshape(row_count, 1)
    attended, logs = attend(qkv, seg_row, seg_col, width)
    attended = after(attended, [w[0] for w in got_w[:chunk]])
    if staged():
        rest = gather_third(rest, attended)
    full_output = rest[:, :width]
    full_router = pad_columns(rest[:, width : width + experts], LANES)
    bias_expert = rest[:, width + experts : width + 2 * experts].T
    resid = inputs + dot(attended, full_output) + bias_output
    unit_two, rstd_two = normed(resid)
    h_two = (unit_two * gain_two + shift_two).astype(BF16)
    h_two = after(h_two, own_z, [w[1] for w in got_w[:chunk]])

    rows = [send(h_two, first, chunk) for first in firsts]
    token_rows = []
    for at in range(len(firsts)):
        if at:
            rows[at] = after(rows[at], token_rows[-1], [w[0] for w in got_w[chunk:]])
        token_rows.append(to_owners(rows[at]))
    token_rows = [after(t, rows) for t in token_rows]
    their_h = [token_rows[l // chunk][:, l % chunk : l % chunk + 1] for l in range(groups)]
    their_h = [lax.optimization_barrier(their_h[first : first + chunk]) for first in firsts]
    other_h = [swap(their_h[l // chunk][l % chunk], "batch", light(l)) for l in range(groups)]
    h_turned, att_turned = turn(h_one, attended)

    router_probs = jax.nn.softmax(dot(h_two, full_router)[:, :experts], axis=-1)
    mixing = kept_float * jnp.sum(router_probs * picked_float, axis=1)
    grad_out = cotangent.astype(F32)
    expert_bias = dot(picked.astype(BF16), bias_expert)
    gate_bias = kept_float * jnp.sum(grad_out * expert_bias, axis=1)
    grad_probs = picked_float * gate_bias[:, None] + BALANCE * experts * fraction[None, :] / token_total
    grad_logits = router_probs * (grad_probs - jnp.sum(grad_probs * router_probs, axis=1, keepdims=True))
    grad_logits = grad_logits.astype(BF16)
    mixed = picked_float * mixing[:, None]
    mixed_high = mixed.astype(BF16)
    mixed_low = (mixed - mixed_high.astype(F32)).astype(BF16)
    grad_bias_expert = dot_tn(cotangent, mixed_high) + dot_tn(cotangent, mixed_low)
    home_router = dot_tn(h_two, grad_logits)
    home_h_two = dot_nt(grad_logits, full_router[:, :experts])
    home_h_two, home_router, grad_bias_expert, probs_sum = lax.optimization_barrier(
        (home_h_two, home_router, grad_bias_expert, jnp.sum(router_probs, axis=0))
    )
    made, returned, piece_sums, got_g = [], [], [], []
    for at, first in enumerate(firsts):
        for l in pair(first):
            number = ((me * groups + l) // split).astype(jnp.int32).reshape(1)
            if l == 0:
                number = after(number, h_turned, home_h_two)
            if l == 1:
                number = after(number, made[-1], got_w[-chunk:], their_h)
            made.append(
                expert(
                    number, token_rows[at], other_h[l], own_z, other_z[l], (l - first, 0, l, 0),
                    (w_in, w_out, bias_rows), (*got_w[l], got_bias[heavy(l) - 1]), (l, l, l, 0, 0, l),
                    full_router, experts,
                )
            )
        sums = [(made[l][2], swap(after(made[l][3], other_h), "batch", light(l))) for l in pair(first)]
        rows = merge(sums, owners, slots)
        if returned:
            rows = after(rows, returned[-1], got_g)
        returned.append(to_owners(rows).reshape(-1, width))
        n = (len(made[0]) - 5) // 2
        if first + chunk == groups:
            piece_sums = [(m[0], swap(after(m[1], sums), "batch", light(l))) for l, m in enumerate(made)]
        for l in pair(first):
            grads = after(made[l][4 + n : 4 + 2 * n], sums, other_h, piece_sums)
            got_g.append([swap(g, "batch", heavy(l)) for g in grads])
    own_g = [m[4 : 4 + n] for m in made]

    grad_router = home_router + sum(m[-1] for m in made)[:, :experts]

    grad_h_two = home_h_two + combine(after(id_col, piece_sums), returned, layout, firsts)
    grad_resid = grad_out + norm_back(grad_h_two, gain_two, unit_two, rstd_two)
    grad_branch = grad_resid.astype(BF16)
    grad_att = dot_nt(grad_branch, full_output).astype(BF16)
    columns = lambda *rows: jnp.stack(rows, axis=1)
    prob_sums = jnp.tile(fold(probs_sum), (devices, 1))
    sums = columns(
        jnp.sum(grad_h_two * unit_two, axis=0), jnp.sum(grad_h_two, axis=0), jnp.sum(grad_branch.astype(F32), axis=0)
    )
    packed = jnp.concatenate([grad_router, grad_bias_expert, sums, prob_sums], axis=1)
    packed = pad_columns(packed, LANES).astype(BF16)
    merged = merge(after(piece_sums, grad_att, packed), owners, slots)
    pieces = to_owners(merged).reshape(-1, width)
    grad_att = after(grad_att, merged, packed)
    dqkv = attend_back(qkv, grad_att, logs, seg_row, seg_col, width)

    dqkv, got_g = after((dqkv, got_g), got_g)
    input_grad, sums = input_back(dqkv, wide, tokens, grad_resid, gain_one[None])
    def close(waiting):
        own, got, _ = waiting
        if n == 1:
            win, wout, bias = finish([g[0] for g in own], [g[0] for g in got])
            return win, bias[:, 0], wout
        both = [[a[0].astype(F32) + b[0].astype(F32) for a, b in zip(*pair_g)] for pair_g in zip(own, got)]
        return (
            jnp.stack([g[0][:width] for g in both]),
            jnp.stack([g[0][width] for g in both]),
            jnp.stack([g[1] for g in both]),
        )

    wide_sum, (grad_w_in, grad_b_in, grad_w_out) = scatter_rows(
        outer(h_turned, att_turned, dqkv, grad_branch, packed, sums), (own_g, got_g, pieces), close
    )
    pieces = after(pieces, grad_b_in)
    fetched = combine(id_col, [pieces], (groups, groups, split, slots), (0,))
    block_out = (resid + mixing[:, None] * (fetched + expert_bias)).astype(BF16)
    router_sum = wide_sum[:, 4 * width : 4 * width + 2 * experts]
    side = wide_sum[:, 4 * width + 2 * experts :]
    late_side = wide_sum[:, 4 * width + LANES :]
    mean_probs = unfold(side[:, 3 : 3 + spread]) / token_total
    balance_loss = experts * jnp.sum(fraction * mean_probs)
    expert_shares = jnp.stack([experts * fraction, experts * mean_probs])

    return (
        block_out,
        balance_loss,
        expert_shares,
        input_grad,
        late_side[:, 0],
        late_side[:, 1],
        wide_sum[:, :width],
        late_side[:, 2],
        wide_sum[:, width : 2 * width],
        wide_sum[:, 2 * width : 3 * width],
        late_side[:, 3],
        wide_sum[:, 3 * width : 4 * width],
        side[:, 2],
        side[:, 0],
        side[:, 1],
        router_sum[:, :experts],
        grad_w_in,
        grad_b_in,
        grad_w_out,
        router_sum[:, experts:].T,
    )


def solution(mesh):
    rows, split = P(ALL, None), P(ALL)
    experts = (P("expert", None, "batch"), P("expert", "batch"), P("expert", "batch", None), P(None, ALL))
    return jax.shard_map(
        local,
        mesh=mesh,
        in_specs=(
            rows, rows, rows, rows, P(), split, split, rows, split, rows, rows, split, rows, split, split, split,
            rows, *experts,
        ),
        out_specs=(
            rows, P(), P(), rows, split, split, rows, split, rows, rows, split, rows, split, split, split, rows,
            *experts,
        ),
        check_vma=False,
    )
```
